128 devices in a mesh: dp: 16 (over y, z), seq: 8 (over x, core).
Axes of the slice: x: 4, y: 4, z: 4, core: 2. Of those that a mesh axis runs over, the one named last changes fastest.
Arguments:
- tokens: bfloat16 [16, 1024, 2048], P('dp', 'seq'), may hold values from -6 to 6
- gain_attn: bfloat16 [2048], P(('dp', 'seq')), may hold values from 0.5 to 1.5
- w_query: bfloat16 [2048, 2048], P(('dp', 'seq')), may hold values from -0.125 to 0.125
- key_weight: bfloat16 [2048, 1024], P(('dp', 'seq')), may hold values from -0.125 to 0.125
- value_weight: bfloat16 [2048, 1024], P(('dp', 'seq')), may hold values from -0.125 to 0.125
- w_out: bfloat16 [2048, 2048], P(('dp', 'seq')), may hold values from -1 to 1
- gain_query: bfloat16 [128], P(('dp', 'seq')), may hold values from 0.5 to 1.5
- key_norm_gain: bfloat16 [128], P(('dp', 'seq')), may hold values from 0.5 to 1.5
- gain_mlp: bfloat16 [2048], P(('dp', 'seq')), may hold values from 0.5 to 1.5
- w_gate: bfloat16 [2048, 6144], P(('dp', 'seq')), may hold values from -0.125 to 0.125
- w_up: bfloat16 [2048, 6144], P(('dp', 'seq')), may hold values from -0.125 to 0.125
- w_down: bfloat16 [6144, 2048], P(('dp', 'seq')), may hold values from -0.078125 to 0.078125
- cotangent: bfloat16 [16, 1024, 2048], P('dp', 'seq'), may hold values from -6 to 6
Outputs:
- block_out: bfloat16 [16, 1024, 2048], P('dp', 'seq')
- grad_tokens: float32 [16, 1024, 2048], P('dp', 'seq')
- grad_gain_attn: float32 [2048], P(('dp', 'seq'))
- grad_w_query: float32 [2048, 2048], P(('dp', 'seq'))
- grad_w_key: float32 [2048, 1024], P(('dp', 'seq'))
- grad_w_value: float32 [2048, 1024], P(('dp', 'seq'))
- grad_w_out: float32 [2048, 2048], P(('dp', 'seq'))
- grad_gain_query: float32 [128], P(('dp', 'seq'))
- grad_gain_key: float32 [128], P(('dp', 'seq'))
- grad_gain_mlp: float32 [2048], P(('dp', 'seq'))
- grad_w_gate: float32 [2048, 6144], P(('dp', 'seq'))
- grad_w_up: float32 [2048, 6144], P(('dp', 'seq'))
- grad_w_down: float32 [6144, 2048], P(('dp', 'seq'))
The draws below stay inside these ranges and needn't reach their ends.
All inputs are finite; a program needn't handle non-finite values.
Results may differ from the reference program's by a relative error of at most 0.035.
Values may be sent and summed in bfloat16 or wider, within the bound.
A program may use at most 512 MiB of HBM per device.

```python
import math
import jax
import jax.numpy as jnp
from jax import lax

MODEL_DIM = 2048
QUERY_HEADS = 16
KEY_VALUE_HEADS = 8
HEAD_DIM = 128
FF = 6144
SEQ_LEN = 1024
BATCH = 16


def level_of(stream_key, extent, cuts, low, high):
    level, own = 1.0, jax.random.fold_in(stream_key, 6)
    for dim, blocks in cuts:
        steps = jnp.exp(jax.random.uniform(jax.random.fold_in(own, dim), (blocks,), jnp.float32, low / len(cuts), high / len(cuts)))
        level = level * jnp.repeat(steps, extent[dim] // blocks).reshape([-1 if axis == dim else 1 for axis in range(len(extent))])
    return level


def bell_draw(own_key, dims, deviation, most, pieces=(), kind=jnp.bfloat16):
    entries = jax.random.normal(own_key, dims, jnp.float32) * deviation
    if len(pieces) > 0:
        entries = level_of(own_key, dims, pieces, -0.22, 0.18) * entries
    return jnp.clip(entries, min=-most, max=most).astype(kind)


def setup_inputs(seed: int = 0) -> dict:
    splits = jax.random.split(jax.random.key(seed), 14)
    return {
        "tokens": bell_draw(splits[0], (BATCH, SEQ_LEN, MODEL_DIM), 1.0, 6.0, ((0, 16), (1, 8))),
        "gain_attn": jnp.clip(1.0 + 0.1 * jax.random.normal(splits[1], (MODEL_DIM,), jnp.float32), 0.5, 1.5).astype(jnp.bfloat16),
        "w_query": bell_draw(splits[2], (MODEL_DIM, QUERY_HEADS * HEAD_DIM), MODEL_DIM ** -0.5, 0.125, ((0, 128),)),
        "key_weight": bell_draw(splits[3], (MODEL_DIM, KEY_VALUE_HEADS * HEAD_DIM), MODEL_DIM ** -0.5, 0.125, ((0, 128),)),
        "value_weight": bell_draw(splits[4], (MODEL_DIM, KEY_VALUE_HEADS * HEAD_DIM), MODEL_DIM ** -0.5, 0.125, ((0, 128),)),
        "w_out": bell_draw(splits[5], (QUERY_HEADS * HEAD_DIM, MODEL_DIM), (max(QUERY_HEADS * HEAD_DIM // 64, 1)) ** -0.5, 1.0, ((0, 128),)),
        "gain_query": jnp.clip(1.0 + 0.1 * jax.random.normal(splits[6], (HEAD_DIM,), jnp.float32), 0.5, 1.5).astype(jnp.bfloat16),
        "key_norm_gain": jnp.clip(1.0 + 0.1 * jax.random.normal(splits[7], (HEAD_DIM,), jnp.float32), 0.5, 1.5).astype(jnp.bfloat16),
        "gain_mlp": jnp.clip(1.0 + 0.1 * jax.random.normal(splits[8], (MODEL_DIM,), jnp.float32), 0.5, 1.5).astype(jnp.bfloat16),
        "w_gate": bell_draw(splits[9], (MODEL_DIM, FF), MODEL_DIM ** -0.5, 0.125, ((0, 128),)),
        "w_up": bell_draw(splits[10], (MODEL_DIM, FF), MODEL_DIM ** -0.5, 0.125, ((0, 128),)),
        "w_down": bell_draw(splits[11], (FF, MODEL_DIM), FF ** -0.5, 0.078125, ((0, 128),)),
        "cotangent": bell_draw(splits[12], (BATCH, SEQ_LEN, MODEL_DIM), 1.0, 6.0, ((0, 16), (1, 8))),
    }


eps_norm = 1e-06
rope_base = 1000000.0
top_precision = lax.Precision.HIGHEST

@jax.custom_vjp
def low(v):
    return lax.optimization_barrier(v.astype(jnp.bfloat16)).astype(jnp.float32)

@jax.custom_vjp
def low_back(v):
    return v

def low_keep(v):
    return (low(v), None)

def low_pass(kept, grad):
    return (grad,)

def back_keep(v):
    return (v, None)

def back_low(kept, grad):
    return (low(grad),)
low.defvjp(low_keep, low_pass)
low_back.defvjp(back_keep, back_low)

def root_mean_square_norm(values, gain_vec):
    return values * lax.rsqrt(lax.optimization_barrier(jnp.mean(values * values, axis=-1, keepdims=True)) + eps_norm) * gain_vec

def rope_tables(positions, half_dim):
    freqs = rope_base ** (-(jnp.arange(half_dim, dtype=jnp.float32) * 2.0 / (2 * half_dim)))
    angles = positions.astype(jnp.float32)[:, None] * freqs[None, :]
    return (jnp.cos(angles), jnp.sin(angles))

def rotate_halves(values, cosine_table, sine_table):
    half_dim = values.shape[-1] // 2
    first = values[..., :half_dim]
    second = values[..., half_dim:]
    cosine_table = cosine_table[:, None, :]
    sine_table = sine_table[:, None, :]
    return jnp.concatenate([first * cosine_table - second * sine_table, second * cosine_table + first * sine_table], axis=-1)

def sequence_layer(seq_x, gain_attn, w_query, key_weight, value_weight, w_out, gain_query, key_norm_gain, gain_mlp, w_gate, w_up, w_down):
    sequence_length = seq_x.shape[0]
    query_groups = QUERY_HEADS // KEY_VALUE_HEADS
    score_scale = 1.0 / math.sqrt(HEAD_DIM)
    normalized_input = low(root_mean_square_norm(seq_x, gain_attn))
    query_pre = low_back(jnp.dot(normalized_input, w_query, precision=top_precision))
    prenorm_key = low_back(jnp.dot(normalized_input, key_weight, precision=top_precision))
    every_value_row = low(low_back(jnp.dot(normalized_input, value_weight, precision=top_precision))).reshape(sequence_length, KEY_VALUE_HEADS, HEAD_DIM)
    cosine_table, sine_table = rope_tables(jnp.arange(sequence_length, dtype=jnp.int32), HEAD_DIM // 2)
    every_query_row = low(rotate_halves(root_mean_square_norm(query_pre.reshape(sequence_length, QUERY_HEADS, HEAD_DIM), gain_query), cosine_table, sine_table))
    every_key_row = low(rotate_halves(root_mean_square_norm(prenorm_key.reshape(sequence_length, KEY_VALUE_HEADS, HEAD_DIM), key_norm_gain), cosine_table, sine_table))
    query_five_axes = every_query_row.reshape(sequence_length, KEY_VALUE_HEADS, query_groups, HEAD_DIM)
    block_rows = min(512, sequence_length)
    key_pos = jnp.arange(sequence_length, dtype=jnp.int32)

    def attend(index):
        query_blk = lax.dynamic_slice_in_dim(query_five_axes, index * block_rows, block_rows, 0)
        scores = low_back(jnp.einsum('qhgd,khd->hgqk', query_blk, every_key_row, precision=top_precision) * score_scale)
        row_pos = index * block_rows + jnp.arange(block_rows, dtype=jnp.int32)
        allowed = key_pos[None, :] <= row_pos[:, None]
        scores = jnp.where(allowed, scores, -1e+30)
        top_val = lax.optimization_barrier(jnp.max(scores, axis=-1, keepdims=True))
        expon = jnp.exp(scores - top_val)
        attn_prob = low(expon / lax.optimization_barrier(jnp.sum(expon, axis=-1, keepdims=True)))
        return jnp.einsum('hgqk,khd->qhgd', attn_prob, every_value_row, precision=top_precision)
    attn_blocks = lax.map(jax.checkpoint(attend), jnp.arange(sequence_length // block_rows, dtype=jnp.int32))
    attn_flat = low(low_back(attn_blocks.reshape(sequence_length, QUERY_HEADS * HEAD_DIM)))
    after_attn = seq_x + low_back(jnp.dot(attn_flat, w_out, precision=top_precision))
    normed_two = low(root_mean_square_norm(after_attn, gain_mlp))
    gate_val = low_back(jnp.dot(normed_two, w_gate, precision=top_precision))
    up_val = low_back(jnp.dot(normed_two, w_up, precision=top_precision))
    hidden = low(jax.nn.silu(gate_val) * up_val)
    return after_attn + low_back(jnp.dot(hidden, w_down, precision=top_precision))

def forward(all_x, params):

    def one_sequence(seq_x):
        return sequence_layer(seq_x, *params)
    return lax.map(jax.checkpoint(one_sequence), all_x)

def reference(tokens, gain_attn, w_query, key_weight, value_weight, w_out, gain_query, key_norm_gain, gain_mlp, w_gate, w_up, w_down, cotangent):
    params = tuple((item.astype(jnp.float32) for item in (gain_attn, w_query, key_weight, value_weight, w_out, gain_query, key_norm_gain, gain_mlp, w_gate, w_up, w_down)))
    block, pullback = jax.vjp(forward, tokens.astype(jnp.float32), params)
    grad_x, grads = pullback(cotangent.astype(jnp.float32))
    return (block.astype(jnp.bfloat16), grad_x, grads[0], grads[1], grads[2], grads[3], grads[4], grads[5], grads[6], grads[7], grads[8], grads[9], grads[10])
```

```python
import math

import jax
import jax.numpy as jnp
from jax import lax
from jax.sharding import PartitionSpec as P

QUERY_HEADS = 16
KEY_VALUE_HEADS = 8
HEAD_DIM = 128

eps_norm = 1e-06
rope_base = 1000000.0

f32 = jnp.float32
bf16 = jnp.bfloat16


def rope_tables(positions, half_dim):
    freqs = rope_base ** (-(jnp.arange(half_dim, dtype=f32) * 2.0 / (2 * half_dim)))
    angles = positions.astype(f32)[:, None] * freqs[None, :]
    return (jnp.cos(angles), jnp.sin(angles))


def rotate(values, cos, sin):
    half = values.shape[-1] // 2
    a, b = values[..., :half], values[..., half:]
    cos, sin = cos[:, None, :], sin[:, None, :]
    return jnp.concatenate([a * cos - b * sin, b * cos + a * sin], axis=-1)


def unrotate(grads, cos, sin):
    half = grads.shape[-1] // 2
    a, b = grads[..., :half], grads[..., half:]
    cos, sin = cos[:, None, :], sin[:, None, :]
    return jnp.concatenate([a * cos + b * sin, b * cos - a * sin], axis=-1)


def rms(values):
    return lax.rsqrt(jnp.mean(values * values, axis=-1, keepdims=True) + eps_norm)


def rms_back(grad_out, gain, unit, inv):
    grad_unit = grad_out * gain
    return inv * (grad_unit - unit * jnp.mean(grad_unit * unit, axis=-1, keepdims=True))


def dot(a, b):
    return jnp.dot(a, b, preferred_element_type=f32)


def dot_tn(a, b):
    return lax.dot_general(a, b, (((0,), (0,)), ((), ())), preferred_element_type=f32)


def dot_nt(a, b):
    return lax.dot_general(a, b, (((1,), (1,)), ((), ())), preferred_element_type=f32)


def shards(
    tokens, gain_attn, w_query, key_weight, value_weight, w_out, gain_query,
    key_norm_gain, gain_mlp, w_gate, w_up, w_down, cotangent,
):
    nd, ns = lax.axis_size("dp"), lax.axis_size("seq")
    _, span, width = tokens.shape
    length = span * ns
    wr = w_query.shape[0]
    heads = QUERY_HEADS // ns
    qw, kw = w_query.shape[1] // ns, key_weight.shape[1] // ns
    ff = w_gate.shape[1] // ns
    fr = w_down.shape[0]
    scale = 1.0 / math.sqrt(HEAD_DIM)

    gains = jnp.concatenate([gain_attn, gain_mlp, gain_query, key_norm_gain])
    gains = jnp.broadcast_to(jnp.pad(gains, (0, 128 - gains.shape[0]))[None, :], (16, 128))
    gains = lax.all_gather(gains, ("dp", "seq"), axis=0, tiled=True).reshape(-1, 16, 128)[:, 0]
    gains = gains.astype(f32)
    gain_one = gains[:, :wr].reshape(1, width)
    gain_two = gains[:, wr : 2 * wr].reshape(1, width)
    gain_q = gains[:, 2 * wr].reshape(1, HEAD_DIM)
    gain_k = gains[:, 2 * wr + 1].reshape(1, HEAD_DIM)

    qkv_blk = jnp.concatenate(
        [
            w_query.reshape(wr, ns, qw),
            key_weight.reshape(wr, ns, kw),
            value_weight.reshape(wr, ns, kw),
        ],
        axis=2,
    )
    mlp_blk = jnp.concatenate(
        [
            w.reshape(wr, nd, ns, fr).transpose(0, 2, 1, 3).reshape(wr, ns, nd * fr)
            for w in (w_gate, w_up)
        ],
        axis=2,
    )
    qkv_blk = lax.all_to_all(qkv_blk, "seq", 1, 0, tiled=True).reshape(ns * wr, -1)
    qkv_mat = lax.all_gather(qkv_blk, "dp", axis=0, tiled=True)
    mlp_blk = lax.all_to_all(mlp_blk, "seq", 1, 0, tiled=True).reshape(ns * wr, -1)
    cw = width // nd
    out_blk = lax.all_to_all(w_out, "dp", 1, 0, tiled=True)
    out_blk = lax.all_to_all(out_blk, "seq", 0, 1, tiled=True)
    d2 = nd // ns
    out_blk = (
        out_blk.reshape(d2, wr, ns, cw).transpose(0, 2, 1, 3).reshape(d2 * ns * wr, cw)
    )
    out_mat = lax.all_gather(out_blk, "dp", axis=1, tiled=True)
    mlp_mat = lax.all_gather(mlp_blk, "dp", axis=0, tiled=True)
    gate_mat, up_mat = mlp_mat[:, :ff], mlp_mat[:, ff:]
    down_mat = lax.all_gather(w_down, "dp", axis=0, tiled=True)

    x_loc = tokens[0].astype(f32)
    x_all = lax.all_gather(tokens[0], "seq", axis=0, tiled=True).astype(f32)
    unit_one = x_all * rms(x_all)
    h1 = (unit_one * gain_one).astype(bf16)
    qkv = dot(h1, qkv_mat)
    q_pre = qkv[:, :qw].reshape(length, heads, HEAD_DIM)
    k_pre = qkv[:, qw : qw + kw].reshape(length, 1, HEAD_DIM)
    vb = qkv[:, qw + kw :].astype(bf16)
    cos, sin = rope_tables(jnp.arange(length, dtype=jnp.int32), HEAD_DIM // 2)
    inv_q, inv_k = rms(q_pre), rms(k_pre)
    unit_q, unit_k = q_pre * inv_q, k_pre * inv_k
    qb = rotate(unit_q * gain_q, cos, sin).astype(bf16)
    kb = rotate(unit_k * gain_k, cos, sin).astype(bf16)[:, 0]
    allowed = (
        jnp.arange(length, dtype=jnp.int32)[None, :]
        <= jnp.arange(length, dtype=jnp.int32)[:, None]
    )
    score = jnp.einsum("qhd,kd->hqk", qb, kb, preferred_element_type=f32) * scale
    score = jnp.where(allowed, score, -1e30)
    top = jnp.max(score, axis=-1, keepdims=True)
    expo = jnp.exp(score - top)
    prob = expo / jnp.sum(expo, axis=-1, keepdims=True)
    pb = prob.astype(bf16)
    ob = jnp.einsum("hqk,kd->qhd", pb, vb, preferred_element_type=f32)
    ob = ob.astype(bf16).reshape(length, qw)
    part = dot(ob, out_mat).astype(bf16)
    x1 = x_loc + lax.psum_scatter(part, "seq", scatter_dimension=0, tiled=True).astype(f32)

    inv_two = rms(x1)
    unit_two = x1 * inv_two
    h2_loc = (unit_two * gain_two).astype(bf16)
    h2 = lax.all_gather(h2_loc, "seq", axis=0, tiled=True)
    dy = cotangent[0].astype(f32)
    dyb = lax.all_gather(cotangent[0], "seq", axis=0, tiled=True)
    gate = dot(h2, gate_mat)
    up = dot(h2, up_mat)
    sig = jax.nn.sigmoid(gate)
    silu = gate * sig
    hid = (silu * up).astype(bf16)
    dhid = dot_nt(dyb, down_mat)
    dgate = (dhid * up * (sig * (1.0 + gate * (1.0 - sig)))).astype(bf16)
    dup = (dhid * silu).astype(bf16)
    dh2 = (dot_nt(dgate, gate_mat) + dot_nt(dup, up_mat)).astype(bf16)
    dh2 = lax.psum_scatter(dh2, "seq", scatter_dimension=0, tiled=True).astype(f32)
    dx1 = dy + rms_back(dh2, gain_two, unit_two, inv_two)
    g_gain_two = jnp.sum(dh2 * unit_two, axis=0)
    part = dot(hid, down_mat).astype(bf16)
    block = x1 + lax.psum_scatter(part, "seq", scatter_dimension=0, tiled=True).astype(f32)
    block_out = block.astype(bf16)[None]
    g_down = dot_tn(hid, dyb).astype(bf16)
    g_mlp = jnp.concatenate([dot_tn(h2, dgate), dot_tn(h2, dup)], axis=1).astype(bf16)
    g_down = lax.psum_scatter(g_down, "dp", scatter_dimension=0, tiled=True).astype(f32)
    g_mlp = lax.psum_scatter(g_mlp, "dp", scatter_dimension=0, tiled=True)
    g_mlp = lax.all_to_all(g_mlp.reshape(ns, wr, 2 * ff), "seq", 0, 0, tiled=True)
    g_mlp = g_mlp.astype(f32).reshape(ns, wr, 2, nd, fr).transpose(2, 1, 3, 0, 4)
    g_mlp = g_mlp.reshape(2, wr, nd * ns * fr)

    dab = lax.all_gather(dx1.astype(bf16), "seq", axis=0, tiled=True)
    g_out = dot_tn(ob, dab).astype(bf16)
    dob = dot_nt(dab, out_mat).astype(bf16).reshape(length, heads, HEAD_DIM)
    dprob = jnp.einsum("qhd,kd->hqk", dob, vb, preferred_element_type=f32)
    delta = jnp.sum(prob * dprob, axis=-1, keepdims=True)
    dscore = (prob * (dprob - delta)).astype(bf16)
    dq = jnp.einsum("hqk,kd->qhd", dscore, kb, preferred_element_type=f32) * scale
    dk = jnp.einsum("hqk,qhd->kd", dscore, qb, preferred_element_type=f32) * scale
    dv = jnp.einsum("hqk,qhd->kd", pb, dob, preferred_element_type=f32)
    dq = unrotate(dq, cos, sin)
    dk = unrotate(dk[:, None], cos, sin)
    g_gain_q = jnp.sum(dq * unit_q, axis=(0, 1))
    g_gain_k = jnp.sum(dk * unit_k, axis=(0, 1))
    dqp = rms_back(dq, gain_q, unit_q, inv_q).reshape(length, qw)
    dkp = rms_back(dk, gain_k, unit_k, inv_k).reshape(length, kw)
    dqkv = jnp.concatenate([dqp, dkp, dv], axis=1).astype(bf16)
    dh1 = dot_nt(dqkv, qkv_mat).astype(bf16)
    dh1 = lax.psum_scatter(dh1, "seq", scatter_dimension=0, tiled=True).astype(f32)
    inv_one = rms(x_loc)
    unit_loc = x_loc * inv_one
    grad_tokens = (dx1 + rms_back(dh1, gain_one, unit_loc, inv_one))[None]
    g_gain_one = jnp.sum(dh1 * unit_loc, axis=0)
    g_qkv = dot_tn(h1, dqkv).astype(bf16)
    g_qkv = lax.psum_scatter(g_qkv, "dp", scatter_dimension=0, tiled=True)
    g_qkv = lax.all_to_all(g_qkv.reshape(ns, wr, -1), "seq", 0, 0, tiled=True).astype(f32)
    g_q = g_qkv[:, :, :qw].transpose(1, 0, 2).reshape(wr, -1)
    g_k = g_qkv[:, :, qw : qw + kw].transpose(1, 0, 2).reshape(wr, -1)
    g_v = g_qkv[:, :, qw + kw :].transpose(1, 0, 2).reshape(wr, -1)
    g_out = lax.psum_scatter(g_out, "dp", scatter_dimension=1, tiled=True)
    g_out = g_out.reshape(d2, ns, wr, cw).transpose(0, 2, 1, 3).reshape(d2 * wr, ns * cw)
    g_out = lax.all_to_all(g_out, "seq", 1, 0, tiled=True)
    g_out = lax.all_to_all(g_out, "dp", 0, 1, tiled=True).astype(f32)

    gg = jnp.concatenate(
        [
            g_gain_one.reshape(nd * ns, wr),
            g_gain_two.reshape(nd * ns, wr),
            g_gain_q[:, None],
            g_gain_k[:, None],
        ],
        axis=1,
    )
    gg = jnp.pad(gg, ((0, 0), (0, 128 - gg.shape[1])))
    gg = lax.psum_scatter(gg, "dp", scatter_dimension=0, tiled=True)
    gg = jnp.sum(lax.all_to_all(gg[:, None], "seq", 0, 1, tiled=True)[0], axis=0)
    return (
        block_out, grad_tokens, gg[:wr], g_q, g_k, g_v, g_out,
        gg[2 * wr : 2 * wr + 1], gg[2 * wr + 1 : 2 * wr + 2], gg[wr : 2 * wr],
        g_mlp[0], g_mlp[1], g_down,
    )


def solution(mesh):
    both = P(("dp", "seq"))
    rows = P(("dp", "seq"), None)
    act = P("dp", "seq", None)
    in_specs = (act, both, rows, rows, rows, rows, both, both, both, rows, rows, rows, act)
    out_specs = (act, act, both, rows, rows, rows, rows, both, both, both, rows, rows, rows)
    return jax.shard_map(
        shards, mesh=mesh, in_specs=in_specs, out_specs=out_specs, check_vma=False
    )
```

```python
import functools
import math

import jax
import jax.numpy as jnp
import numpy as np
from jax import lax
from jax.experimental import pallas as pl
from jax.experimental.pallas import tpu as pltpu
from jax.sharding import PartitionSpec as P

QUERY_HEADS = 16
KEY_VALUE_HEADS = 8
HEAD_DIM = 128

eps_norm = 1e-06
rope_base = 1000000.0
score_scale = 1.0 / math.sqrt(HEAD_DIM)

f32 = jnp.float32
bf16 = jnp.bfloat16

AXIS = 4
ND, NS = 16, 8
SPAN = 128
WIDTH = 2048
LENGTH = SPAN * NS
WR = 16
FR = 48
FFS = ND * FR
QKV = 512
GCOL = 128
VMEM_LIMIT = 60 * 2**20
MESH = pl.DeviceIdType.MESH


def dot(a, b):
    return jnp.dot(a, b, preferred_element_type=f32)


def dot_tn(a, b):
    return lax.dot_general(a, b, (((0,), (0,)), ((), ())), preferred_element_type=f32)


def dot_nt(a, b):
    return lax.dot_general(a, b, (((1,), (1,)), ((), ())), preferred_element_type=f32)


def rms(values):
    return lax.rsqrt(jnp.mean(values * values, axis=-1, keepdims=True) + eps_norm)


def rms_back(grad_out, gain, unit, inv):
    grad_unit = grad_out * gain
    return inv * (grad_unit - unit * jnp.mean(grad_unit * unit, axis=-1, keepdims=True))


def rope_constants():
    half = HEAD_DIM // 2
    freqs = np.float32(rope_base) ** (
        -(np.arange(half, dtype=np.float32) * np.float32(2.0) / np.float32(2 * half))
    )
    angles = np.arange(LENGTH, dtype=np.float32)[:, None] * freqs.astype(np.float32)[None, :]
    cos, sin = np.cos(angles), np.sin(angles)
    return (
        np.concatenate([cos, cos], axis=1).astype(np.float32),
        np.concatenate([-sin, sin], axis=1).astype(np.float32),
    )


def coords():
    dp, sq = lax.axis_index("dp"), lax.axis_index("seq")
    return dp // AXIS, dp % AXIS, sq // 2, sq % 2


def device(y, z, x, c):
    return (y * AXIS + z, x * 2 + c)


def seq_peers(y, z, x, c):
    return [
        (k, j, device(y, z, (x + k) % AXIS, (c + j) % 2))
        for k in range(AXIS)
        for j in range(2)
        if (k, j) != (0, 0)
    ]


def barrier(peers):
    sem = pltpu.get_barrier_semaphore()
    for peer in peers:
        pl.semaphore_signal(sem, inc=1, device_id=peer, device_id_type=MESH)
    pl.semaphore_wait(sem, len(peers))


class Copies:
    def __init__(self, send, recv, local):
        self.send, self.recv, self.local = send, recv, local
        self.n, self.n_local = 0, 0
        self.sent = []

    def to(self, src, dst, dev):
        copy = pltpu.make_async_remote_copy(
            src_ref=src, dst_ref=dst, send_sem=self.send.at[self.n], recv_sem=self.recv.at[self.n],
            device_id=dev, device_id_type=MESH,
        )
        self.n += 1
        copy.start()
        self.sent.append(copy)
        return copy

    def here(self, src, dst):
        copy = pltpu.make_async_copy(src, dst, self.local.at[self.n_local])
        self.n_local += 1
        copy.start()
        return copy

    def finish(self):
        for copy in self.sent:
            copy.wait_send()
        self.sent = []


class SeqGather:
    def __init__(self, cm, own, buf, co):
        self.cm, self.own, self.buf, self.co = cm, own, buf, co
        self.half = buf.shape[1] // 2

    def slot(self, k):
        y, z, x, c = self.co
        return self.buf.at[((x + k) % AXIS) * 2 + c]

    def start(self):
        y, z, x, c = self.co
        self.sib = device(y, z, x, 1 - c)
        self.plus, self.minus = device(y, z, (x + 1) % AXIS, c), device(y, z, (x + 3) % AXIS, c)
        self.a = self.cm.to(self.own, self.slot(0), self.plus)
        self.b = self.cm.to(self.own, self.slot(0), self.minus)
        self.s0 = self.cm.to(self.own, self.slot(0), self.sib)
        self.l = self.cm.here(self.own, self.slot(0))

    def forward(self):
        h = self.half
        lo, hi = pl.ds(0, h), pl.ds(h, h)
        self.a.wait_recv()
        left = self.slot(3)
        self.fa = self.cm.to(left.at[lo], left.at[lo], self.plus)
        self.s1 = self.cm.to(left, left, self.sib)
        self.b.wait_recv()
        right = self.slot(1)
        self.fb = self.cm.to(right.at[hi], right.at[hi], self.minus)
        self.s2 = self.cm.to(right, right, self.sib)

    def last(self):
        h = self.half
        lo, hi = pl.ds(0, h), pl.ds(h, h)
        opp = self.slot(2)
        self.fa.wait_recv()
        self.s3 = self.cm.to(opp.at[lo], opp.at[lo], self.sib)
        self.fb.wait_recv()
        self.s4 = self.cm.to(opp.at[hi], opp.at[hi], self.sib)

    def wait_chip(self, k):
        if k == 0:
            self.l.wait()
            self.s0.wait_recv()
        elif k == 3:
            self.s1.wait_recv()
        elif k == 1:
            self.s2.wait_recv()
        else:
            self.s3.wait_recv()
            self.s4.wait_recv()


class DpGather:
    def __init__(self, cm, own, buf, co, axis):
        self.cm, self.own, self.buf, self.co, self.axis = cm, own, buf, co, axis
        n = own.shape[axis]
        self.h, self.q = n // 2, n // 4

    def part(self, ref, half, quarter=None):
        lo = half * self.h + (0 if quarter is None else quarter * self.q)
        size = self.h if quarter is None else self.q
        cut = pl.ds(lo, size)
        lead = len(ref.shape) - 2
        index = (slice(None),) * lead + ((cut, slice(None)) if self.axis == 0 else (slice(None), cut))
        return ref.at[index]

    def both(self, src_p, dst_p, src_m, dst_m, along):
        y, z, x, c = self.co
        if along == 0:
            plus, minus = device((y + 1) % AXIS, z, x, c), device((y + 3) % AXIS, z, x, c)
        else:
            plus, minus = device(y, (z + 1) % AXIS, x, c), device(y, (z + 3) % AXIS, x, c)
        return (self.cm.to(src_p, dst_p, plus), self.cm.to(src_m, dst_m, minus))

    def start(self):
        y, z, _, _ = self.co
        mine = self.buf.at[y, z]
        self.l = self.cm.here(self.own, mine)
        self.one = []
        for half in (0, 1):
            src, dst = self.part(self.own, half), self.part(mine, half)
            self.one.append(self.both(src, dst, src, dst, half))

    def spread(self):
        y, z, _, _ = self.co
        self.two = []
        for half in (0, 1):
            if half == 0:
                left, right = self.buf.at[(y + 3) % AXIS, z], self.buf.at[(y + 1) % AXIS, z]
            else:
                left, right = self.buf.at[y, (z + 3) % AXIS], self.buf.at[y, (z + 1) % AXIS]
            for copy in self.one[half]:
                copy.wait_recv()
            lp, rp = self.part(left, half, 0), self.part(right, half, 1)
            self.two.append(self.both(lp, lp, rp, rp, half))

    def line(self, half, k):
        y, z, _, _ = self.co
        if half == 0:
            return self.buf.at[:, (z + k) % AXIS]
        return self.buf.at[(y + k) % AXIS]

    def turn(self):
        self.l.wait()
        self.three = []
        for half in (0, 1):
            for copy in self.two[half]:
                copy.wait_recv()
            mine = self.part(self.line(half, 0), half)
            self.three.append(self.both(mine, mine, mine, mine, 1 - half))

    def last(self):
        self.four = []
        for half in (0, 1):
            for copy in self.three[half]:
                copy.wait_recv()
            lp = self.part(self.line(half, 3), half, 0)
            rp = self.part(self.line(half, 1), half, 1)
            self.four.append(self.both(lp, lp, rp, rp, 1 - half))

    def wait(self):
        for half in (0, 1):
            for copy in self.four[half]:
                copy.wait_recv()


def off(n):
    return jnp.where(n == 0, 2, jnp.where(n == 1, 1, jnp.where(n == 2, 3, 0)))


class SeqScatter:
    def __init__(self, part, sib_recv, x_recv, sems, co):
        self.part, self.sib_recv, self.x_recv, self.sems, self.co = part, sib_recv, x_recv, sems, co

    def sib_copy(self, n):
        y, z, x, c = self.co
        return pltpu.make_async_remote_copy(
            src_ref=self.part.at[2 * n], dst_ref=self.sib_recv.at[n],
            send_sem=self.sems.at[0, n], recv_sem=self.sems.at[1, n],
            device_id=device(y, z, x, 1 - c), device_id_type=MESH,
        )

    def x_copy(self, n):
        y, z, x, c = self.co
        return pltpu.make_async_remote_copy(
            src_ref=self.part.at[2 * n + 1], dst_ref=self.x_recv.at[n],
            send_sem=self.sems.at[2, n], recv_sem=self.sems.at[3, n],
            device_id=device(y, z, (x + off(n)) % AXIS, c), device_id_type=MESH,
        )

    def combine(self, n):
        self.sib_copy(n).wait_recv()
        rows = self.part.shape[1]

        def add(i, _):
            cut = pl.ds(i * 32, 32)
            total = self.part[2 * n + 1, cut, :].astype(f32) + self.sib_recv[n, cut, :].astype(f32)
            self.part[2 * n + 1, cut, :] = total.astype(bf16)
            return 0

        lax.fori_loop(0, rows // 32, add, 0)

        @pl.when(n < 3)
        def _():
            self.x_copy(n).start()

    def arrive(self):
        for n in range(3):
            self.x_copy(n).wait_recv()

    def rows(self, cut):
        total = self.part[7, cut, :].astype(f32)
        for n in range(3):
            total = total + self.x_recv[n, cut, :].astype(f32)
        return total

    def finish(self):
        for n in range(4):
            self.sib_copy(n).wait_send()
        for n in range(3):
            self.x_copy(n).wait_send()


def scatter_scratch():
    return [
        pltpu.VMEM((8, SPAN, WIDTH), bf16),
        pltpu.VMEM((4, SPAN, WIDTH), bf16),
        pltpu.VMEM((3, SPAN, WIDTH), bf16),
        pltpu.SemaphoreType.DMA((4, 4)),
    ]


def swap(u):
    return pltpu.roll(u, HEAD_DIM // 2, 1)


def attn_forward_kernel(
    tok, cot, pq, pm, wd, wo, cos, sin,
    x1_o, h2_o, h1_o, pre_o, qb, kb, vb, ob, lse, gains, gq_o, gm, gd, wo_o, cot_o,
    xg, a2a_q, a2a_m, wq, wo_b, wo_v, o1, o2, o3, part, sib_recv, x_recv, rs_sems, send, recv, local,
):
    co = y, z, x, c = coords()
    s = x * 2 + c
    peers = seq_peers(*co)
    yp = [device((y + k) % AXIS, z, x, c) for k in (1, 2, 3)]
    zp = [device(y, (z + k) % AXIS, x, c) for k in (1, 2, 3)]
    barrier([p for _, _, p in peers] + yp + zp)
    cm = Copies(send, recv, local)

    aq = []
    for k, j, p in peers:
        t = ((x + k) % AXIS) * 2 + (c + j) % 2
        aq.append(cm.to(pq.at[t], a2a_q.at[s], p))
    lq = cm.here(pq.at[s], a2a_q.at[s])
    g_tok = SeqGather(cm, tok, xg, co)
    g_tok.start()
    o_one = [
        cm.to(wo.at[:, pl.ds(pl.multiple_of(((y + k) % AXIS) * 512, 512), 512)], o1.at[y], yp[k - 1])
        for k in (1, 2, 3)
    ]
    l_one = cm.here(wo.at[:, pl.ds(pl.multiple_of(y * 512, 512), 512)], o1.at[y])
    g_d = DpGather(cm, wd, gd, co, 1)
    g_d.start()
    am = []
    for k, j, p in peers:
        t = ((x + k) % AXIS) * 2 + (c + j) % 2
        am.append(cm.to(pm.at[t], a2a_m.at[s], p))
    lm = cm.here(pm.at[s], a2a_m.at[s])
    lq.wait()
    for copy in aq:
        copy.wait_recv()
    g_q = DpGather(cm, a2a_q.reshape(NS * WR, QKV + GCOL), gq_o, co, 0)
    g_q.start()
    l_one.wait()
    for copy in o_one:
        copy.wait_recv()
    o_two = [
        cm.to(o1.at[:, :, pl.ds(pl.multiple_of(((z + k) % AXIS) * 128, 128), 128)], o2.at[z], zp[k - 1])
        for k in (1, 2, 3)
    ]
    l_two = cm.here(o1.at[:, :, pl.ds(pl.multiple_of(z * 128, 128), 128)], o2.at[z])
    g_tok.forward()
    g_q.spread()
    g_q.turn()
    lm.wait()
    for copy in am:
        copy.wait_recv()
    g_m = DpGather(cm, a2a_m.reshape(NS * WR, 2 * FFS), gm, co, 0)
    g_m.start()
    l_two.wait()
    for copy in o_two:
        copy.wait_recv()
    o_three = []
    for k, j, p in peers:
        t = ((x + k) % AXIS) * 2 + (c + j) % 2
        for h in range(2):
            o_three.append(cm.to(o2.at[(t % 2) * 2 + h, t // 2], o3.at[h, s], p))
    l_three = [cm.here(o2.at[(s % 2) * 2 + h, s // 2], o3.at[h, s]) for h in range(2)]
    g_tok.last()
    g_d.spread()
    g_q.last()
    for copy in l_three:
        copy.wait()
    for copy in o_three:
        copy.wait_recv()
    g_o = DpGather(cm, o3.reshape(2 * SPAN, SPAN), wo_b, co, 0)
    g_o.start()
    g_cot = SeqGather(cm, cot, cot_o, co)
    for k in (0, 1, 3, 2):
        g_tok.wait_chip(k)
    g_cot.start()
    g_m.spread()
    g_o.spread()
    g_q.wait()
    wq_copy = [
        cm.here(gq_o.at[yy], wq.at[pl.ds(yy * AXIS, AXIS)]) for yy in range(AXIS)
    ]
    g_o.turn()
    g_d.turn()
    g_m.turn()
    for copy in wq_copy:
        copy.wait()

    wq2 = wq.reshape(WIDTH, QKV + GCOL)
    gcols = wq2[:, QKV:]
    flat = gcols.astype(f32).T
    gains[...] = flat[:8]
    gain_one, gain_two = flat[0:1], flat[1:2]
    rows = lax.broadcasted_iota(jnp.int32, (WIDTH, HEAD_DIM), 0)
    cols = lax.broadcasted_iota(jnp.int32, (WIDTH, HEAD_DIM), 1)
    pick = (rows == cols * WR).astype(bf16)
    head_gains = dot_tn(gcols, pick)
    gain_q, gain_k = head_gains[2:3], head_gains[3:4]
    gains[2:4, 0:HEAD_DIM] = head_gains[2:4]

    def normed(i, _):
        cut = pl.ds(i * 32, 32)
        v = xg[i // 4, pl.ds((i % 4) * 32, 32), :].astype(f32)
        part[i // 4, pl.ds((i % 4) * 32, 32), :] = (v * rms(v) * gain_one).astype(bf16)
        return 0

    lax.fori_loop(0, LENGTH // 32, normed, 0)
    h1_copy = cm.here(part, h1_o)

    def project(i, _):
        h = part[pl.ds(2 * i, 2)].reshape(2 * SPAN, WIDTH)
        p = dot(h, wq2[:, :QKV])
        cut = pl.ds(pl.multiple_of(i * 256, 256), 256)
        pre_o[cut, :] = p[:, :384]
        vb[cut, :] = p[:, 384:].astype(bf16)
        co_t, si_t = cos[cut, :], sin[cut, :]
        for h_i in range(2):
            u = p[:, h_i * 128 : h_i * 128 + 128]
            u = u * rms(u) * gain_q
            u = (u * co_t + swap(u) * si_t).astype(bf16)
            qb[pl.ds(2 * i, 2), pl.ds(h_i * SPAN, SPAN), :] = u.reshape(2, SPAN, HEAD_DIM)
        u = p[:, 256:384]
        u = u * rms(u) * gain_k
        kb[cut, :] = (u * co_t + swap(u) * si_t).astype(bf16)
        return 0

    lax.fori_loop(0, 4, project, 0)
    g_cot.forward()
    g_o.last()
    h1_copy.wait()
    g_o.wait()
    wo_copy = [
        cm.here(wo_b.at[yy, zz], wo_v.at[:, pl.ds((yy * AXIS + zz) * 128, 128)])
        for yy in range(AXIS)
        for zz in range(AXIS)
    ]
    for copy in wo_copy:
        copy.wait()
    wo_out = cm.here(wo_v, wo_o)

    rs = SeqScatter(part, sib_recv, x_recv, rs_sems, co)

    def attend(i, slot):
        sc = dot_nt(qb[i], kb[...]) * score_scale
        r = lax.broadcasted_iota(jnp.int32, (2 * SPAN, LENGTH), 0) % SPAN + i * SPAN
        k = lax.broadcasted_iota(jnp.int32, (2 * SPAN, LENGTH), 1)
        sc = jnp.where(k <= r, sc, -1e30)
        top = jnp.max(sc, axis=-1, keepdims=True)
        ex = jnp.exp(sc - top)
        tot = jnp.sum(ex, axis=-1, keepdims=True)
        lse[i] = jnp.broadcast_to(top + jnp.log(tot), (2 * SPAN, 128))
        pb = (ex / tot).astype(bf16)
        o = dot(pb, vb[...]).astype(bf16)
        o = jnp.concatenate([o[:SPAN], o[SPAN:]], axis=1)
        ob[pl.ds(pl.multiple_of(i * SPAN, SPAN), SPAN), :] = o
        part[slot] = dot(o, wo_v[...]).astype(bf16)

    def pair(n, _):
        chip = (x + off(n)) % AXIS
        attend(chip * 2 + 1 - c, 2 * n)
        rs.sib_copy(n).start()
        attend(chip * 2 + c, 2 * n + 1)
        rs.combine(n)
        return 0

    lax.fori_loop(0, 4, pair, 0)
    g_cot.last()
    g_d.last()
    g_m.last()
    rs.arrive()

    def residual(i, _):
        cut = pl.ds(i * 32, 32)
        v = xg[s, cut, :].astype(f32) + rs.rows(cut)
        x1_o[cut, :] = v
        h2_o[cut, :] = (v * rms(v) * gains[1:2, :]).astype(bf16)
        return 0

    lax.fori_loop(0, SPAN // 32, residual, 0)
    rs.finish()
    wo_out.wait()
    for k in (0, 1, 3, 2):
        g_cot.wait_chip(k)
    g_d.wait()
    g_m.wait()
    cm.finish()


def attn_forward(tok, cot, pq, pm, wd, wo, cos, sin):
    any_, vm = pl.BlockSpec(memory_space=pl.ANY), pl.BlockSpec(memory_space=pltpu.VMEM)
    sds = jax.ShapeDtypeStruct
    n_copies, n_local = 160, 48
    return pl.pallas_call(
        attn_forward_kernel,
        name="attn_forward",
        out_shape=[
            sds((SPAN, WIDTH), f32), sds((SPAN, WIDTH), bf16), sds((8, SPAN, WIDTH), bf16),
            sds((LENGTH, 384), f32), sds((8, 2 * SPAN, 128), bf16), sds((LENGTH, 128), bf16),
            sds((LENGTH, 128), bf16), sds((LENGTH, 256), bf16), sds((8, 2 * SPAN, 128), f32),
            sds((8, WIDTH), f32), sds((4, 4, 128, QKV + GCOL), bf16), sds((4, 4, 128, 2 * FFS), bf16),
            sds((4, 4, FR, WIDTH), bf16), sds((256, WIDTH), bf16), sds((8, SPAN, WIDTH), bf16),
        ],
        in_specs=[any_] * 6 + [vm] * 2,
        out_specs=[vm, vm, any_, vm, vm, vm, vm, vm, vm, vm, any_, any_, any_, any_, any_],
        scratch_shapes=[
            pltpu.VMEM((8, SPAN, WIDTH), bf16),
            pltpu.VMEM((NS, WR, QKV + GCOL), bf16),
            pltpu.VMEM((NS, WR, 2 * FFS), bf16),
            pltpu.VMEM((ND, 128, QKV + GCOL), bf16),
            pltpu.VMEM((4, 4, 256, 128), bf16),
            pltpu.VMEM((256, WIDTH), bf16),
            pltpu.VMEM((4, WR, 512), bf16),
            pltpu.VMEM((4, 4, WR, 128), bf16),
            pltpu.VMEM((2, NS, WR, 128), bf16),
            *scatter_scratch(),
            pltpu.SemaphoreType.DMA((n_copies,)),
            pltpu.SemaphoreType.DMA((n_copies,)),
            pltpu.SemaphoreType.DMA((n_local,)),
        ],
        compiler_params=pltpu.CompilerParams(
            collective_id=1, has_side_effects=True, vmem_limit_bytes=VMEM_LIMIT
        ),
    )(tok, cot, pq, pm, wd, wo, cos, sin)


def shards(
    tokens, gain_attn, w_query, key_weight, value_weight, w_out, gain_query,
    key_norm_gain, gain_mlp, w_gate, w_up, w_down, cotangent,
):
    qw, kw = 256, 128
    extra = jnp.stack(
        [
            gain_attn,
            gain_mlp,
            jnp.broadcast_to(gain_query, (WR,)),
            jnp.broadcast_to(key_norm_gain, (WR,)),
        ],
        axis=1,
    )
    extra = jnp.broadcast_to(jnp.pad(extra, ((0, 0), (0, GCOL - 4)))[:, None], (WR, NS, GCOL))
    pq = jnp.concatenate(
        [
            w_query.reshape(WR, NS, qw),
            key_weight.reshape(WR, NS, kw),
            value_weight.reshape(WR, NS, kw),
            extra,
        ],
        axis=2,
    ).transpose(1, 0, 2)
    pm = jnp.concatenate(
        [
            w.reshape(WR, ND, NS, FR).transpose(2, 0, 1, 3).reshape(NS, WR, FFS)
            for w in (w_gate, w_up)
        ],
        axis=2,
    )
    cos, sin = rope_constants()
    (x1, h2_loc, h1, pre, qb, kb, vb, ob, lse, gains, gq, gm, gd, wo, dyb) = attn_forward(
        tokens[0], cotangent[0], pq, pm, w_down, w_out, cos, sin
    )
    gain_one, gain_two = gains[0:1], gains[1:2]
    gain_q, gain_k = gains[2:3, :128], gains[3:4, :128]
    qkv_mat = gq.reshape(WIDTH, QKV + GCOL)[:, :QKV]
    mlp_mat = gm.reshape(WIDTH, 2 * FFS)
    gate_mat, up_mat = mlp_mat[:, :FFS], mlp_mat[:, FFS:]
    down_mat = gd.reshape(FFS, WIDTH)
    h1 = h1.reshape(LENGTH, WIDTH)
    dyb = dyb.reshape(LENGTH, WIDTH)
    x_loc = tokens[0].astype(f32)
    heads = 2
    length, ns, nd, wr, ff, fr, out_mat = LENGTH, NS, ND, WR, FFS, FR, wo
    d2, cw = 2, 128
    q_pre = pre[:, :qw].reshape(length, heads, HEAD_DIM)
    k_pre = pre[:, qw:].reshape(length, 1, HEAD_DIM)
    inv_q, inv_k = rms(q_pre), rms(k_pre)
    unit_q, unit_k = q_pre * inv_q, k_pre * inv_k
    qb = qb.reshape(8, 2, SPAN, HEAD_DIM).transpose(0, 2, 1, 3).reshape(length, heads, HEAD_DIM)
    lse = lse[:, :, 0].reshape(8, 2, SPAN).transpose(1, 0, 2).reshape(2, length, 1)
    cos_h, sin_h = jnp.asarray(cos[:, :64]), jnp.asarray(sin[:, 64:])

    def unrotate(grads):
        a, b = grads[..., :64], grads[..., 64:]
        co, si = cos_h[:, None, :], sin_h[:, None, :]
        return jnp.concatenate([a * co + b * si, b * co - a * si], axis=-1)

    inv_two = rms(x1)
    unit_two = x1 * inv_two
    h2 = lax.all_gather(h2_loc, "seq", axis=0, tiled=True)
    dy = cotangent[0].astype(f32)
    gate = dot(h2, gate_mat)
    up = dot(h2, up_mat)
    sig = jax.nn.sigmoid(gate)
    silu = gate * sig
    hid = (silu * up).astype(bf16)
    dhid = dot_nt(dyb, down_mat)
    dgate = (dhid * up * (sig * (1.0 + gate * (1.0 - sig)))).astype(bf16)
    dup = (dhid * silu).astype(bf16)
    dh2 = (dot_nt(dgate, gate_mat) + dot_nt(dup, up_mat)).astype(bf16)
    dh2 = lax.psum_scatter(dh2, "seq", scatter_dimension=0, tiled=True).astype(f32)
    dx1 = dy + rms_back(dh2, gain_two, unit_two, inv_two)
    g_gain_two = jnp.sum(dh2 * unit_two, axis=0)
    part = dot(hid, down_mat).astype(bf16)
    block = x1 + lax.psum_scatter(part, "seq", scatter_dimension=0, tiled=True).astype(f32)
    block_out = block.astype(bf16)[None]
    g_down = dot_tn(hid, dyb).astype(bf16)
    g_mlp = jnp.concatenate([dot_tn(h2, dgate), dot_tn(h2, dup)], axis=1).astype(bf16)
    g_down = lax.psum_scatter(g_down, "dp", scatter_dimension=0, tiled=True).astype(f32)
    g_mlp = lax.psum_scatter(g_mlp, "dp", scatter_dimension=0, tiled=True)
    g_mlp = lax.all_to_all(g_mlp.reshape(ns, wr, 2 * ff), "seq", 0, 0, tiled=True)
    g_mlp = g_mlp.astype(f32).reshape(ns, wr, 2, nd, fr).transpose(2, 1, 3, 0, 4)
    g_mlp = g_mlp.reshape(2, wr, nd * ns * fr)

    allowed = (
        jnp.arange(length, dtype=jnp.int32)[None, :]
        <= jnp.arange(length, dtype=jnp.int32)[:, None]
    )
    score = jnp.einsum("qhd,kd->hqk", qb, kb, preferred_element_type=f32) * score_scale
    prob = jnp.where(allowed, jnp.exp(score - lse), 0.0)
    pb = prob.astype(bf16)
    dab = lax.all_gather(dx1.astype(bf16), "seq", axis=0, tiled=True)
    g_out = dot_tn(ob, dab).astype(bf16)
    dob = dot_nt(dab, out_mat).astype(bf16).reshape(length, heads, HEAD_DIM)
    dprob = jnp.einsum("qhd,kd->hqk", dob, vb, preferred_element_type=f32)
    delta = jnp.sum(prob * dprob, axis=-1, keepdims=True)
    dscore = (prob * (dprob - delta)).astype(bf16)
    dq = jnp.einsum("hqk,kd->qhd", dscore, kb, preferred_element_type=f32) * score_scale
    dk = jnp.einsum("hqk,qhd->kd", dscore, qb, preferred_element_type=f32) * score_scale
    dv = jnp.einsum("hqk,qhd->kd", pb, dob, preferred_element_type=f32)
    dq = unrotate(dq)
    dk = unrotate(dk[:, None])
    g_gain_q = jnp.sum(dq * unit_q, axis=(0, 1))
    g_gain_k = jnp.sum(dk * unit_k, axis=(0, 1))
    dqp = rms_back(dq, gain_q, unit_q, inv_q).reshape(length, qw)
    dkp = rms_back(dk, gain_k, unit_k, inv_k).reshape(length, kw)
    dqkv = jnp.concatenate([dqp, dkp, dv], axis=1).astype(bf16)
    dh1 = dot_nt(dqkv, qkv_mat).astype(bf16)
    dh1 = lax.psum_scatter(dh1, "seq", scatter_dimension=0, tiled=True).astype(f32)
    inv_one = rms(x_loc)
    unit_loc = x_loc * inv_one
    grad_tokens = (dx1 + rms_back(dh1, gain_one, unit_loc, inv_one))[None]
    g_gain_one = jnp.sum(dh1 * unit_loc, axis=0)
    g_qkv = dot_tn(h1, dqkv).astype(bf16)
    g_qkv = lax.psum_scatter(g_qkv, "dp", scatter_dimension=0, tiled=True)
    g_qkv = lax.all_to_all(g_qkv.reshape(ns, wr, -1), "seq", 0, 0, tiled=True).astype(f32)
    g_q = g_qkv[:, :, :qw].transpose(1, 0, 2).reshape(wr, -1)
    g_k = g_qkv[:, :, qw : qw + kw].transpose(1, 0, 2).reshape(wr, -1)
    g_v = g_qkv[:, :, qw + kw :].transpose(1, 0, 2).reshape(wr, -1)
    g_out = lax.psum_scatter(g_out, "dp", scatter_dimension=1, tiled=True)
    g_out = g_out.reshape(d2, ns, wr, cw).transpose(0, 2, 1, 3).reshape(d2 * wr, ns * cw)
    g_out = lax.all_to_all(g_out, "seq", 1, 0, tiled=True)
    g_out = lax.all_to_all(g_out, "dp", 0, 1, tiled=True).astype(f32)

    gg = jnp.concatenate(
        [
            g_gain_one.reshape(nd * ns, wr),
            g_gain_two.reshape(nd * ns, wr),
            g_gain_q[:, None],
            g_gain_k[:, None],
        ],
        axis=1,
    )
    gg = jnp.pad(gg, ((0, 0), (0, 128 - gg.shape[1])))
    gg = lax.psum_scatter(gg, "dp", scatter_dimension=0, tiled=True)
    gg = jnp.sum(lax.all_to_all(gg[:, None], "seq", 0, 1, tiled=True)[0], axis=0)
    return (
        block_out, grad_tokens, gg[:wr], g_q, g_k, g_v, g_out,
        gg[2 * wr : 2 * wr + 1], gg[2 * wr + 1 : 2 * wr + 2], gg[wr : 2 * wr],
        g_mlp[0], g_mlp[1], g_down,
    )


def solution(mesh):
    both = P(("dp", "seq"))
    rows = P(("dp", "seq"), None)
    act = P("dp", "seq", None)
    in_specs = (act, both, rows, rows, rows, rows, both, both, both, rows, rows, rows, act)
    out_specs = (act, act, both, rows, rows, rows, rows, both, both, both, rows, rows, rows)
    return jax.shard_map(
        shards, mesh=mesh, in_specs=in_specs, out_specs=out_specs, check_vma=False
    )
```

```python
import functools
import math

import jax
import jax.numpy as jnp
import numpy as np
from jax import lax
from jax.experimental import pallas as pl
from jax.experimental.pallas import tpu as pltpu
from jax.sharding import PartitionSpec as P

QUERY_HEADS = 16
KEY_VALUE_HEADS = 8
HEAD_DIM = 128

eps_norm = 1e-06
rope_base = 1000000.0
score_scale = 1.0 / math.sqrt(HEAD_DIM)

f32 = jnp.float32
bf16 = jnp.bfloat16

AXIS = 4
ND, NS = 16, 8
SPAN = 128
WIDTH = 2048
LENGTH = SPAN * NS
WR = 16
FR = 48
FFS = ND * FR
QKV = 512
GCOL = 128
VMEM_LIMIT = 60 * 2**20
MESH = pl.DeviceIdType.MESH


def dot(a, b):
    return jnp.dot(a, b, preferred_element_type=f32)


def dot_tn(a, b):
    return lax.dot_general(a, b, (((0,), (0,)), ((), ())), preferred_element_type=f32)


def dot_nt(a, b):
    return lax.dot_general(a, b, (((1,), (1,)), ((), ())), preferred_element_type=f32)


def rms(values):
    return lax.rsqrt(jnp.mean(values * values, axis=-1, keepdims=True) + eps_norm)


def rms_back(grad_out, gain, unit, inv):
    grad_unit = grad_out * gain
    return inv * (grad_unit - unit * jnp.mean(grad_unit * unit, axis=-1, keepdims=True))


def rope_constants():
    half = HEAD_DIM // 2
    freqs = np.float32(rope_base) ** (
        -(np.arange(half, dtype=np.float32) * np.float32(2.0) / np.float32(2 * half))
    )
    angles = np.arange(LENGTH, dtype=np.float32)[:, None] * freqs.astype(np.float32)[None, :]
    cos, sin = np.cos(angles), np.sin(angles)
    return (
        np.concatenate([cos, cos], axis=1).astype(np.float32),
        np.concatenate([-sin, sin], axis=1).astype(np.float32),
    )


def coords():
    dp, sq = lax.axis_index("dp"), lax.axis_index("seq")
    return dp // AXIS, dp % AXIS, sq // 2, sq % 2


def device(y, z, x, c):
    return (y * AXIS + z, x * 2 + c)


def seq_peers(y, z, x, c):
    return [
        (k, j, device(y, z, (x + k) % AXIS, (c + j) % 2))
        for k in range(AXIS)
        for j in range(2)
        if (k, j) != (0, 0)
    ]


def barrier(peers):
    sem = pltpu.get_barrier_semaphore()
    for peer in peers:
        pl.semaphore_signal(sem, inc=1, device_id=peer, device_id_type=MESH)
    pl.semaphore_wait(sem, len(peers))


class Copies:
    def __init__(self, send, recv, local):
        self.send, self.recv, self.local = send, recv, local
        self.n, self.n_local = 0, 0
        self.sent = []

    def to(self, src, dst, dev):
        copy = pltpu.make_async_remote_copy(
            src_ref=src, dst_ref=dst, send_sem=self.send.at[self.n], recv_sem=self.recv.at[self.n],
            device_id=dev, device_id_type=MESH,
        )
        self.n += 1
        copy.start()
        self.sent.append(copy)
        return copy

    def here(self, src, dst):
        copy = pltpu.make_async_copy(src, dst, self.local.at[self.n_local])
        self.n_local += 1
        copy.start()
        return copy

    def finish(self):
        for copy in self.sent:
            copy.wait_send()
        self.sent = []


class SeqGather:
    def __init__(self, cm, own, buf, co):
        self.cm, self.own, self.buf, self.co = cm, own, buf, co
        self.half = buf.shape[1] // 2

    def slot(self, k):
        y, z, x, c = self.co
        return self.buf.at[((x + k) % AXIS) * 2 + c]

    def start(self):
        y, z, x, c = self.co
        self.sib = device(y, z, x, 1 - c)
        self.plus, self.minus = device(y, z, (x + 1) % AXIS, c), device(y, z, (x + 3) % AXIS, c)
        self.a = self.cm.to(self.own, self.slot(0), self.plus)
        self.b = self.cm.to(self.own, self.slot(0), self.minus)
        self.s0 = self.cm.to(self.own, self.slot(0), self.sib)
        self.l = self.cm.here(self.own, self.slot(0))

    def forward(self):
        h = self.half
        lo, hi = pl.ds(0, h), pl.ds(h, h)
        self.a.wait_recv()
        left = self.slot(3)
        self.fa = self.cm.to(left.at[lo], left.at[lo], self.plus)
        self.s1 = self.cm.to(left, left, self.sib)
        self.b.wait_recv()
        right = self.slot(1)
        self.fb = self.cm.to(right.at[hi], right.at[hi], self.minus)
        self.s2 = self.cm.to(right, right, self.sib)

    def last(self):
        h = self.half
        lo, hi = pl.ds(0, h), pl.ds(h, h)
        opp = self.slot(2)
        self.fa.wait_recv()
        self.s3 = self.cm.to(opp.at[lo], opp.at[lo], self.sib)
        self.fb.wait_recv()
        self.s4 = self.cm.to(opp.at[hi], opp.at[hi], self.sib)

    def wait_chip(self, k):
        if k == 0:
            self.l.wait()
            self.s0.wait_recv()
        elif k == 3:
            self.s1.wait_recv()
        elif k == 1:
            self.s2.wait_recv()
        else:
            self.s3.wait_recv()
            self.s4.wait_recv()


class DpGather:
    def __init__(self, cm, own, buf, co, axis):
        self.cm, self.own, self.buf, self.co, self.axis = cm, own, buf, co, axis
        n = own.shape[axis]
        self.h, self.q = n // 2, n // 4

    def part(self, ref, half, quarter=None):
        lo = half * self.h + (0 if quarter is None else quarter * self.q)
        size = self.h if quarter is None else self.q
        cut = pl.ds(lo, size)
        lead = len(ref.shape) - 2
        index = (slice(None),) * lead + ((cut, slice(None)) if self.axis == 0 else (slice(None), cut))
        return ref.at[index]

    def both(self, src_p, dst_p, src_m, dst_m, along):
        y, z, x, c = self.co
        if along == 0:
            plus, minus = device((y + 1) % AXIS, z, x, c), device((y + 3) % AXIS, z, x, c)
        else:
            plus, minus = device(y, (z + 1) % AXIS, x, c), device(y, (z + 3) % AXIS, x, c)
        return (self.cm.to(src_p, dst_p, plus), self.cm.to(src_m, dst_m, minus))

    def start(self):
        y, z, _, _ = self.co
        mine = self.buf.at[y, z]
        self.l = self.cm.here(self.own, mine)
        self.one = []
        for half in (0, 1):
            src, dst = self.part(self.own, half), self.part(mine, half)
            self.one.append(self.both(src, dst, src, dst, half))

    def spread(self):
        y, z, _, _ = self.co
        self.two = []
        for half in (0, 1):
            if half == 0:
                left, right = self.buf.at[(y + 3) % AXIS, z], self.buf.at[(y + 1) % AXIS, z]
            else:
                left, right = self.buf.at[y, (z + 3) % AXIS], self.buf.at[y, (z + 1) % AXIS]
            for copy in self.one[half]:
                copy.wait_recv()
            lp, rp = self.part(left, half, 0), self.part(right, half, 1)
            self.two.append(self.both(lp, lp, rp, rp, half))

    def line(self, half, k):
        y, z, _, _ = self.co
        if half == 0:
            return self.buf.at[:, (z + k) % AXIS]
        return self.buf.at[(y + k) % AXIS]

    def turn(self):
        self.l.wait()
        self.three = []
        for half in (0, 1):
            for copy in self.two[half]:
                copy.wait_recv()
            mine = self.part(self.line(half, 0), half)
            self.three.append(self.both(mine, mine, mine, mine, 1 - half))

    def last(self):
        self.four = []
        for half in (0, 1):
            for copy in self.three[half]:
                copy.wait_recv()
            lp = self.part(self.line(half, 3), half, 0)
            rp = self.part(self.line(half, 1), half, 1)
            self.four.append(self.both(lp, lp, rp, rp, 1 - half))

    def wait(self):
        for half in (0, 1):
            for copy in self.four[half]:
                copy.wait_recv()


def off(n):
    return jnp.where(n == 0, 2, jnp.where(n == 1, 1, jnp.where(n == 2, 3, 0)))


class SeqScatter:
    def __init__(self, part, sib_recv, x_recv, sems, co, kept=None):
        self.part, self.sib_recv, self.x_recv, self.sems, self.co = part, sib_recv, x_recv, sems, co
        self.kept = kept

    def ours(self, n):
        return self.part.at[2 * n + 1] if self.kept is None else self.kept.at[n]

    def sib_copy(self, n):
        y, z, x, c = self.co
        return pltpu.make_async_remote_copy(
            src_ref=self.part.at[2 * n], dst_ref=self.sib_recv.at[n],
            send_sem=self.sems.at[0, n], recv_sem=self.sems.at[1, n],
            device_id=device(y, z, x, 1 - c), device_id_type=MESH,
        )

    def x_copy(self, n):
        y, z, x, c = self.co
        return pltpu.make_async_remote_copy(
            src_ref=self.ours(n), dst_ref=self.x_recv.at[n],
            send_sem=self.sems.at[2, n], recv_sem=self.sems.at[3, n],
            device_id=device(y, z, (x + off(n)) % AXIS, c), device_id_type=MESH,
        )

    def combine(self, n, go=True):
        self.sib_copy(n).wait_recv()
        ours = self.ours(n)

        def add(i, _):
            cut = pl.ds(i * 32, 32)
            total = ours[cut, :].astype(f32) + self.sib_recv[n, cut, :].astype(f32)
            ours[cut, :] = total.astype(bf16)
            return 0

        lax.fori_loop(0, SPAN // 32, add, 0)
        if go:

            @pl.when(n < 3)
            def _():
                self.x_copy(n).start()

    def arrive(self):
        for n in range(3):
            self.x_copy(n).wait_recv()

    def rows(self, cut):
        total = self.ours(3)[cut, :].astype(f32)
        for n in range(3):
            total = total + self.x_recv[n, cut, :].astype(f32)
        return total

    def finish(self):
        for n in range(4):
            self.sib_copy(n).wait_send()
        for n in range(3):
            self.x_copy(n).wait_send()


def scatter_scratch():
    return [
        pltpu.VMEM((8, SPAN, WIDTH), bf16),
        pltpu.VMEM((4, SPAN, WIDTH), bf16),
        pltpu.VMEM((3, SPAN, WIDTH), bf16),
        pltpu.SemaphoreType.DMA((4, 4)),
    ]


def swap(u):
    return pltpu.roll(u, HEAD_DIM // 2, 1)


def attn_forward_kernel(
    tok, cot, pq, pm, wd, wo, cos, sin,
    x1_o, h2_o, h1_o, pre_o, qb, kb, vb, ob, lse, gains, gq_o, gm, gd, wo_o, cot_o,
    xg, a2a_q, a2a_m, wq, wo_b, wo_v, o1, o2, o3, part, sib_recv, x_recv, rs_sems, send, recv, local,
):
    co = y, z, x, c = coords()
    s = x * 2 + c
    peers = seq_peers(*co)
    yp = [device((y + k) % AXIS, z, x, c) for k in (1, 2, 3)]
    zp = [device(y, (z + k) % AXIS, x, c) for k in (1, 2, 3)]
    barrier([p for _, _, p in peers] + yp + zp)
    cm = Copies(send, recv, local)

    aq = []
    for k, j, p in peers:
        t = ((x + k) % AXIS) * 2 + (c + j) % 2
        aq.append(cm.to(pq.at[t], a2a_q.at[s], p))
    lq = cm.here(pq.at[s], a2a_q.at[s])
    g_tok = SeqGather(cm, tok, xg, co)
    g_tok.start()
    o_one = [
        cm.to(wo.at[:, pl.ds(pl.multiple_of(((y + k) % AXIS) * 512, 512), 512)], o1.at[y], yp[k - 1])
        for k in (1, 2, 3)
    ]
    l_one = cm.here(wo.at[:, pl.ds(pl.multiple_of(y * 512, 512), 512)], o1.at[y])
    g_d = DpGather(cm, wd, gd, co, 1)
    g_d.start()
    am = []
    for k, j, p in peers:
        t = ((x + k) % AXIS) * 2 + (c + j) % 2
        am.append(cm.to(pm.at[t], a2a_m.at[s], p))
    lm = cm.here(pm.at[s], a2a_m.at[s])
    lq.wait()
    for copy in aq:
        copy.wait_recv()
    g_q = DpGather(cm, a2a_q.reshape(NS * WR, QKV + GCOL), gq_o, co, 0)
    g_q.start()
    l_one.wait()
    for copy in o_one:
        copy.wait_recv()
    o_two = [
        cm.to(o1.at[:, :, pl.ds(pl.multiple_of(((z + k) % AXIS) * 128, 128), 128)], o2.at[z], zp[k - 1])
        for k in (1, 2, 3)
    ]
    l_two = cm.here(o1.at[:, :, pl.ds(pl.multiple_of(z * 128, 128), 128)], o2.at[z])
    g_tok.forward()
    g_q.spread()
    g_q.turn()
    lm.wait()
    for copy in am:
        copy.wait_recv()
    g_m = DpGather(cm, a2a_m.reshape(NS * WR, 2 * FFS), gm, co, 0)
    g_m.start()
    l_two.wait()
    for copy in o_two:
        copy.wait_recv()
    o_three = []
    for k, j, p in peers:
        t = ((x + k) % AXIS) * 2 + (c + j) % 2
        for h in range(2):
            o_three.append(cm.to(o2.at[(t % 2) * 2 + h, t // 2], o3.at[h, s], p))
    l_three = [cm.here(o2.at[(s % 2) * 2 + h, s // 2], o3.at[h, s]) for h in range(2)]
    g_tok.last()
    g_d.spread()
    g_q.last()
    for copy in l_three:
        copy.wait()
    for copy in o_three:
        copy.wait_recv()
    g_o = DpGather(cm, o3.reshape(2 * SPAN, SPAN), wo_b, co, 0)
    g_o.start()
    g_cot = SeqGather(cm, cot, cot_o, co)
    for k in (0, 1, 3, 2):
        g_tok.wait_chip(k)
    g_cot.start()
    g_m.spread()
    g_o.spread()
    g_q.wait()
    wq_copy = [
        cm.here(gq_o.at[yy], wq.at[pl.ds(yy * AXIS, AXIS)]) for yy in range(AXIS)
    ]
    g_o.turn()
    g_d.turn()
    g_m.turn()
    for copy in wq_copy:
        copy.wait()

    wq2 = wq.reshape(WIDTH, QKV + GCOL)
    gcols = wq2[:, QKV:]
    flat = gcols.astype(f32).T
    gains[...] = flat[:8]
    gain_one, gain_two = flat[0:1], flat[1:2]
    rows = lax.broadcasted_iota(jnp.int32, (WIDTH, HEAD_DIM), 0)
    cols = lax.broadcasted_iota(jnp.int32, (WIDTH, HEAD_DIM), 1)
    pick = (rows == cols * WR).astype(bf16)
    head_gains = dot_tn(gcols, pick)
    gain_q, gain_k = head_gains[2:3], head_gains[3:4]
    gains[2:4, 0:HEAD_DIM] = head_gains[2:4]

    def normed(i, _):
        cut = pl.ds(i * 32, 32)
        v = xg[i // 4, pl.ds((i % 4) * 32, 32), :].astype(f32)
        part[i // 4, pl.ds((i % 4) * 32, 32), :] = (v * rms(v) * gain_one).astype(bf16)
        return 0

    lax.fori_loop(0, LENGTH // 32, normed, 0)
    h1_copy = cm.here(part, h1_o)

    def project(i, _):
        h = part[pl.ds(2 * i, 2)].reshape(2 * SPAN, WIDTH)
        p = dot(h, wq2[:, :QKV])
        cut = pl.ds(pl.multiple_of(i * 256, 256), 256)
        pre_o[cut, :] = p[:, :384]
        vb[cut, :] = p[:, 384:].astype(bf16)
        co_t, si_t = cos[cut, :], sin[cut, :]
        for h_i in range(2):
            u = p[:, h_i * 128 : h_i * 128 + 128]
            u = u * rms(u) * gain_q
            u = (u * co_t + swap(u) * si_t).astype(bf16)
            qb[pl.ds(2 * i, 2), pl.ds(h_i * SPAN, SPAN), :] = u.reshape(2, SPAN, HEAD_DIM)
        u = p[:, 256:384]
        u = u * rms(u) * gain_k
        kb[cut, :] = (u * co_t + swap(u) * si_t).astype(bf16)
        return 0

    lax.fori_loop(0, 4, project, 0)
    g_cot.forward()
    g_o.last()
    h1_copy.wait()
    g_o.wait()
    wo_copy = [
        cm.here(wo_b.at[yy, zz], wo_v.at[:, pl.ds((yy * AXIS + zz) * 128, 128)])
        for yy in range(AXIS)
        for zz in range(AXIS)
    ]
    for copy in wo_copy:
        copy.wait()
    wo_out = cm.here(wo_v, wo_o)

    rs = SeqScatter(part, sib_recv, x_recv, rs_sems, co)

    def attend(i, slot):
        sc = dot_nt(qb[i], kb[...]) * score_scale
        r = lax.broadcasted_iota(jnp.int32, (2 * SPAN, LENGTH), 0) % SPAN + i * SPAN
        k = lax.broadcasted_iota(jnp.int32, (2 * SPAN, LENGTH), 1)
        sc = jnp.where(k <= r, sc, -1e30)
        top = jnp.max(sc, axis=-1, keepdims=True)
        ex = jnp.exp(sc - top)
        tot = jnp.sum(ex, axis=-1, keepdims=True)
        lse[i] = jnp.broadcast_to(top + jnp.log(tot), (2 * SPAN, 128))
        pb = (ex / tot).astype(bf16)
        o = dot(pb, vb[...]).astype(bf16)
        o = jnp.concatenate([o[:SPAN], o[SPAN:]], axis=1)
        ob[pl.ds(pl.multiple_of(i * SPAN, SPAN), SPAN), :] = o
        part[slot] = dot(o, wo_v[...]).astype(bf16)

    def pair(n, _):
        chip = (x + off(n)) % AXIS
        attend(chip * 2 + 1 - c, 2 * n)
        rs.sib_copy(n).start()
        attend(chip * 2 + c, 2 * n + 1)
        rs.combine(n)
        return 0

    lax.fori_loop(0, 4, pair, 0)
    g_cot.last()
    g_d.last()
    g_m.last()
    rs.arrive()

    def residual(i, _):
        cut = pl.ds(i * 32, 32)
        v = xg[s, cut, :].astype(f32) + rs.rows(cut)
        x1_o[cut, :] = v
        h2_o[cut, :] = (v * rms(v) * gains[1:2, :]).astype(bf16)
        return 0

    lax.fori_loop(0, SPAN // 32, residual, 0)
    rs.finish()
    wo_out.wait()
    for k in (0, 1, 3, 2):
        g_cot.wait_chip(k)
    g_d.wait()
    g_m.wait()
    cm.finish()


def attn_forward(tok, cot, pq, pm, wd, wo, cos, sin):
    any_, vm = pl.BlockSpec(memory_space=pl.ANY), pl.BlockSpec(memory_space=pltpu.VMEM)
    sds = jax.ShapeDtypeStruct
    n_copies, n_local = 160, 48
    return pl.pallas_call(
        attn_forward_kernel,
        name="attn_forward",
        out_shape=[
            sds((SPAN, WIDTH), f32), sds((SPAN, WIDTH), bf16), sds((8, SPAN, WIDTH), bf16),
            sds((LENGTH, 384), f32), sds((8, 2 * SPAN, 128), bf16), sds((LENGTH, 128), bf16),
            sds((LENGTH, 128), bf16), sds((LENGTH, 256), bf16), sds((8, 2 * SPAN, 128), f32),
            sds((8, WIDTH), f32), sds((4, 4, 128, QKV + GCOL), bf16), sds((4, 4, 128, 2 * FFS), bf16),
            sds((4, 4, FR, WIDTH), bf16), sds((256, WIDTH), bf16), sds((8, SPAN, WIDTH), bf16),
        ],
        in_specs=[any_] * 6 + [vm] * 2,
        out_specs=[vm, vm, any_, vm, vm, vm, vm, vm, vm, vm, any_, any_, any_, any_, any_],
        scratch_shapes=[
            pltpu.VMEM((8, SPAN, WIDTH), bf16),
            pltpu.VMEM((NS, WR, QKV + GCOL), bf16),
            pltpu.VMEM((NS, WR, 2 * FFS), bf16),
            pltpu.VMEM((ND, 128, QKV + GCOL), bf16),
            pltpu.VMEM((4, 4, 256, 128), bf16),
            pltpu.VMEM((256, WIDTH), bf16),
            pltpu.VMEM((4, WR, 512), bf16),
            pltpu.VMEM((4, 4, WR, 128), bf16),
            pltpu.VMEM((2, NS, WR, 128), bf16),
            *scatter_scratch(),
            pltpu.SemaphoreType.DMA((n_copies,)),
            pltpu.SemaphoreType.DMA((n_copies,)),
            pltpu.SemaphoreType.DMA((n_local,)),
        ],
        compiler_params=pltpu.CompilerParams(
            collective_id=1, has_side_effects=True, vmem_limit_bytes=VMEM_LIMIT
        ),
    )(tok, cot, pq, pm, wd, wo, cos, sin)


def mlp_kernel(
    h2_loc, dyg, gm, gd, x1, cot, gains,
    dx1_o, dab_o, gain_o, ggu_o, gwd_o, pd_o,
    h2g, dy_v, wgu, wd, hid, dgu, ggu, gwd, pdv,
    part, sib_recv, x_recv, rs_sems, send, recv, local,
):
    co = y, z, x, c = coords()
    peers = seq_peers(*co)
    cm = Copies(send, recv, local)
    loads = [
        cm.here(gm, wgu),
        cm.here(dyg, dy_v),
        cm.here(gd, wd),
    ]
    barrier([p for _, _, p in peers])
    g_h2 = SeqGather(cm, h2_loc, h2g, co)
    g_h2.start()
    rs = SeqScatter(part, sib_recv, x_recv, rs_sems, co)
    wgu2 = wgu.reshape(WIDTH, 2 * FFS)
    wd2 = wd.reshape(FFS, WIDTH)
    order = {2: 0, 1: 1, 3: 2, 0: 3}
    for copy in loads:
        copy.wait()

    def chip_of(k):
        return (x + k) % AXIS

    def forward(k):
        chip = chip_of(k)
        rows = pl.ds(pl.multiple_of(chip * 256, 256), 256)
        two = pl.ds(2 * chip, 2)

        def tile(f, _):
            lo = pl.multiple_of(f * 256, 256)
            h = h2g[two].reshape(256, WIDTH)
            gate = dot(h, wgu2[:, pl.ds(lo, 256)])
            up = dot(h, wgu2[:, pl.ds(pl.multiple_of(lo + FFS, 256), 256)])
            dh = dot_nt(dy_v[two].reshape(256, WIDTH), wd2[pl.ds(lo, 256), :])
            sig = jax.nn.sigmoid(gate)
            silu = gate * sig
            hid[rows, pl.ds(lo, 256)] = (silu * up).astype(bf16)
            dgate = dh * up * (sig * (1.0 + gate * (1.0 - sig)))
            dgu[rows, pl.ds(lo, 256)] = dgate.astype(bf16)
            dgu[rows, pl.ds(pl.multiple_of(lo + FFS, 256), 256)] = (dh * silu).astype(bf16)
            return 0

        lax.fori_loop(0, FFS // 256, tile, 0)

    def put(ref, n, cols, o):
        ref[2 * n + 1 - c, :, cols] = o[:SPAN]
        ref[2 * n + c, :, cols] = o[SPAN:]

    def back(k):
        n = order[k]
        rows = pl.ds(pl.multiple_of(chip_of(k) * 256, 256), 256)

        def tile(m, _):
            cols = pl.ds(pl.multiple_of(m * 256, 256), 256)
            put(part, n, cols, dot_nt(dgu[rows, :], wgu2[cols, :]).astype(bf16))
            return 0

        lax.fori_loop(0, WIDTH // 256, tile, 0)
        rs.sib_copy(n).start()

    g_h2.wait_chip(0)
    forward(0)
    g_h2.forward()
    back(0)
    g_h2.wait_chip(3)
    forward(3)
    g_h2.last()
    back(3)
    g_h2.wait_chip(1)
    forward(1)
    rs.combine(order[3])
    back(1)
    g_h2.wait_chip(2)
    forward(2)
    rs.combine(order[1])
    back(2)
    rs.combine(order[0])

    def gate_up(m, _):
        cols = pl.ds(pl.multiple_of(m * 256, 256), 256)
        ggu[cols, :] = dot_tn(h2g[:, :, cols].reshape(LENGTH, 256), dgu[...]).astype(bf16)
        return 0

    lax.fori_loop(0, 1, gate_up, 0)
    rs.combine(order[2])
    lax.fori_loop(1, WIDTH // 256, gate_up, 0)
    outs = [cm.here(ggu, ggu_o)]

    for k in range(4):
        n = order[k]
        rows = pl.ds(pl.multiple_of(chip_of(k) * 256, 256), 256)

        def down(m, _):
            cols = pl.ds(pl.multiple_of(m * 512, 512), 512)
            put(pdv, n, cols, dot(hid[rows, :], wd2[:, cols]).astype(bf16))
            return 0

        lax.fori_loop(0, WIDTH // 512, down, 0)
    outs.append(cm.here(pdv, pd_o))

    def down_grad(m, _):
        cols = pl.ds(pl.multiple_of(m * 256, 256), 256)
        gwd[cols, :] = dot_tn(hid[:, cols], dy_v[...].reshape(LENGTH, WIDTH)).astype(bf16)
        return 0

    lax.fori_loop(0, FFS // 256, down_grad, 0)
    outs.append(cm.here(gwd, gwd_o))
    rs.arrive()
    gain_two = gains[1:2, :]

    def residual(i, acc):
        cut = pl.ds(i * 32, 32)
        v = x1[cut, :]
        inv = rms(v)
        unit = v * inv
        dh2 = rs.rows(cut)
        dx1 = cot[cut, :].astype(f32) + rms_back(dh2, gain_two, unit, inv)
        dx1_o[cut, :] = dx1
        dab_o[cut, :] = dx1.astype(bf16)
        return acc + jnp.sum(dh2 * unit, axis=0, keepdims=True)

    acc = lax.fori_loop(0, SPAN // 32, residual, jnp.zeros((1, WIDTH), f32))
    gain_o[...] = jnp.broadcast_to(acc, (8, WIDTH))
    rs.finish()
    for copy in outs:
        copy.wait()
    cm.finish()


def mlp(h2_loc, dyg, gm, gd, x1, cot, gains):
    any_, vm = pl.BlockSpec(memory_space=pl.ANY), pl.BlockSpec(memory_space=pltpu.VMEM)
    sds = jax.ShapeDtypeStruct
    n_copies, n_local = 9, 8
    return pl.pallas_call(
        mlp_kernel,
        name="feed_forward",
        out_shape=[
            sds((SPAN, WIDTH), f32), sds((SPAN, WIDTH), bf16), sds((8, WIDTH), f32),
            sds((WIDTH, 2 * FFS), bf16), sds((FFS, WIDTH), bf16), sds((8, SPAN, WIDTH), bf16),
        ],
        in_specs=[any_] * 4 + [vm] * 3,
        out_specs=[vm, vm, vm, any_, any_, any_],
        scratch_shapes=[
            pltpu.VMEM((8, SPAN, WIDTH), bf16),
            pltpu.VMEM((8, SPAN, WIDTH), bf16),
            pltpu.VMEM((4, 4, 128, 2 * FFS), bf16),
            pltpu.VMEM((4, 4, FR, WIDTH), bf16),
            pltpu.VMEM((LENGTH, FFS), bf16),
            pltpu.VMEM((LENGTH, 2 * FFS), bf16),
            pltpu.VMEM((WIDTH, 2 * FFS), bf16),
            pltpu.VMEM((FFS, WIDTH), bf16),
            pltpu.VMEM((8, SPAN, WIDTH), bf16),
            *scatter_scratch(),
            pltpu.SemaphoreType.DMA((n_copies,)),
            pltpu.SemaphoreType.DMA((n_copies,)),
            pltpu.SemaphoreType.DMA((n_local,)),
        ],
        compiler_params=pltpu.CompilerParams(
            collective_id=2, has_side_effects=True, vmem_limit_bytes=VMEM_LIMIT
        ),
    )(h2_loc, dyg, gm, gd, x1, cot, gains)


class DpScatter:
    def __init__(self, cm, grad, acc, one, two, co, axis, tile):
        self.cm, self.grad, self.acc, self.r1, self.r2 = cm, grad, acc, one, two
        self.co, self.axis, self.tile = co, axis, tile
        self.h = grad.shape[2 + axis] // 2

    def part(self, ref, half):
        cut = pl.ds(half * self.h, self.h)
        lead = (slice(None),) * (len(ref.shape) - 2)
        return ref.at[lead + ((cut, slice(None)) if self.axis == 0 else (slice(None), cut))]

    def line(self, half, k):
        y, z, _, _ = self.co
        if half == 0:
            return self.part(self.grad.at[(y + k) % AXIS], half)
        return self.part(self.grad.at[:, (z + k) % AXIS], half)

    def away(self, along, k):
        y, z, x, c = self.co
        if along == 0:
            return device((y + k) % AXIS, z, x, c)
        return device(y, (z + k) % AXIS, x, c)

    def start(self):
        self.own = [self.cm.here(self.line(h, 0), self.acc.at[h]) for h in (0, 1)]
        self.first = [[], []]
        for k in (2, 1, 3):
            for h in (0, 1):
                self.first[h].append(
                    self.cm.to(self.line(h, k), self.r1.at[h, k - 1], self.away(h, k))
                )

    def mid(self):
        y, z, _, _ = self.co
        rows = self.acc.shape[2]
        self.second = [[], []]
        for h in (0, 1):
            self.own[h].wait()
            for copy in self.first[h]:
                copy.wait_recv()

            def add(t, _, h=h):
                q = t // (rows // self.tile)
                cut = pl.ds((t % (rows // self.tile)) * self.tile, self.tile)
                total = self.acc[h, q, cut, :].astype(f32)
                for k in range(3):
                    total = total + self.r1[h, k, q, cut, :].astype(f32)
                self.acc[h, q, cut, :] = total.astype(bf16)
                return 0

            lax.fori_loop(0, AXIS * (rows // self.tile), add, 0)
            mine = z if h == 0 else y
            for k in (2, 1, 3):
                self.second[h].append(
                    self.cm.to(self.acc.at[h, (mine + k) % AXIS], self.r2.at[h, k - 1], self.away(1 - h, k))
                )

    def last(self, out):
        y, z, _, _ = self.co
        rows, cols = self.acc.shape[2:]
        for h in (0, 1):
            for copy in self.second[h]:
                copy.wait_recv()
            mine = z if h == 0 else y

            def add(t, _, h=h, mine=mine):
                cut = pl.ds(t * self.tile, self.tile)
                total = self.acc[h, mine, cut, :].astype(f32)
                for k in range(3):
                    total = total + self.r2[h, k, cut, :].astype(f32)
                if self.axis == 0:
                    out[pl.ds(h * self.h + t * self.tile, self.tile), :] = total.astype(out.dtype)
                else:
                    out[cut, pl.ds(h * self.h, self.h)] = total.astype(out.dtype)
                return 0

            lax.fori_loop(0, rows // self.tile, add, 0)


def dp_scatter_scratch(rows, cols):
    return [
        pltpu.VMEM((2, AXIS, rows, cols), bf16),
        pltpu.VMEM((2, 3, AXIS, rows, cols), bf16),
        pltpu.VMEM((2, 3, rows, cols), bf16),
    ]


def attn_backward_kernel(
    dab_loc, pd, ggu, gwd, h1, gq, wo,
    dx1, tok, x1, gain2, pre, qb, kb, vb, ob, lse, gains, cos, sin,
    gt_o, block_o, gu_o, gwd_o, gqkv_o, gwo_o, gg_o,
    dab, h1_v, wq, wo_v, pbuf, dob, dk, dv, dqkv, gacc,
    part, sib_recv, x_recv, rs_sems, kept, sib2, x2, rs2_sems,
    m_acc, m_one, m_two, d_acc, d_one, d_two, o_acc, o_one, o_two, q_acc, q_one, q_two,
    mo, go, oo, o2g, o1g, ow, gqk, qo, gg, g_one, g_two, g_all, g_sum,
    send, recv, local,
):
    co = y, z, x, c = coords()
    s = x * 2 + c
    peers = seq_peers(*co)
    yp = [device((y + k) % AXIS, z, x, c) for k in (1, 2, 3)]
    zp = [device(y, (z + k) % AXIS, x, c) for k in (1, 2, 3)]
    cm = Copies(send, recv, local)
    l_wo = cm.here(wo, wo_v)
    l_pd = [cm.here(pd.at[2 * n + 1], kept.at[n]) for n in range(4)]
    l_wq = cm.here(gq.at[:, :, :, pl.ds(0, QKV)], wq)

    def h1_load(m):
        return cm.here(h1.at[:, :, pl.ds(m * 256, 256)], h1_v.at[m % 2])

    l_h1 = [h1_load(0), h1_load(1)]
    barrier([p for _, _, p in peers] + yp + zp)
    g_dab = SeqGather(cm, dab_loc, dab, co)
    g_dab.start()
    r_m = DpScatter(cm, ggu, m_acc, m_one, m_two, co, 0, 16)
    r_d = DpScatter(cm, gwd, d_acc, d_one, d_two, co, 1, 16)
    r_m.start()
    r_d.start()
    rs2 = SeqScatter(pd, sib2, x2, rs2_sems, co, kept)
    for n in range(4):
        l_pd[n].wait()
        rs2.sib_copy(n).start()

    def probs(i, _):
        sc = dot_nt(qb[i], kb[...]) * score_scale
        r = lax.broadcasted_iota(jnp.int32, (2 * SPAN, LENGTH), 0) % SPAN + i * SPAN
        k = lax.broadcasted_iota(jnp.int32, (2 * SPAN, LENGTH), 1)
        p = jnp.where(k <= r, jnp.exp(sc - lse[i][:, 0:1]), 0.0)
        pbuf[i] = p.astype(bf16)
        return 0

    lax.fori_loop(0, 4, probs, 0)
    g_dab.forward()
    lax.fori_loop(4, 8, probs, 0)
    dk[...] = jnp.zeros_like(dk)
    dv[...] = jnp.zeros_like(dv)
    gacc[...] = jnp.zeros_like(gacc)
    l_wo.wait()

    def out_back(k):
        g_dab.wait_chip(k)
        two = pl.ds(2 * ((x + k) % AXIS), 2)
        o = dot_nt(dab[two].reshape(2 * SPAN, WIDTH), wo_v[...]).astype(bf16)
        for j in range(2):
            blk = o[j * SPAN : (j + 1) * SPAN]
            dob[2 * ((x + k) % AXIS) + j] = jnp.concatenate([blk[:, :128], blk[:, 128:]], axis=0)

    out_back(0)
    out_back(3)
    out_back(1)
    for n in range(4):
        rs2.combine(n, False)
    g_dab.last()
    out_back(2)

    def out_grad(m, _):
        cols = pl.ds(pl.multiple_of(m * 512, 512), 512)
        o = dot_tn(ob[...], dab[:, :, cols].reshape(LENGTH, 512)).astype(bf16)
        for j in range(AXIS):
            go[m, j] = o[:, j * 128 : j * 128 + 128]
        return 0

    lax.fori_loop(0, AXIS, out_grad, 0)
    r_o = DpScatter(cm, go, o_acc, o_one, o_two, co, 0, 128)
    r_o.start()

    rs = SeqScatter(part, sib_recv, x_recv, rs_sems, co)
    l_wq.wait()
    wq2 = wq.reshape(WIDTH, QKV)
    gain_q, gain_k = gains[2:3, 0:128], gains[3:4, 0:128]

    def head_back(g, u, gain, co_t, si_t):
        g = g * co_t - swap(g) * si_t
        inv = rms(u)
        unit = u * inv
        return rms_back(g, gain, unit, inv), jnp.sum(g * unit, axis=0, keepdims=True)

    def slot_of(chip):
        k = (chip - x + AXIS) % AXIS
        return jnp.where(k == 2, 0, jnp.where(k == 1, 1, jnp.where(k == 3, 2, 3)))

    def chip_back(t, _):
        chip = 3 - t

        def block(j, _):
            i = chip * 2 + 1 - j
            q, do, p = qb[i], dob[i], pbuf[i]
            dp = dot_nt(do, vb[...])
            pf = p.astype(f32)
            delta = jnp.sum(pf * dp, axis=-1, keepdims=True)
            ds = (pf * (dp - delta)).astype(bf16)
            dk[...] += dot_tn(ds, q)
            dv[...] += dot_tn(p, do)
            dq = dot(ds, kb[...]) * score_scale
            cut = pl.ds(pl.multiple_of(i * SPAN, SPAN), SPAN)
            u = jnp.concatenate([pre[cut, 0:128], pre[cut, 128:256]], axis=0)
            co_t = jnp.concatenate([cos[cut, :]] * 2, axis=0)
            si_t = jnp.concatenate([sin[cut, :]] * 2, axis=0)
            dqp, gsum = head_back(dq, u, gain_q, co_t, si_t)
            gacc[0:1, :] += gsum
            dqp = dqp.astype(bf16)
            dqkv[cut, 0:128] = dqp[:SPAN]
            dqkv[cut, 128:256] = dqp[SPAN:]
            return 0

        lax.fori_loop(0, 2, block, 0)
        cut = pl.ds(pl.multiple_of(chip * 256, 256), 256)
        dkp, gsum = head_back(dk[cut, :] * score_scale, pre[cut, 256:384], gain_k, cos[cut, :], sin[cut, :])
        gacc[1:2, :] += gsum
        dqkv[cut, 256:384] = dkp.astype(bf16)
        dqkv[cut, 384:512] = dv[cut, :].astype(bf16)
        n = slot_of(chip)

        def tile(m, _):
            cols = pl.ds(pl.multiple_of(m * 512, 512), 512)
            o = dot_nt(dqkv[cut, :], wq2[cols, :]).astype(bf16)
            part[2 * n + 1 - c, :, cols] = o[:SPAN]
            part[2 * n + c, :, cols] = o[SPAN:]
            return 0

        lax.fori_loop(0, WIDTH // 512, tile, 0)
        rs.sib_copy(n).start()
        rs.combine(n)
        return 0

    lax.fori_loop(0, 4, chip_back, 0)

    for m in range(8):
        l_h1[m].wait()
        o = dot_tn(h1_v[m % 2].reshape(LENGTH, 256), dqkv[...]).astype(bf16)
        gqk[m // 2, 2 * (m % 2)] = o[:SPAN]
        gqk[m // 2, 2 * (m % 2) + 1] = o[SPAN:]
        if m < 6:
            l_h1.append(h1_load(m + 2))
    r_q = DpScatter(cm, gqk, q_acc, q_one, q_two, co, 0, 64)
    r_q.start()
    for n in range(3):
        rs2.x_copy(n).start()
    r_m.mid()
    r_d.mid()
    r_o.mid()

    rs.arrive()
    gain_one = gains[0:1, :]

    def input_back(i, acc):
        cut = pl.ds(i * 32, 32)
        v = tok[cut, :].astype(f32)
        inv = rms(v)
        unit = v * inv
        dh1 = rs.rows(cut)
        gt_o[cut, :] = dx1[cut, :] + rms_back(dh1, gain_one, unit, inv)
        return acc + jnp.sum(dh1 * unit, axis=0, keepdims=True)

    gain1 = lax.fori_loop(0, SPAN // 32, input_back, jnp.zeros((1, WIDTH), f32))

    dev_i = lax.broadcasted_iota(jnp.int32, (ND * NS, WIDTH), 0)
    col_j = lax.broadcasted_iota(jnp.int32, (ND * NS, WIDTH), 1)
    mine = col_j // WR == dev_i
    row_j = lax.broadcasted_iota(jnp.int32, (WIDTH, 128), 0)
    lane = lax.broadcasted_iota(jnp.int32, (WIDTH, 128), 1)
    rows = jnp.zeros((ND * NS, 128), f32)
    for v, shift in ((gain1, 0), (gain2[0:1, :], WR)):
        rows = rows + dot(
            jnp.where(mine, v, 0.0).astype(bf16), (lane == row_j % WR + shift).astype(bf16)
        )
    eye_i = lax.broadcasted_iota(jnp.int32, (128, 128), 0)
    eye_j = lax.broadcasted_iota(jnp.int32, (128, 128), 1)
    for n in range(2):
        rows = rows + dot(
            jnp.where(eye_i == eye_j, gacc[n : n + 1, :], 0.0).astype(bf16),
            (eye_j == 2 * WR + n).astype(bf16),
        )
    gg[...] = rows.reshape(AXIS, AXIS, NS, 128)
    g_first = [cm.to(gg.at[(y + k) % AXIS], g_one.at[k - 1], yp[k - 1]) for k in (1, 2, 3)]
    r_q.mid()
    for copy in g_first:
        copy.wait_recv()
    gg[y] = gg[y] + g_one[0] + g_one[1] + g_one[2]
    g_second = [cm.to(gg.at[y, (z + k) % AXIS], g_two.at[k - 1], zp[k - 1]) for k in (1, 2, 3)]

    r_m.last(mo.reshape(NS * WR, 2 * FFS))
    a2a = []
    for k, j, p in peers:
        t = ((x + k) % AXIS) * 2 + (c + j) % 2
        a2a.append(cm.to(mo.at[t], gu_o.at[s], p))
    l_mo = cm.here(mo.at[s], gu_o.at[s])
    r_o.last(oo.reshape(2 * SPAN, SPAN))
    o_three = []
    for k, j, p in peers:
        t = ((x + k) % AXIS) * 2 + (c + j) % 2
        for h in range(2):
            o_three.append(cm.to(oo.at[h, t], o2g.at[(s % 2) * 2 + h, s // 2], p))
    l_three = [cm.here(oo.at[h, s], o2g.at[(s % 2) * 2 + h, s // 2]) for h in range(2)]
    r_d.last(gwd_o)
    rs2.arrive()

    def out_rows(i, _):
        cut = pl.ds(i * 32, 32)
        block_o[cut, :] = (x1[cut, :] + rs2.rows(cut)).astype(bf16)
        return 0

    lax.fori_loop(0, SPAN // 32, out_rows, 0)
    for copy in l_three:
        copy.wait()
    for copy in o_three:
        copy.wait_recv()
    o_two_c = [
        cm.to(o2g.at[(z + k) % AXIS], o1g.at[:, :, pl.ds(pl.multiple_of(z * 128, 128), 128)], zp[k - 1])
        for k in (1, 2, 3)
    ]
    l_two = cm.here(o2g.at[z], o1g.at[:, :, pl.ds(pl.multiple_of(z * 128, 128), 128)])
    for copy in g_second:
        copy.wait_recv()
    g_all[s] = gg[y, z] + g_two[0] + g_two[1] + g_two[2]
    g_third = [cm.to(g_all.at[s], g_all.at[s], p) for _, _, p in peers]
    r_q.last(qo.reshape(NS * WR, QKV))
    for k, j, p in peers:
        t = ((x + k) % AXIS) * 2 + (c + j) % 2
        a2a.append(cm.to(qo.at[t], gqkv_o.at[s], p))
    l_qo = cm.here(qo.at[s], gqkv_o.at[s])
    l_two.wait()
    for copy in o_two_c:
        copy.wait_recv()
    o_one_c = [
        cm.to(o1g.at[(y + k) % AXIS], ow.at[:, pl.ds(pl.multiple_of(y * 512, 512), 512)], yp[k - 1])
        for k in (1, 2, 3)
    ]
    l_one = cm.here(o1g.at[y], ow.at[:, pl.ds(pl.multiple_of(y * 512, 512), 512)])
    for copy in g_third:
        copy.wait_recv()
    total = g_all[0]
    for t in range(1, NS):
        total = total + g_all[t]
    g_sum[...] = total
    gg_o[...] = jnp.broadcast_to(g_sum[pl.ds(s, 1), :], (8, 128))
    l_one.wait()
    for copy in o_one_c:
        copy.wait_recv()
    gwo_o[...] = ow[...].astype(f32)
    l_mo.wait()
    l_qo.wait()
    for copy in a2a:
        copy.wait_recv()
    rs.finish()
    rs2.finish()
    cm.finish()


def attn_backward(dab_loc, pd, ggu, gwd, h1, gq, wo, *rest):
    any_, vm = pl.BlockSpec(memory_space=pl.ANY), pl.BlockSpec(memory_space=pltpu.VMEM)
    sds = jax.ShapeDtypeStruct
    vmem = pltpu.VMEM
    n_copies, n_local = 128, 32
    return pl.pallas_call(
        attn_backward_kernel,
        name="attn_backward",
        out_shape=[
            sds((SPAN, WIDTH), f32), sds((SPAN, WIDTH), bf16), sds((NS, WR, 2 * FFS), bf16),
            sds((FR, WIDTH), f32), sds((NS, WR, QKV), bf16), sds((WR, WIDTH), f32), sds((8, 128), f32),
        ],
        in_specs=[any_] * 7 + [vm] * len(rest),
        out_specs=[vm, vm, any_, vm, any_, vm, vm],
        scratch_shapes=[
            vmem((8, SPAN, WIDTH), bf16), vmem((2, 8, SPAN, 256), bf16),
            vmem((4, 4, 128, QKV), bf16), vmem((256, WIDTH), bf16),
            vmem((8, 2 * SPAN, LENGTH), bf16), vmem((8, 2 * SPAN, 128), bf16),
            vmem((LENGTH, 128), f32), vmem((LENGTH, 128), f32), vmem((LENGTH, QKV), bf16),
            vmem((8, 128), f32),
            *scatter_scratch(), vmem((4, SPAN, WIDTH), bf16), *scatter_scratch()[1:],
            *dp_scatter_scratch(64, 2 * FFS), *dp_scatter_scratch(FR, WIDTH // 2),
            *dp_scatter_scratch(SPAN, 128), *dp_scatter_scratch(64, QKV),
            vmem((NS, WR, 2 * FFS), bf16), vmem((4, 4, 256, 128), bf16), vmem((2, NS, WR, 128), bf16),
            vmem((4, 4, WR, 128), bf16), vmem((4, WR, 512), bf16), vmem((WR, WIDTH), bf16),
            vmem((4, 4, SPAN, QKV), bf16), vmem((NS, WR, QKV), bf16),
            vmem((4, 4, NS, 128), f32), vmem((3, 4, NS, 128), f32), vmem((3, NS, 128), f32),
            vmem((NS, NS, 128), f32), vmem((NS, 128), f32),
            pltpu.SemaphoreType.DMA((n_copies,)),
            pltpu.SemaphoreType.DMA((n_copies,)),
            pltpu.SemaphoreType.DMA((n_local,)),
        ],
        compiler_params=pltpu.CompilerParams(
            collective_id=3, has_side_effects=True, vmem_limit_bytes=VMEM_LIMIT
        ),
    )(dab_loc, pd, ggu, gwd, h1, gq, wo, *rest)


def shards(
    tokens, gain_attn, w_query, key_weight, value_weight, w_out, gain_query,
    key_norm_gain, gain_mlp, w_gate, w_up, w_down, cotangent,
):
    qw, kw = 256, 128
    extra = jnp.stack(
        [
            gain_attn,
            gain_mlp,
            jnp.broadcast_to(gain_query, (WR,)),
            jnp.broadcast_to(key_norm_gain, (WR,)),
        ],
        axis=1,
    )
    extra = jnp.broadcast_to(jnp.pad(extra, ((0, 0), (0, GCOL - 4)))[:, None], (WR, NS, GCOL))
    pq = jnp.concatenate(
        [
            w_query.reshape(WR, NS, qw),
            key_weight.reshape(WR, NS, kw),
            value_weight.reshape(WR, NS, kw),
            extra,
        ],
        axis=2,
    ).transpose(1, 0, 2)
    pm = jnp.concatenate(
        [
            w.reshape(WR, ND, NS, FR).transpose(2, 0, 1, 3).reshape(NS, WR, FFS)
            for w in (w_gate, w_up)
        ],
        axis=2,
    )
    cos, sin = rope_constants()
    (x1, h2_loc, h1, pre, qb, kb, vb, ob, lse, gains, gq, gm, gd, wo, dyb) = attn_forward(
        tokens[0], cotangent[0], pq, pm, w_down, w_out, cos, sin
    )
    dx1, dab_loc, gain2, ggu, gwd, pd = mlp(h2_loc, dyb, gm, gd, x1, cotangent[0], gains)
    gt, block, g_gu, g_down, g_qkv, g_out, gg = attn_backward(
        dab_loc, pd, ggu.reshape(4, 4, 128, 2 * FFS), gwd.reshape(4, 4, FR, WIDTH), h1, gq, wo,
        dx1, tokens[0], x1, gain2, pre, qb, kb, vb, ob, lse, gains, cos, sin,
    )
    g_mlp = g_gu.astype(f32).reshape(NS, WR, 2, ND, FR).transpose(2, 1, 3, 0, 4)
    g_mlp = g_mlp.reshape(2, WR, ND * NS * FR)
    g_qkv = g_qkv.astype(f32)
    g_q = g_qkv[:, :, :qw].transpose(1, 0, 2).reshape(WR, -1)
    g_k = g_qkv[:, :, qw : qw + kw].transpose(1, 0, 2).reshape(WR, -1)
    g_v = g_qkv[:, :, qw + kw :].transpose(1, 0, 2).reshape(WR, -1)
    gg = gg[0]
    return (
        block[None], gt[None], gg[:WR], g_q, g_k, g_v, g_out,
        gg[2 * WR : 2 * WR + 1], gg[2 * WR + 1 : 2 * WR + 2], gg[WR : 2 * WR],
        g_mlp[0], g_mlp[1], g_down,
    )


def solution(mesh):
    both = P(("dp", "seq"))
    rows = P(("dp", "seq"), None)
    act = P("dp", "seq", None)
    in_specs = (act, both, rows, rows, rows, rows, both, both, both, rows, rows, rows, act)
    out_specs = (act, act, both, rows, rows, rows, rows, both, both, both, rows, rows, rows)
    return jax.shard_map(
        shards, mesh=mesh, in_specs=in_specs, out_specs=out_specs, check_vma=False
    )
```

```python
import functools
import math

import jax
import jax.numpy as jnp
import numpy as np
from jax import lax
from jax.experimental import pallas as pl
from jax.experimental.pallas import tpu as pltpu
from jax.sharding import PartitionSpec as P

QUERY_HEADS = 16
KEY_VALUE_HEADS = 8
HEAD_DIM = 128

eps_norm = 1e-06
rope_base = 1000000.0
score_scale = 1.0 / math.sqrt(HEAD_DIM)

f32 = jnp.float32
bf16 = jnp.bfloat16

AXIS = 4
ND, NS = 16, 8
SPAN = 128
WIDTH = 2048
LENGTH = SPAN * NS
WR = 16
FR = 48
FFS = ND * FR
QKV = 512
GCOL = 128
VMEM_LIMIT = 60 * 2**20
MESH = pl.DeviceIdType.MESH


def dot(a, b):
    return jnp.dot(a, b, preferred_element_type=f32)


def dot_tn(a, b):
    return lax.dot_general(a, b, (((0,), (0,)), ((), ())), preferred_element_type=f32)


def dot_nt(a, b):
    return lax.dot_general(a, b, (((1,), (1,)), ((), ())), preferred_element_type=f32)


def rms(values):
    return lax.rsqrt(jnp.mean(values * values, axis=-1, keepdims=True) + eps_norm)


def rms_back(grad_out, gain, unit, inv):
    grad_unit = grad_out * gain
    return inv * (grad_unit - unit * jnp.mean(grad_unit * unit, axis=-1, keepdims=True))


def rope_constants():
    half = HEAD_DIM // 2
    freqs = np.float32(rope_base) ** (
        -(np.arange(half, dtype=np.float32) * np.float32(2.0) / np.float32(2 * half))
    )
    angles = np.arange(LENGTH, dtype=np.float32)[:, None] * freqs.astype(np.float32)[None, :]
    cos, sin = np.cos(angles), np.sin(angles)
    return np.concatenate([cos, sin], axis=1).astype(np.float32)


def coords():
    dp, sq = lax.axis_index("dp"), lax.axis_index("seq")
    return dp // AXIS, dp % AXIS, sq // 2, sq % 2


def device(y, z, x, c):
    return (y * AXIS + z, x * 2 + c)


def seq_peers(y, z, x, c):
    return [
        (k, j, device(y, z, (x + k) % AXIS, (c + j) % 2))
        for k in range(AXIS)
        for j in range(2)
        if (k, j) != (0, 0)
    ]


def greet(peers):
    sem = pltpu.get_barrier_semaphore()
    for peer in peers:
        pl.semaphore_signal(sem, inc=1, device_id=peer, device_id_type=MESH)


def all_in(peers):
    pl.semaphore_wait(pltpu.get_barrier_semaphore(), len(peers))


def around(y, z, x, c):
    yp = [device((y + k) % AXIS, z, x, c) for k in (1, 2, 3)]
    zp = [device(y, (z + k) % AXIS, x, c) for k in (1, 2, 3)]
    return seq_peers(y, z, x, c), yp, zp


class Copies:
    def __init__(self, send, recv, local):
        self.send, self.recv, self.local = send, recv, local
        self.n, self.n_local = 0, 0
        self.sent = []

    def to(self, src, dst, dev):
        copy = pltpu.make_async_remote_copy(
            src_ref=src, dst_ref=dst, send_sem=self.send.at[self.n], recv_sem=self.recv.at[self.n],
            device_id=dev, device_id_type=MESH,
        )
        self.n += 1
        copy.start()
        self.sent.append(copy)
        return copy

    def here(self, src, dst):
        copy = pltpu.make_async_copy(src, dst, self.local.at[self.n_local])
        self.n_local += 1
        copy.start()
        return copy

    def finish(self):
        for copy in self.sent:
            copy.wait_send()
        self.sent = []

    def drain(self, copies):
        for copy in copies:
            copy.wait_send()
        done = {id(copy) for copy in copies}
        self.sent = [copy for copy in self.sent if id(copy) not in done]


class SeqGather:
    def __init__(self, cm, own, buf, co):
        self.cm, self.own, self.buf, self.co = cm, own, buf, co
        self.half = buf.shape[1] // 2

    def slot(self, k):
        y, z, x, c = self.co
        return self.buf.at[((x + k) % AXIS) * 2 + c]

    def start(self):
        y, z, x, c = self.co
        self.sib = device(y, z, x, 1 - c)
        self.plus, self.minus = device(y, z, (x + 1) % AXIS, c), device(y, z, (x + 3) % AXIS, c)
        self.a = self.cm.to(self.own, self.slot(0), self.plus)
        self.b = self.cm.to(self.own, self.slot(0), self.minus)
        self.s0 = self.cm.to(self.own, self.slot(0), self.sib)
        self.l = self.cm.here(self.own, self.slot(0))

    def forward(self):
        h = self.half
        lo, hi = pl.ds(0, h), pl.ds(h, h)
        self.a.wait_recv()
        left = self.slot(3)
        self.fa = self.cm.to(left.at[lo], left.at[lo], self.plus)
        self.s1 = self.cm.to(left, left, self.sib)
        self.b.wait_recv()
        right = self.slot(1)
        self.fb = self.cm.to(right.at[hi], right.at[hi], self.minus)
        self.s2 = self.cm.to(right, right, self.sib)

    def last(self):
        h = self.half
        lo, hi = pl.ds(0, h), pl.ds(h, h)
        opp = self.slot(2)
        self.fa.wait_recv()
        self.s3 = self.cm.to(opp.at[lo], opp.at[lo], self.sib)
        self.fb.wait_recv()
        self.s4 = self.cm.to(opp.at[hi], opp.at[hi], self.sib)

    def drain(self):
        self.cm.drain(
            [self.a, self.b, self.s0, self.fa, self.s1, self.fb, self.s2, self.s3, self.s4]
        )

    def wait_chip(self, k):
        if k == 0:
            self.l.wait()
            self.s0.wait_recv()
        elif k == 3:
            self.s1.wait_recv()
        elif k == 1:
            self.s2.wait_recv()
        else:
            self.s3.wait_recv()
            self.s4.wait_recv()


class DpGather:
    def __init__(self, cm, own, buf, co, axis):
        self.cm, self.own, self.buf, self.co, self.axis = cm, own, buf, co, axis
        n = own.shape[axis]
        self.h, self.q = n // 2, n // 4

    def part(self, ref, half, quarter=None):
        lo = half * self.h + (0 if quarter is None else quarter * self.q)
        size = self.h if quarter is None else self.q
        cut = pl.ds(lo, size)
        lead = len(ref.shape) - 2
        index = (slice(None),) * lead + ((cut, slice(None)) if self.axis == 0 else (slice(None), cut))
        return ref.at[index]

    def both(self, src_p, dst_p, src_m, dst_m, along):
        y, z, x, c = self.co
        if along == 0:
            plus, minus = device((y + 1) % AXIS, z, x, c), device((y + 3) % AXIS, z, x, c)
        else:
            plus, minus = device(y, (z + 1) % AXIS, x, c), device(y, (z + 3) % AXIS, x, c)
        return (self.cm.to(src_p, dst_p, plus), self.cm.to(src_m, dst_m, minus))

    def start(self):
        y, z, _, _ = self.co
        mine = self.buf.at[y, z]
        self.l = self.cm.here(self.own, mine)
        self.one = []
        for half in (0, 1):
            src, dst = self.part(self.own, half), self.part(mine, half)
            self.one.append(self.both(src, dst, src, dst, half))

    def spread(self):
        y, z, _, _ = self.co
        self.two = []
        for half in (0, 1):
            if half == 0:
                left, right = self.buf.at[(y + 3) % AXIS, z], self.buf.at[(y + 1) % AXIS, z]
            else:
                left, right = self.buf.at[y, (z + 3) % AXIS], self.buf.at[y, (z + 1) % AXIS]
            for copy in self.one[half]:
                copy.wait_recv()
            lp, rp = self.part(left, half, 0), self.part(right, half, 1)
            self.two.append(self.both(lp, lp, rp, rp, half))

    def line(self, half, k):
        y, z, _, _ = self.co
        if half == 0:
            return self.buf.at[:, (z + k) % AXIS]
        return self.buf.at[(y + k) % AXIS]

    def turn(self):
        self.l.wait()
        self.three = []
        for half in (0, 1):
            for copy in self.two[half]:
                copy.wait_recv()
            mine = self.part(self.line(half, 0), half)
            self.three.append(self.both(mine, mine, mine, mine, 1 - half))

    def last(self):
        self.four = []
        for half in (0, 1):
            for copy in self.three[half]:
                copy.wait_recv()
            lp = self.part(self.line(half, 3), half, 0)
            rp = self.part(self.line(half, 1), half, 1)
            self.four.append(self.both(lp, lp, rp, rp, 1 - half))

    def wait(self):
        for half in (0, 1):
            for copy in self.four[half]:
                copy.wait_recv()


def off(n):
    return jnp.where(n == 0, 2, jnp.where(n == 1, 1, jnp.where(n == 2, 3, 0)))


class SeqScatter:
    def __init__(self, part, sib_recv, x_recv, sems, co, kept=None):
        self.part, self.sib_recv, self.x_recv, self.sems, self.co = part, sib_recv, x_recv, sems, co
        self.kept = kept

    def ours(self, n):
        return self.part.at[2 * n + 1] if self.kept is None else self.kept.at[n]

    def sib_copy(self, n):
        y, z, x, c = self.co
        return pltpu.make_async_remote_copy(
            src_ref=self.part.at[2 * n], dst_ref=self.sib_recv.at[n],
            send_sem=self.sems.at[0, n], recv_sem=self.sems.at[1, n],
            device_id=device(y, z, x, 1 - c), device_id_type=MESH,
        )

    def x_copy(self, n):
        y, z, x, c = self.co
        return pltpu.make_async_remote_copy(
            src_ref=self.ours(n), dst_ref=self.x_recv.at[n],
            send_sem=self.sems.at[2, n], recv_sem=self.sems.at[3, n],
            device_id=device(y, z, (x + off(n)) % AXIS, c), device_id_type=MESH,
        )

    def combine(self, n, go=True):
        self.sib_copy(n).wait_recv()
        ours = self.ours(n)

        def add(i, _):
            cut = pl.ds(i * 32, 32)
            total = ours[cut, :].astype(f32) + self.sib_recv[n, cut, :].astype(f32)
            ours[cut, :] = total.astype(bf16)
            return 0

        lax.fori_loop(0, SPAN // 32, add, 0)
        if go:

            @pl.when(n < 3)
            def _():
                self.x_copy(n).start()

    def arrive(self):
        for n in range(3):
            self.x_copy(n).wait_recv()

    def rows(self, cut):
        total = self.ours(3)[cut, :].astype(f32)
        for n in range(3):
            total = total + self.x_recv[n, cut, :].astype(f32)
        return total

    def finish(self):
        for n in range(4):
            self.sib_copy(n).wait_send()
        for n in range(3):
            self.x_copy(n).wait_send()


def scatter_scratch():
    return [
        pltpu.VMEM((8, SPAN, WIDTH), bf16),
        pltpu.VMEM((4, SPAN, WIDTH), bf16),
        pltpu.VMEM((3, SPAN, WIDTH), bf16),
        pltpu.SemaphoreType.DMA((4, 4)),
    ]


def swap(u):
    return pltpu.roll(u, HEAD_DIM // 2, 1)


def rope_rows(table):
    low = lax.broadcasted_iota(jnp.int32, table.shape, 1) < HEAD_DIM // 2
    other = swap(table)
    return jnp.where(low, table, other), jnp.where(low, -other, table)


def peer_index(x, c, k, j):
    return ((x + k) % AXIS) * 2 + (c + j) % 2


class DpScatter:
    def __init__(self, cm, grad, acc, one, two, co, tile):
        self.cm, self.grad, self.acc, self.r1, self.r2 = cm, grad, acc, one, two
        self.co, self.tile = co, tile
        self.h = acc.shape[2]

    def part(self, ref, half):
        return ref.at[:, pl.ds(half * self.h, self.h)]

    def line(self, half, k):
        y, z, _, _ = self.co
        if half == 0:
            return self.part(self.grad.at[(y + k) % AXIS], half)
        return self.part(self.grad.at[:, (z + k) % AXIS], half)

    def away(self, along, k):
        y, z, x, c = self.co
        if along == 0:
            return device((y + k) % AXIS, z, x, c)
        return device(y, (z + k) % AXIS, x, c)

    def start(self):
        self.own = [self.cm.here(self.line(h, 0), self.acc.at[h]) for h in (0, 1)]
        self.first = [[], []]
        for k in (2, 1, 3):
            for h in (0, 1):
                self.first[h].append(
                    self.cm.to(self.line(h, k), self.r1.at[h, k - 1], self.away(h, k))
                )

    def add_first(self):
        rows = self.acc.shape[2]
        for h in (0, 1):
            self.own[h].wait()
            for copy in self.first[h]:
                copy.wait_recv()

            def add(t, _, h=h):
                q = t // (rows // self.tile)
                cut = pl.ds((t % (rows // self.tile)) * self.tile, self.tile)
                total = self.acc[h, q, cut, :].astype(f32)
                for k in range(3):
                    total = total + self.r1[h, k, q, cut, :].astype(f32)
                self.acc[h, q, cut, :] = total.astype(bf16)
                return 0

            lax.fori_loop(0, AXIS * (rows // self.tile), add, 0)

    def send_second(self):
        y, z, _, _ = self.co
        self.second = [[], []]
        for h in (0, 1):
            mine = z if h == 0 else y
            for k in (2, 1, 3):
                self.second[h].append(
                    self.cm.to(self.acc.at[h, (mine + k) % AXIS], self.r2.at[h, k - 1], self.away(1 - h, k))
                )

    def mid(self):
        self.add_first()
        self.send_second()

    def last(self, out):
        y, z, _, _ = self.co
        rows, cols = self.acc.shape[2:]
        for h in (0, 1):
            for copy in self.second[h]:
                copy.wait_recv()
            mine = z if h == 0 else y

            def add(t, _, h=h, mine=mine):
                cut = pl.ds(t * self.tile, self.tile)
                total = self.acc[h, mine, cut, :].astype(f32)
                for k in range(3):
                    total = total + self.r2[h, k, cut, :].astype(f32)
                out[pl.ds(h * self.h + t * self.tile, self.tile), :] = total.astype(out.dtype)
                return 0

            lax.fori_loop(0, rows // self.tile, add, 0)


def dp_scatter_scratch(rows, cols):
    return [
        pltpu.VMEM((2, AXIS, rows, cols), bf16),
        pltpu.VMEM((2, 3, AXIS, rows, cols), bf16),
        pltpu.VMEM((2, 3, rows, cols), bf16),
    ]


def front_kernel(
    tok, cot, extra, w_query, w_key, w_value, w_out, w_gate, w_up, w_down, table,
    x1_o, dx1_o, dab_o, gain2_o, h1_o, pre_o, qb, kb, vb, ob, gains, gq_o, wo_o, ggu_o, pd_o, dacc_o,
    xg, pq, pm, wod, a2a_q, a2a_m, wq, wo_b, wo_v, wd_b, wd_v, wgu, o1, o2, o3o, o3d, h2_loc,
    dy_v, hid, dgu, pdv, d_one,
    part, sib_recv, x_recv, rs_sems, rs_sems2, send, recv, local,
):
    co = y, z, x, c = coords()
    s = x * 2 + c
    peers, yp, zp = around(*co)
    everyone = [p for _, _, p in peers] + yp + zp
    greet(everyone)
    cm = Copies(send, recv, local)
    for t in range(NS):
        pq[t, :, 0:256] = w_query[:, t * 256 : t * 256 + 256]
        pq[t, :, 256:384] = w_key[:, t * 128 : t * 128 + 128]
        pq[t, :, 384:512] = w_value[:, t * 128 : t * 128 + 128]
        pq[t, :, 512:640] = extra[...]
        pm[t, :, 0:FFS] = w_gate[:, t * FFS : t * FFS + FFS]
        pm[t, :, FFS : 2 * FFS] = w_up[:, t * FFS : t * FFS + FFS]
    wod[0:WR, :] = w_out[...]
    wod[WR : WR + FR, :] = w_down[...]
    all_in(everyone)

    aq = [cm.to(pq.at[peer_index(x, c, k, j)], a2a_q.at[s], p) for k, j, p in peers]
    lq = cm.here(pq.at[s], a2a_q.at[s])
    g_tok = SeqGather(cm, tok, xg, co)
    g_tok.start()

    def quarter(i):
        return pl.ds(pl.multiple_of(i * 512, 512), 512)

    def chunk(i):
        return pl.ds(pl.multiple_of(i * 128, 128), 128)

    o_one = [cm.to(wod.at[:, quarter((y + k) % AXIS)], o1.at[y], yp[k - 1]) for k in (1, 2, 3)]
    l_one = cm.here(wod.at[:, quarter(y)], o1.at[y])
    am = [cm.to(pm.at[peer_index(x, c, k, j)], a2a_m.at[s], p) for k, j, p in peers]
    lm = cm.here(pm.at[s], a2a_m.at[s])
    lq.wait()
    for copy in aq:
        copy.wait_recv()
    g_q = DpGather(cm, a2a_q.reshape(NS * WR, QKV + GCOL), wq, co, 0)
    g_q.start()
    l_one.wait()
    for copy in o_one:
        copy.wait_recv()
    o_two = [cm.to(o1.at[:, :, chunk((z + k) % AXIS)], o2.at[z], zp[k - 1]) for k in (1, 2, 3)]
    l_two = cm.here(o1.at[:, :, chunk(z)], o2.at[z])
    g_q.spread()
    l_two.wait()
    for copy in o_two:
        copy.wait_recv()

    def rows_of(t, lo, n):
        return o2.at[pl.ds((t % 2) * 2, 2), t // 2, pl.ds(lo, n)]

    o_three = []
    for k, j, p in peers:
        t = peer_index(x, c, k, j)
        o_three.append(cm.to(rows_of(t, 0, WR), o3o.at[:, s], p))
        o_three.append(cm.to(rows_of(t, WR, FR), o3d.at[:, s], p))
    l_three = [
        cm.here(rows_of(s, 0, WR), o3o.at[:, s]),
        cm.here(rows_of(s, WR, FR), o3d.at[:, s]),
    ]
    g_q.turn()
    g_tok.forward()
    lm.wait()
    for copy in am:
        copy.wait_recv()
    g_m = DpGather(cm, a2a_m.reshape(NS * WR, 2 * FFS), wgu, co, 0)
    g_m.start()
    for copy in l_three:
        copy.wait()
    for copy in o_three:
        copy.wait_recv()
    g_o = DpGather(cm, o3o.reshape(2 * SPAN, SPAN), wo_b, co, 0)
    g_o.start()
    g_d = DpGather(cm, o3d.reshape(FFS, SPAN), wd_b, co, 0)
    g_d.start()
    g_q.last()
    g_o.spread()
    g_tok.last()
    g_cot = SeqGather(cm, cot, dy_v, co)
    g_cot.start()
    g_o.turn()
    g_m.spread()
    g_d.spread()
    g_q.wait()
    wq_out = cm.here(wq.at[:, :, :, pl.ds(0, QKV)], gq_o)
    g_o.last()
    g_m.turn()
    g_d.turn()

    wq2 = wq.reshape(WIDTH, QKV + GCOL)
    gcols = wq2[:, QKV:]
    flat = gcols.astype(f32).T
    gains[...] = flat[:8]
    gain_one = flat[0:1]
    rows = lax.broadcasted_iota(jnp.int32, (WIDTH, HEAD_DIM), 0)
    cols = lax.broadcasted_iota(jnp.int32, (WIDTH, HEAD_DIM), 1)
    pick = (rows == cols * WR).astype(bf16)
    head_gains = dot(flat[:8].astype(bf16), pick)
    gain_q, gain_k = head_gains[2:3], head_gains[3:4]
    gains[2:4, 0:HEAD_DIM] = head_gains[2:4]

    def normed(i, _):
        cut = pl.ds((i % 4) * 32, 32)
        v = xg[i // 4, cut, :].astype(f32)
        part[i // 4, cut, :] = (v * rms(v) * gain_one).astype(bf16)
        return 0

    for k in (0, 1, 3, 2):
        g_tok.wait_chip(k)
    lax.fori_loop(0, LENGTH // 32, normed, 0)
    h1_copy = cm.here(part, h1_o)
    g_cot.forward()

    def project(i, _):
        h = part[pl.ds(2 * i, 2)].reshape(2 * SPAN, WIDTH)
        p = dot(h, wq2[:, :QKV])
        cut = pl.ds(pl.multiple_of(i * 256, 256), 256)
        pre_o[cut, :] = p[:, :384]
        vb[cut, :] = p[:, 384:].astype(bf16)
        co_t, si_t = rope_rows(table[cut, :])
        for h_i in range(2):
            u = p[:, h_i * 128 : h_i * 128 + 128]
            u = u * rms(u) * gain_q
            u = (u * co_t + swap(u) * si_t).astype(bf16)
            qb[pl.ds(2 * i, 2), pl.ds(h_i * SPAN, SPAN), :] = u.reshape(2, SPAN, HEAD_DIM)
        u = p[:, 256:384]
        u = u * rms(u) * gain_k
        kb[cut, :] = (u * co_t + swap(u) * si_t).astype(bf16)
        return 0

    lax.fori_loop(0, 4, project, 0)
    h1_copy.wait()
    g_tok.drain()
    g_o.wait()
    wo_copy = [
        cm.here(wo_b.at[yy, zz], wo_v.at[:, pl.ds((yy * AXIS + zz) * 128, 128)])
        for yy in range(AXIS)
        for zz in range(AXIS)
    ]
    for copy in wo_copy:
        copy.wait()
    wo_out = cm.here(wo_v, wo_o)

    rs = SeqScatter(part, sib_recv, x_recv, rs_sems, co)

    def attend(i, slot):
        sc = dot_nt(qb[i], kb[...]) * score_scale
        r = lax.broadcasted_iota(jnp.int32, (2 * SPAN, LENGTH), 0) % SPAN + i * SPAN
        k = lax.broadcasted_iota(jnp.int32, (2 * SPAN, LENGTH), 1)
        sc = jnp.where(k <= r, sc, -1e30)
        top = jnp.max(sc, axis=-1, keepdims=True)
        ex = jnp.exp(sc - top)
        tot = jnp.sum(ex, axis=-1, keepdims=True)
        pb = (ex / tot).astype(bf16)
        o = dot(pb, vb[...]).astype(bf16)
        o = jnp.concatenate([o[:SPAN], o[SPAN:]], axis=1)
        ob[pl.ds(pl.multiple_of(i * SPAN, SPAN), SPAN), :] = o
        part[slot] = dot(o, wo_v[...]).astype(bf16)

    def pair(n, _):
        chip = (x + off(n)) % AXIS
        attend(chip * 2 + 1 - c, 2 * n)
        rs.sib_copy(n).start()
        attend(chip * 2 + c, 2 * n + 1)
        rs.combine(n)
        return 0

    lax.fori_loop(0, 4, pair, 0)
    g_cot.last()
    g_m.last()
    g_d.last()
    rs.arrive()

    def residual(i, _):
        cut = pl.ds(i * 32, 32)
        v = xg[s, cut, :].astype(f32) + rs.rows(cut)
        x1_o[cut, :] = v
        h2_loc[cut, :] = (v * rms(v) * gains[1:2, :]).astype(bf16)
        return 0

    lax.fori_loop(0, SPAN // 32, residual, 0)
    rs.finish()

    g_h2 = SeqGather(cm, h2_loc, xg, co)
    g_h2.start()
    for k in (0, 1, 3, 2):
        g_cot.wait_chip(k)
    g_d.wait()
    wd_copy = [
        cm.here(wd_b.at[yy, zz], wd_v.at[:, pl.ds((yy * AXIS + zz) * 128, 128)])
        for yy in range(AXIS)
        for zz in range(AXIS)
    ]
    g_m.wait()
    for copy in wd_copy:
        copy.wait()
    rs = SeqScatter(part, sib_recv, x_recv, rs_sems2, co)
    wgu2 = wgu.reshape(WIDTH, 2 * FFS)
    order = {2: 0, 1: 1, 3: 2, 0: 3}

    def chip_of(k):
        return (x + k) % AXIS

    def forward(k):
        chip = chip_of(k)
        rows = pl.ds(pl.multiple_of(chip * 256, 256), 256)
        two = pl.ds(2 * chip, 2)

        def tile(f, _):
            lo = pl.multiple_of(f * 256, 256)
            h = xg[two].reshape(256, WIDTH)
            gate = dot(h, wgu2[:, pl.ds(lo, 256)])
            up = dot(h, wgu2[:, pl.ds(pl.multiple_of(lo + FFS, 256), 256)])
            dh = dot_nt(dy_v[two].reshape(256, WIDTH), wd_v[pl.ds(lo, 256), :])
            sig = jax.nn.sigmoid(gate)
            silu = gate * sig
            hid[rows, pl.ds(lo, 256)] = (silu * up).astype(bf16)
            dgate = dh * up * (sig * (1.0 + gate * (1.0 - sig)))
            dgu[rows, pl.ds(lo, 256)] = dgate.astype(bf16)
            dgu[rows, pl.ds(pl.multiple_of(lo + FFS, 256), 256)] = (dh * silu).astype(bf16)
            return 0

        lax.fori_loop(0, FFS // 256, tile, 0)

    def put(ref, n, cols, o):
        ref[2 * n + 1 - c, :, cols] = o[:SPAN]
        ref[2 * n + c, :, cols] = o[SPAN:]

    def back(k):
        n = order[k]
        rows = pl.ds(pl.multiple_of(chip_of(k) * 256, 256), 256)

        def tile(m, _):
            cols = pl.ds(pl.multiple_of(m * 256, 256), 256)
            put(part, n, cols, dot_nt(dgu[rows, :], wgu2[cols, :]).astype(bf16))
            return 0

        lax.fori_loop(0, WIDTH // 256, tile, 0)
        rs.sib_copy(n).start()

    g_h2.wait_chip(0)
    forward(0)
    g_h2.forward()
    back(0)
    g_h2.wait_chip(3)
    forward(3)
    g_h2.last()
    back(3)
    g_h2.wait_chip(1)
    forward(1)
    rs.combine(order[3])
    back(1)
    g_h2.wait_chip(2)
    forward(2)
    rs.combine(order[1])
    back(2)
    rs.combine(order[0])
    cm.finish()

    def down_grad(m, _):
        cut = pl.ds(pl.multiple_of(m * 256, 256), 256)
        o = dot_tn(hid[:, cut], dy_v[...].reshape(LENGTH, WIDTH)).astype(bf16)
        for yy in range(AXIS):
            for zz in range(AXIS):
                lo = (yy * AXIS + zz) * 128
                wd_b[yy, zz, cut, :] = o[:, lo : lo + 128]
        return 0

    lax.fori_loop(0, 1, down_grad, 0)
    rs.combine(order[2])
    lax.fori_loop(1, FFS // 256, down_grad, 0)
    r_d = DpScatter(cm, wd_b, dacc_o, d_one, None, co, 128)
    r_d.start()

    for k in range(4):
        n = order[k]
        rows = pl.ds(pl.multiple_of(chip_of(k) * 256, 256), 256)

        def down(m, _):
            cols = pl.ds(pl.multiple_of(m * 512, 512), 512)
            put(pdv, n, cols, dot(hid[rows, :], wd_v[:, cols]).astype(bf16))
            return 0

        lax.fori_loop(0, WIDTH // 512, down, 0)
    outs = [cm.here(pdv, pd_o)]

    def gate_up(m, _):
        cols = pl.ds(pl.multiple_of(m * 256, 256), 256)
        wgu2[cols, :] = dot_tn(xg[:, :, cols].reshape(LENGTH, 256), dgu[...]).astype(bf16)
        return 0

    lax.fori_loop(0, WIDTH // 256, gate_up, 0)
    outs.append(cm.here(wgu, ggu_o))
    rs.arrive()
    gain_two = gains[1:2, :]

    def mlp_back(i, acc):
        cut = pl.ds(i * 32, 32)
        v = x1_o[cut, :]
        inv = rms(v)
        unit = v * inv
        dh2 = rs.rows(cut)
        dx1 = dy_v[s, cut, :].astype(f32) + rms_back(dh2, gain_two, unit, inv)
        dx1_o[cut, :] = dx1
        dab_o[cut, :] = dx1.astype(bf16)
        return acc + jnp.sum(dh2 * unit, axis=0, keepdims=True)

    acc = lax.fori_loop(0, SPAN // 32, mlp_back, jnp.zeros((1, WIDTH), f32))
    gain2_o[...] = jnp.broadcast_to(acc, (8, WIDTH))
    r_d.add_first()
    rs.finish()
    wo_out.wait()
    wq_out.wait()
    for copy in outs:
        copy.wait()
    cm.finish()


def front(*args):
    any_, vm = pl.BlockSpec(memory_space=pl.ANY), pl.BlockSpec(memory_space=pltpu.VMEM)
    sds = jax.ShapeDtypeStruct
    vmem = pltpu.VMEM
    n_copies, n_local = 160, 64
    return pl.pallas_call(
        front_kernel,
        name="attn_forward",
        out_shape=[
            sds((SPAN, WIDTH), f32), sds((SPAN, WIDTH), f32), sds((SPAN, WIDTH), bf16),
            sds((8, WIDTH), f32), sds((8, SPAN, WIDTH), bf16), sds((LENGTH, 384), f32),
            sds((8, 2 * SPAN, 128), bf16), sds((LENGTH, 128), bf16), sds((LENGTH, 128), bf16),
            sds((LENGTH, 256), bf16), sds((8, WIDTH), f32), sds((4, 4, 128, QKV), bf16),
            sds((256, WIDTH), bf16), sds((4, 4, 128, 2 * FFS), bf16), sds((8, SPAN, WIDTH), bf16),
            sds((2, 4, FFS // 2, 128), bf16),
        ],
        in_specs=[any_] * 2 + [vm] * 9,
        out_specs=[vm, vm, vm, vm, any_, vm, vm, vm, vm, vm, vm, any_, any_, any_, any_, vm],
        scratch_shapes=[
            vmem((8, SPAN, WIDTH), bf16),
            vmem((NS, WR, QKV + GCOL), bf16), vmem((NS, WR, 2 * FFS), bf16),
            vmem((WR + FR, WIDTH), bf16),
            vmem((NS, WR, QKV + GCOL), bf16), vmem((NS, WR, 2 * FFS), bf16),
            vmem((4, 4, 128, QKV + GCOL), bf16),
            vmem((4, 4, 256, 128), bf16), vmem((256, WIDTH), bf16),
            vmem((4, 4, FFS, 128), bf16), vmem((FFS, WIDTH), bf16),
            vmem((4, 4, 128, 2 * FFS), bf16),
            vmem((4, WR + FR, 512), bf16), vmem((4, 4, WR + FR, 128), bf16),
            vmem((2, NS, WR, 128), bf16), vmem((2, NS, FR, 128), bf16),
            vmem((SPAN, WIDTH), bf16),
            vmem((8, SPAN, WIDTH), bf16), vmem((LENGTH, FFS), bf16), vmem((LENGTH, 2 * FFS), bf16),
            vmem((8, SPAN, WIDTH), bf16), vmem((2, 3, AXIS, FFS // 2, 128), bf16),
            *scatter_scratch(),
            pltpu.SemaphoreType.DMA((4, 4)),
            pltpu.SemaphoreType.DMA((n_copies,)),
            pltpu.SemaphoreType.DMA((n_copies,)),
            pltpu.SemaphoreType.DMA((n_local,)),
        ],
        compiler_params=pltpu.CompilerParams(
            collective_id=1, has_side_effects=True, vmem_limit_bytes=VMEM_LIMIT
        ),
    )(*args)


class RowsHome:
    def __init__(self, cm, res, r2, r1, out, co):
        self.cm, self.res, self.r2, self.r1, self.out, self.co = cm, res, r2, r1, out, co
        self.peers, self.yp, self.zp = around(*co)

    def step(self, sends, here):
        self.wait()
        self.arriving = [self.cm.to(*a) for a in sends]
        self.local = self.cm.here(*here)

    def wait(self):
        if hasattr(self, "arriving"):
            self.local.wait()
            for copy in self.arriving:
                copy.wait_recv()

    def over_seq(self):
        y, z, x, c = self.co
        s = x * 2 + c
        dst = self.r2.at[pl.ds((s % 2) * 2, 2), s // 2]
        self.step(
            [(self.res.at[:, peer_index(x, c, k, j)], dst, p) for k, j, p in self.peers],
            (self.res.at[:, s], dst),
        )

    def over_z(self):
        y, z, x, c = self.co
        dst = self.r1.at[:, :, pl.ds(pl.multiple_of(z * 128, 128), 128)]
        self.step(
            [(self.r2.at[(z + k) % AXIS], dst, self.zp[k - 1]) for k in (1, 2, 3)],
            (self.r2.at[z], dst),
        )

    def over_y(self):
        y, z, x, c = self.co
        dst = self.out.at[:, pl.ds(pl.multiple_of(y * 512, 512), 512)]
        self.step(
            [(self.r1.at[(y + k) % AXIS], dst, self.yp[k - 1]) for k in (1, 2, 3)],
            (self.r1.at[y], dst),
        )


def back_kernel(
    dab_loc, pd, ggu, h1, gq, wo,
    dacc, dx1, tok, x1, gain2, pre, qb, kb, vb, ob, gains, table,
    gt_o, block_o, gwq_o, gwk_o, gwv_o, gwo_o, gwg_o, gwu_o, gwd_o, gg_o,
    dab, h1_v, wq, wo_v, pbuf, dob, dk, dv, dqkv, gacc,
    part, sib_recv, x_recv, rs_sems, kept, sib2, x2, rs2_sems,
    m_acc, m_one, m_two, o_acc, o_one, o_two, q_acc, q_one, q_two, d_two,
    mo, mr, qo, qr, go, gqk, oo, o2g, o1g, ow, od, d2g, d1g, dw,
    gg, g_one, g_two, g_all, g_sum,
    send, recv, local,
):
    co = y, z, x, c = coords()
    s = x * 2 + c
    peers, yp, zp = around(*co)
    everyone = [p for _, _, p in peers] + yp + zp
    greet(everyone)
    cm = Copies(send, recv, local)
    l_pd = [cm.here(pd.at[2 * n + 1], kept.at[n]) for n in range(4)]
    l_wo = cm.here(wo, wo_v)
    l_wq = cm.here(gq, wq)

    def h1_load(m):
        return cm.here(h1.at[:, :, pl.ds(m * 256, 256)], h1_v.at[m % 2])

    l_h1 = [h1_load(0), h1_load(1)]
    all_in(everyone)
    g_dab = SeqGather(cm, dab_loc, dab, co)
    g_dab.start()
    r_d = DpScatter(cm, None, dacc, None, d_two, co, 128)
    r_d.send_second()
    r_m = DpScatter(cm, ggu, m_acc, m_one, m_two, co, 16)
    r_m.start()
    rs2 = SeqScatter(pd, sib2, x2, rs2_sems, co, kept)
    for n in range(4):
        l_pd[n].wait()
        rs2.sib_copy(n).start()

    def probs(i, _):
        sc = dot_nt(qb[i], kb[...]) * score_scale
        r = lax.broadcasted_iota(jnp.int32, (2 * SPAN, LENGTH), 0) % SPAN + i * SPAN
        k = lax.broadcasted_iota(jnp.int32, (2 * SPAN, LENGTH), 1)
        sc = jnp.where(k <= r, sc, -1e30)
        ex = jnp.exp(sc - jnp.max(sc, axis=-1, keepdims=True))
        pbuf[i] = (ex / jnp.sum(ex, axis=-1, keepdims=True)).astype(bf16)
        return 0

    lax.fori_loop(0, 4, probs, 0)
    g_dab.forward()
    lax.fori_loop(4, 8, probs, 0)
    dk[...] = jnp.zeros_like(dk)
    dv[...] = jnp.zeros_like(dv)
    gacc[...] = jnp.zeros_like(gacc)
    l_wo.wait()

    def out_back(k):
        g_dab.wait_chip(k)
        two = pl.ds(2 * ((x + k) % AXIS), 2)
        o = dot_nt(dab[two].reshape(2 * SPAN, WIDTH), wo_v[...]).astype(bf16)
        for j in range(2):
            blk = o[j * SPAN : (j + 1) * SPAN]
            dob[2 * ((x + k) % AXIS) + j] = jnp.concatenate([blk[:, :128], blk[:, 128:]], axis=0)

    out_back(0)
    out_back(3)
    out_back(1)
    for n in range(4):
        rs2.combine(n, False)
    g_dab.last()
    rs2.x_copy(0).start()
    out_back(2)

    def out_grad(m, _):
        cols = pl.ds(pl.multiple_of(m * 512, 512), 512)
        o = dot_tn(ob[...], dab[:, :, cols].reshape(LENGTH, 512)).astype(bf16)
        for j in range(AXIS):
            go[m, j] = o[:, j * 128 : j * 128 + 128]
        return 0

    lax.fori_loop(0, AXIS, out_grad, 0)
    r_o = DpScatter(cm, go, o_acc, o_one, o_two, co, 128)
    r_o.start()

    rs = SeqScatter(part, sib_recv, x_recv, rs_sems, co)
    l_wq.wait()
    wq2 = wq.reshape(WIDTH, QKV)
    gain_q, gain_k = gains[2:3, 0:128], gains[3:4, 0:128]

    def head_back(g, u, gain, co_t, si_t):
        g = g * co_t - swap(g) * si_t
        inv = rms(u)
        unit = u * inv
        return rms_back(g, gain, unit, inv), jnp.sum(g * unit, axis=0, keepdims=True)

    def slot_of(chip):
        k = (chip - x + AXIS) % AXIS
        return jnp.where(k == 2, 0, jnp.where(k == 1, 1, jnp.where(k == 3, 2, 3)))

    def chip_back(t, _):
        chip = 3 - t

        def block(j, _):
            i = chip * 2 + 1 - j
            q, do, p = qb[i], dob[i], pbuf[i]
            dp = dot_nt(do, vb[...])
            pf = p.astype(f32)
            delta = jnp.sum(pf * dp, axis=-1, keepdims=True)
            ds = (pf * (dp - delta)).astype(bf16)
            dk[...] += dot_tn(ds, q)
            dv[...] += dot_tn(p, do)
            dq = dot(ds, kb[...]) * score_scale
            cut = pl.ds(pl.multiple_of(i * SPAN, SPAN), SPAN)
            u = jnp.concatenate([pre[cut, 0:128], pre[cut, 128:256]], axis=0)
            co_t, si_t = rope_rows(table[cut, :])
            co_t = jnp.concatenate([co_t] * 2, axis=0)
            si_t = jnp.concatenate([si_t] * 2, axis=0)
            dqp, gsum = head_back(dq, u, gain_q, co_t, si_t)
            gacc[0:1, :] += gsum
            dqp = dqp.astype(bf16)
            dqkv[cut, 0:128] = dqp[:SPAN]
            dqkv[cut, 128:256] = dqp[SPAN:]
            return 0

        lax.fori_loop(0, 2, block, 0)
        cut = pl.ds(pl.multiple_of(chip * 256, 256), 256)
        co_t, si_t = rope_rows(table[cut, :])
        dkp, gsum = head_back(dk[cut, :] * score_scale, pre[cut, 256:384], gain_k, co_t, si_t)
        gacc[1:2, :] += gsum
        dqkv[cut, 256:384] = dkp.astype(bf16)
        dqkv[cut, 384:512] = dv[cut, :].astype(bf16)
        n = slot_of(chip)

        def tile(m, _):
            cols = pl.ds(pl.multiple_of(m * 512, 512), 512)
            o = dot_nt(dqkv[cut, :], wq2[cols, :]).astype(bf16)
            part[2 * n + 1 - c, :, cols] = o[:SPAN]
            part[2 * n + c, :, cols] = o[SPAN:]
            return 0

        lax.fori_loop(0, WIDTH // 512, tile, 0)
        rs.sib_copy(n).start()
        rs.combine(n)
        return 0

    lax.fori_loop(0, 2, chip_back, 0)
    r_m.mid()
    lax.fori_loop(2, 4, chip_back, 0)
    for n in (1, 2):
        rs2.x_copy(n).start()

    for m in range(8):
        l_h1[m].wait()
        o = dot_tn(h1_v[m % 2].reshape(LENGTH, 256), dqkv[...]).astype(bf16)
        gqk[m // 2, 2 * (m % 2)] = o[:SPAN]
        gqk[m // 2, 2 * (m % 2) + 1] = o[SPAN:]
        if m < 6:
            l_h1.append(h1_load(m + 2))
    r_q = DpScatter(cm, gqk, q_acc, q_one, q_two, co, 64)
    r_q.start()
    r_o.mid()
    r_d.last(od.reshape(FFS, SPAN))
    h_d = RowsHome(cm, od, d2g, d1g, dw, co)
    h_d.over_seq()
    r_m.last(mo.reshape(NS * WR, 2 * FFS))
    a_m = [cm.to(mo.at[peer_index(x, c, k, j)], mr.at[s], p) for k, j, p in peers]
    l_mo = cm.here(mo.at[s], mr.at[s])

    rs.arrive()
    gain_one = gains[0:1, :]

    def input_back(i, acc):
        cut = pl.ds(i * 32, 32)
        v = tok[cut, :].astype(f32)
        inv = rms(v)
        unit = v * inv
        dh1 = rs.rows(cut)
        gt_o[cut, :] = dx1[cut, :] + rms_back(dh1, gain_one, unit, inv)
        return acc + jnp.sum(dh1 * unit, axis=0, keepdims=True)

    gain1 = lax.fori_loop(0, SPAN // 32, input_back, jnp.zeros((1, WIDTH), f32))

    dev_i = lax.broadcasted_iota(jnp.int32, (ND * NS, WIDTH), 0)
    col_j = lax.broadcasted_iota(jnp.int32, (ND * NS, WIDTH), 1)
    mine = col_j // WR == dev_i
    row_j = lax.broadcasted_iota(jnp.int32, (WIDTH, 128), 0)
    lane = lax.broadcasted_iota(jnp.int32, (WIDTH, 128), 1)
    rows = jnp.zeros((ND * NS, 128), f32)
    for v, shift in ((gain1, 0), (gain2[0:1, :], WR)):
        rows = rows + dot(
            jnp.where(mine, v, 0.0).astype(bf16), (lane == row_j % WR + shift).astype(bf16)
        )
    eye_i = lax.broadcasted_iota(jnp.int32, (128, 128), 0)
    eye_j = lax.broadcasted_iota(jnp.int32, (128, 128), 1)
    for n in range(2):
        rows = rows + dot(
            jnp.where(eye_i == eye_j, gacc[n : n + 1, :], 0.0).astype(bf16),
            (eye_j == 2 * WR + n).astype(bf16),
        )
    gg[...] = rows.reshape(AXIS, AXIS, NS, 128)
    g_first = [cm.to(gg.at[(y + k) % AXIS], g_one.at[k - 1], yp[k - 1]) for k in (1, 2, 3)]
    h_d.over_z()
    r_q.mid()
    r_o.last(oo.reshape(2 * SPAN, SPAN))
    h_o = RowsHome(cm, oo, o2g, o1g, ow, co)
    h_o.over_seq()
    for copy in g_first:
        copy.wait_recv()
    gg[y] = gg[y] + g_one[0] + g_one[1] + g_one[2]
    g_second = [cm.to(gg.at[y, (z + k) % AXIS], g_two.at[k - 1], zp[k - 1]) for k in (1, 2, 3)]
    l_mo.wait()
    for copy in a_m:
        copy.wait_recv()
    for t in range(NS):
        gwg_o[:, t * FFS : t * FFS + FFS] = mr[t, :, 0:FFS].astype(f32)
        gwu_o[:, t * FFS : t * FFS + FFS] = mr[t, :, FFS : 2 * FFS].astype(f32)
    h_d.over_y()
    h_o.over_z()
    for copy in g_second:
        copy.wait_recv()
    g_all[s] = gg[y, z] + g_two[0] + g_two[1] + g_two[2]
    g_third = [cm.to(g_all.at[s], g_all.at[s], p) for _, _, p in peers]
    r_q.last(qo.reshape(NS * WR, QKV))
    a_q = [cm.to(qo.at[peer_index(x, c, k, j)], qr.at[s], p) for k, j, p in peers]
    l_qo = cm.here(qo.at[s], qr.at[s])
    h_d.wait()
    gwd_o[...] = dw[...].astype(f32)
    h_o.over_y()
    rs2.arrive()

    def out_rows(i, _):
        cut = pl.ds(i * 32, 32)
        block_o[cut, :] = (x1[cut, :] + rs2.rows(cut)).astype(bf16)
        return 0

    lax.fori_loop(0, SPAN // 32, out_rows, 0)
    for copy in g_third:
        copy.wait_recv()
    total = g_all[0]
    for t in range(1, NS):
        total = total + g_all[t]
    g_sum[...] = total
    gg_o[...] = jnp.broadcast_to(g_sum[pl.ds(s, 1), :], (8, 128))
    h_o.wait()
    gwo_o[...] = ow[...].astype(f32)
    l_qo.wait()
    for copy in a_q:
        copy.wait_recv()
    for t in range(NS):
        gwq_o[:, t * 256 : t * 256 + 256] = qr[t, :, 0:256].astype(f32)
        gwk_o[:, t * 128 : t * 128 + 128] = qr[t, :, 256:384].astype(f32)
        gwv_o[:, t * 128 : t * 128 + 128] = qr[t, :, 384:512].astype(f32)
    rs.finish()
    rs2.finish()
    cm.finish()


def back(*args):
    any_, vm = pl.BlockSpec(memory_space=pl.ANY), pl.BlockSpec(memory_space=pltpu.VMEM)
    sds = jax.ShapeDtypeStruct
    vmem = pltpu.VMEM
    n_copies, n_local = 128, 32
    return pl.pallas_call(
        back_kernel,
        name="attn_backward",
        out_shape=[
            sds((SPAN, WIDTH), f32), sds((SPAN, WIDTH), bf16),
            sds((WR, 2048), f32), sds((WR, 1024), f32), sds((WR, 1024), f32), sds((WR, WIDTH), f32),
            sds((WR, NS * FFS), f32), sds((WR, NS * FFS), f32), sds((FR, WIDTH), f32),
            sds((8, 128), f32),
        ],
        in_specs=[any_] * 6 + [vm] * (len(args) - 6),
        out_specs=[vm] * 10,
        scratch_shapes=[
            vmem((8, SPAN, WIDTH), bf16), vmem((2, 8, SPAN, 256), bf16),
            vmem((4, 4, 128, QKV), bf16), vmem((256, WIDTH), bf16),
            vmem((8, 2 * SPAN, LENGTH), bf16), vmem((8, 2 * SPAN, 128), bf16),
            vmem((LENGTH, 128), f32), vmem((LENGTH, 128), f32), vmem((LENGTH, QKV), bf16),
            vmem((8, 128), f32),
            *scatter_scratch(), vmem((4, SPAN, WIDTH), bf16), *scatter_scratch()[1:],
            *dp_scatter_scratch(64, 2 * FFS), *dp_scatter_scratch(SPAN, 128),
            *dp_scatter_scratch(64, QKV), vmem((2, 3, FFS // 2, 128), bf16),
            vmem((NS, WR, 2 * FFS), bf16), vmem((NS, WR, 2 * FFS), bf16),
            vmem((NS, WR, QKV), bf16), vmem((NS, WR, QKV), bf16),
            vmem((4, 4, 256, 128), bf16), vmem((4, 4, SPAN, QKV), bf16),
            vmem((2, NS, WR, 128), bf16), vmem((4, 4, WR, 128), bf16), vmem((4, WR, 512), bf16),
            vmem((WR, WIDTH), bf16),
            vmem((2, NS, FR, 128), bf16), vmem((4, 4, FR, 128), bf16), vmem((4, FR, 512), bf16),
            vmem((FR, WIDTH), bf16),
            vmem((4, 4, NS, 128), f32), vmem((3, 4, NS, 128), f32), vmem((3, NS, 128), f32),
            vmem((NS, NS, 128), f32), vmem((NS, 128), f32),
            pltpu.SemaphoreType.DMA((n_copies,)),
            pltpu.SemaphoreType.DMA((n_copies,)),
            pltpu.SemaphoreType.DMA((n_local,)),
        ],
        compiler_params=pltpu.CompilerParams(
            collective_id=2, has_side_effects=True, vmem_limit_bytes=VMEM_LIMIT
        ),
    )(*args)


def shards(
    tokens, gain_attn, w_query, key_weight, value_weight, w_out, gain_query,
    key_norm_gain, gain_mlp, w_gate, w_up, w_down, cotangent,
):
    extra = jnp.stack(
        [
            gain_attn,
            gain_mlp,
            jnp.broadcast_to(gain_query, (WR,)),
            jnp.broadcast_to(key_norm_gain, (WR,)),
        ],
        axis=1,
    )
    extra = jnp.pad(extra, ((0, 0), (0, GCOL - 4)))
    table = rope_constants()
    (x1, dx1, dab, gain2, h1, pre, qb, kb, vb, ob, gains, gq, wo, ggu, pd, dacc) = front(
        tokens[0], cotangent[0], extra, w_query, key_weight, value_weight, w_out, w_gate, w_up,
        w_down, table,
    )
    gt, block, g_q, g_k, g_v, g_out, g_gate, g_up, g_down, gg = back(
        dab, pd, ggu, h1, gq, wo,
        dacc, dx1, tokens[0], x1, gain2, pre, qb, kb, vb, ob, gains, table,
    )
    gg = gg[0]
    return (
        block[None], gt[None], gg[:WR], g_q, g_k, g_v, g_out,
        gg[2 * WR : 2 * WR + 1], gg[2 * WR + 1 : 2 * WR + 2], gg[WR : 2 * WR],
        g_gate, g_up, g_down,
    )


def solution(mesh):
    both = P(("dp", "seq"))
    rows = P(("dp", "seq"), None)
    act = P("dp", "seq", None)
    in_specs = (act, both, rows, rows, rows, rows, both, both, both, rows, rows, rows, act)
    out_specs = (act, act, both, rows, rows, rows, rows, both, both, both, rows, rows, rows)
    return jax.shard_map(
        shards, mesh=mesh, in_specs=in_specs, out_specs=out_specs, check_vma=False
    )
```

```python
import functools
import math

import jax
import jax.numpy as jnp
import numpy as np
from jax import lax
from jax.experimental import pallas as pl
from jax.experimental.pallas import tpu as pltpu
from jax.sharding import PartitionSpec as P

QUERY_HEADS = 16
KEY_VALUE_HEADS = 8
HEAD_DIM = 128

eps_norm = 1e-06
rope_base = 1000000.0
score_scale = 1.0 / math.sqrt(HEAD_DIM)

f32 = jnp.float32
bf16 = jnp.bfloat16

AXIS = 4
ND, NS = 16, 8
SPAN = 128
WIDTH = 2048
LENGTH = SPAN * NS
WR = 16
FR = 48
FFS = ND * FR
QKV = 512
GCOL = 128
VMEM_LIMIT = 60 * 2**20
MESH = pl.DeviceIdType.MESH


def dot(a, b):
    return jnp.dot(a, b, preferred_element_type=f32)


def dot_tn(a, b):
    return lax.dot_general(a, b, (((0,), (0,)), ((), ())), preferred_element_type=f32)


def dot_nt(a, b):
    return lax.dot_general(a, b, (((1,), (1,)), ((), ())), preferred_element_type=f32)


def rms(values):
    return lax.rsqrt(jnp.mean(values * values, axis=-1, keepdims=True) + eps_norm)


def rms_back(grad_out, gain, unit, inv):
    grad_unit = grad_out * gain
    return inv * (grad_unit - unit * jnp.mean(grad_unit * unit, axis=-1, keepdims=True))


def rope_constants():
    half = HEAD_DIM // 2
    freqs = np.float32(rope_base) ** (
        -(np.arange(half, dtype=np.float32) * np.float32(2.0) / np.float32(2 * half))
    )
    angles = np.arange(LENGTH, dtype=np.float32)[:, None] * freqs.astype(np.float32)[None, :]
    cos, sin = np.cos(angles), np.sin(angles)
    return np.concatenate([cos, sin], axis=1).astype(np.float32)


def coords():
    dp, sq = lax.axis_index("dp"), lax.axis_index("seq")
    return dp // AXIS, dp % AXIS, sq // 2, sq % 2


def device(y, z, x, c):
    return (y * AXIS + z, x * 2 + c)


def seq_peers(y, z, x, c):
    return [
        (k, j, device(y, z, (x + k) % AXIS, (c + j) % 2))
        for k in range(AXIS)
        for j in range(2)
        if (k, j) != (0, 0)
    ]


def greet(peers):
    sem = pltpu.get_barrier_semaphore()
    for peer in peers:
        pl.semaphore_signal(sem, inc=1, device_id=peer, device_id_type=MESH)


def all_in(peers):
    pl.semaphore_wait(pltpu.get_barrier_semaphore(), len(peers))


def around(y, z, x, c):
    yp = [device((y + k) % AXIS, z, x, c) for k in (1, 2, 3)]
    zp = [device(y, (z + k) % AXIS, x, c) for k in (1, 2, 3)]
    return seq_peers(y, z, x, c), yp, zp


class Copies:
    def __init__(self, send, recv, local):
        self.send, self.recv, self.local = send, recv, local
        self.n, self.n_local = 0, 0
        self.sent = []

    def to(self, src, dst, dev):
        copy = pltpu.make_async_remote_copy(
            src_ref=src, dst_ref=dst, send_sem=self.send.at[self.n], recv_sem=self.recv.at[self.n],
            device_id=dev, device_id_type=MESH,
        )
        self.n += 1
        copy.start()
        self.sent.append(copy)
        return copy

    def here(self, src, dst):
        copy = pltpu.make_async_copy(src, dst, self.local.at[self.n_local])
        self.n_local += 1
        copy.start()
        return copy

    def finish(self):
        for copy in self.sent:
            copy.wait_send()
        self.sent = []

    def drain(self, copies):
        for copy in copies:
            copy.wait_send()
        done = {id(copy) for copy in copies}
        self.sent = [copy for copy in self.sent if id(copy) not in done]


class SeqGather:
    def __init__(self, cm, own, buf, co):
        self.cm, self.own, self.buf, self.co = cm, own, buf, co
        self.half = buf.shape[1] // 2

    def slot(self, k):
        y, z, x, c = self.co
        return self.buf.at[((x + k) % AXIS) * 2 + c]

    def start(self):
        y, z, x, c = self.co
        self.sib = device(y, z, x, 1 - c)
        self.plus, self.minus = device(y, z, (x + 1) % AXIS, c), device(y, z, (x + 3) % AXIS, c)
        self.a = self.cm.to(self.own, self.slot(0), self.plus)
        self.b = self.cm.to(self.own, self.slot(0), self.minus)
        self.s0 = self.cm.to(self.own, self.slot(0), self.sib)
        self.l = self.cm.here(self.own, self.slot(0))

    def forward(self):
        h = self.half
        lo, hi = pl.ds(0, h), pl.ds(h, h)
        self.a.wait_recv()
        left = self.slot(3)
        self.fa = self.cm.to(left.at[lo], left.at[lo], self.plus)
        self.s1 = self.cm.to(left, left, self.sib)
        self.b.wait_recv()
        right = self.slot(1)
        self.fb = self.cm.to(right.at[hi], right.at[hi], self.minus)
        self.s2 = self.cm.to(right, right, self.sib)

    def last(self):
        h = self.half
        lo, hi = pl.ds(0, h), pl.ds(h, h)
        opp = self.slot(2)
        self.fa.wait_recv()
        self.s3 = self.cm.to(opp.at[lo], opp.at[lo], self.sib)
        self.fb.wait_recv()
        self.s4 = self.cm.to(opp.at[hi], opp.at[hi], self.sib)

    def drain(self):
        self.cm.drain(
            [self.a, self.b, self.s0, self.fa, self.s1, self.fb, self.s2, self.s3, self.s4]
        )

    def wait_chip(self, k):
        if k == 0:
            self.l.wait()
            self.s0.wait_recv()
        elif k == 3:
            self.s1.wait_recv()
        elif k == 1:
            self.s2.wait_recv()
        else:
            self.s3.wait_recv()
            self.s4.wait_recv()


class DpGather:
    def __init__(self, cm, own, buf, co, axis):
        self.cm, self.own, self.buf, self.co, self.axis = cm, own, buf, co, axis
        n = own.shape[axis]
        self.h, self.q = n // 2, n // 4

    def part(self, ref, half, quarter=None):
        lo = half * self.h + (0 if quarter is None else quarter * self.q)
        size = self.h if quarter is None else self.q
        cut = pl.ds(lo, size)
        lead = len(ref.shape) - 2
        index = (slice(None),) * lead + ((cut, slice(None)) if self.axis == 0 else (slice(None), cut))
        return ref.at[index]

    def both(self, src_p, dst_p, src_m, dst_m, along):
        y, z, x, c = self.co
        if along == 0:
            plus, minus = device((y + 1) % AXIS, z, x, c), device((y + 3) % AXIS, z, x, c)
        else:
            plus, minus = device(y, (z + 1) % AXIS, x, c), device(y, (z + 3) % AXIS, x, c)
        return (self.cm.to(src_p, dst_p, plus), self.cm.to(src_m, dst_m, minus))

    def start(self):
        y, z, _, _ = self.co
        mine = self.buf.at[y, z]
        self.l = self.cm.here(self.own, mine)
        self.one = []
        for half in (0, 1):
            src, dst = self.part(self.own, half), self.part(mine, half)
            self.one.append(self.both(src, dst, src, dst, half))

    def spread(self):
        y, z, _, _ = self.co
        self.two = []
        for half in (0, 1):
            if half == 0:
                left, right = self.buf.at[(y + 3) % AXIS, z], self.buf.at[(y + 1) % AXIS, z]
            else:
                left, right = self.buf.at[y, (z + 3) % AXIS], self.buf.at[y, (z + 1) % AXIS]
            for copy in self.one[half]:
                copy.wait_recv()
            lp, rp = self.part(left, half, 0), self.part(right, half, 1)
            self.two.append(self.both(lp, lp, rp, rp, half))

    def line(self, half, k):
        y, z, _, _ = self.co
        if half == 0:
            return self.buf.at[:, (z + k) % AXIS]
        return self.buf.at[(y + k) % AXIS]

    def turn(self, far=False):
        y, z, xx, c = self.co
        self.l.wait()
        self.three, self.four = [], [[], []]
        for half in (0, 1):
            for copy in self.two[half]:
                copy.wait_recv()
            mine = self.part(self.line(half, 0), half)
            self.three.append(self.both(mine, mine, mine, mine, 1 - half))
            if far:
                there = device(y, (z + 2) % AXIS, xx, c) if half == 0 else device((y + 2) % AXIS, z, xx, c)
                self.four[half] = [self.cm.to(mine, mine, there), *self.three[half]]

    def last(self):
        self.four = []
        for half in (0, 1):
            for copy in self.three[half]:
                copy.wait_recv()
            lp = self.part(self.line(half, 3), half, 0)
            rp = self.part(self.line(half, 1), half, 1)
            self.four.append(self.both(lp, lp, rp, rp, 1 - half))

    def wait(self):
        for half in (0, 1):
            for copy in self.four[half]:
                copy.wait_recv()


def off(n):
    return jnp.where(n == 0, 2, jnp.where(n == 1, 1, jnp.where(n == 2, 3, 0)))


class SeqScatter:
    def __init__(self, part, sib_recv, x_recv, sems, co, kept=None):
        self.part, self.sib_recv, self.x_recv, self.sems, self.co = part, sib_recv, x_recv, sems, co
        self.kept = kept

    def ours(self, n):
        return self.part.at[2 * n + 1] if self.kept is None else self.kept.at[n]

    def sib_copy(self, n):
        y, z, x, c = self.co
        return pltpu.make_async_remote_copy(
            src_ref=self.part.at[2 * n], dst_ref=self.sib_recv.at[n],
            send_sem=self.sems.at[0, n], recv_sem=self.sems.at[1, n],
            device_id=device(y, z, x, 1 - c), device_id_type=MESH,
        )

    def x_copy(self, n):
        y, z, x, c = self.co
        return pltpu.make_async_remote_copy(
            src_ref=self.ours(n), dst_ref=self.x_recv.at[n],
            send_sem=self.sems.at[2, n], recv_sem=self.sems.at[3, n],
            device_id=device(y, z, (x + off(n)) % AXIS, c), device_id_type=MESH,
        )

    def combine(self, n, go=True):
        self.sib_copy(n).wait_recv()
        ours = self.ours(n)

        def add(i, _):
            cut = pl.ds(i * 32, 32)
            total = ours[cut, :].astype(f32) + self.sib_recv[n, cut, :].astype(f32)
            ours[cut, :] = total.astype(bf16)
            return 0

        lax.fori_loop(0, SPAN // 32, add, 0)
        if go:

            @pl.when(n < 3)
            def _():
                self.x_copy(n).start()

    def arrive(self):
        for n in range(3):
            self.x_copy(n).wait_recv()

    def rows(self, cut):
        total = self.ours(3)[cut, :].astype(f32)
        for n in range(3):
            total = total + self.x_recv[n, cut, :].astype(f32)
        return total

    def finish(self):
        for n in range(4):
            self.sib_copy(n).wait_send()
        for n in range(3):
            self.x_copy(n).wait_send()


def scatter_scratch():
    return [
        pltpu.VMEM((8, SPAN, WIDTH), bf16),
        pltpu.VMEM((4, SPAN, WIDTH), bf16),
        pltpu.VMEM((3, SPAN, WIDTH), bf16),
        pltpu.SemaphoreType.DMA((4, 4)),
    ]


def swap(u):
    return pltpu.roll(u, HEAD_DIM // 2, 1)


def rope_rows(table):
    low = lax.broadcasted_iota(jnp.int32, table.shape, 1) < HEAD_DIM // 2
    other = swap(table)
    return jnp.where(low, table, other), jnp.where(low, -other, table)


def peer_index(x, c, k, j):
    return ((x + k) % AXIS) * 2 + (c + j) % 2


class DpScatter:
    def __init__(self, cm, grad, acc, one, two, co, tile):
        self.cm, self.grad, self.acc, self.r1, self.r2 = cm, grad, acc, one, two
        self.co, self.tile = co, tile
        self.h = acc.shape[2]

    def part(self, ref, half):
        return ref.at[:, pl.ds(half * self.h, self.h)]

    def line(self, half, k):
        y, z, _, _ = self.co
        if half == 0:
            return self.part(self.grad.at[(y + k) % AXIS], half)
        return self.part(self.grad.at[:, (z + k) % AXIS], half)

    def away(self, along, k):
        y, z, x, c = self.co
        if along == 0:
            return device((y + k) % AXIS, z, x, c)
        return device(y, (z + k) % AXIS, x, c)

    def start(self):
        self.own = [self.cm.here(self.line(h, 0), self.acc.at[h]) for h in (0, 1)]
        self.first = [[], []]
        for k in (2, 1, 3):
            for h in (0, 1):
                self.first[h].append(
                    self.cm.to(self.line(h, k), self.r1.at[h, k - 1], self.away(h, k))
                )

    def add_first(self):
        rows = self.acc.shape[2]
        for h in (0, 1):
            self.own[h].wait()
            for copy in self.first[h]:
                copy.wait_recv()

            def add(t, _, h=h):
                q = t // (rows // self.tile)
                cut = pl.ds((t % (rows // self.tile)) * self.tile, self.tile)
                total = self.acc[h, q, cut, :].astype(f32)
                for k in range(3):
                    total = total + self.r1[h, k, q, cut, :].astype(f32)
                self.acc[h, q, cut, :] = total.astype(bf16)
                return 0

            lax.fori_loop(0, AXIS * (rows // self.tile), add, 0)

    def send_second(self):
        y, z, _, _ = self.co
        self.second = [[], []]
        for h in (0, 1):
            mine = z if h == 0 else y
            for k in (2, 1, 3):
                self.second[h].append(
                    self.cm.to(self.acc.at[h, (mine + k) % AXIS], self.r2.at[h, k - 1], self.away(1 - h, k))
                )

    def mid(self):
        self.add_first()
        self.send_second()

    def last(self, out):
        y, z, _, _ = self.co
        rows, cols = self.acc.shape[2:]
        for h in (0, 1):
            for copy in self.second[h]:
                copy.wait_recv()
            mine = z if h == 0 else y

            def add(t, _, h=h, mine=mine):
                cut = pl.ds(t * self.tile, self.tile)
                total = self.acc[h, mine, cut, :].astype(f32)
                for k in range(3):
                    total = total + self.r2[h, k, cut, :].astype(f32)
                out[pl.ds(h * self.h + t * self.tile, self.tile), :] = total.astype(out.dtype)
                return 0

            lax.fori_loop(0, rows // self.tile, add, 0)


def dp_scatter_scratch(rows, cols):
    return [
        pltpu.VMEM((2, AXIS, rows, cols), bf16),
        pltpu.VMEM((2, 3, AXIS, rows, cols), bf16),
        pltpu.VMEM((2, 3, rows, cols), bf16),
    ]


def front_kernel(
    tok, cot, extra, w_query, w_key, w_value, w_out, w_gate, w_up, w_down, table,
    x1_o, dx1_o, dab_o, gain2_o, h1_o, pre_o, qb_o, kb_o, vb_o, ob_o, gains, gq_o, wo_o, ggu_o, pd_o, dacc_o,
    xg, pq, pm, wod, a2a_q, a2a_m, wq, wo_b, wo_v, wd_b, wd_v, wgu, o1, o2, o3o, o3d, h2_loc,
    dy_v, hid, dgu, pdv, d_one, x1_v, pre, qb, kb, vb, ob, d_acc,
    part, sib_recv, x_recv, rs_sems, rs_sems2, send, recv, local,
):
    co = y, z, x, c = coords()
    s = x * 2 + c
    peers, yp, zp = around(*co)
    everyone = [p for _, _, p in peers] + yp + zp
    greet(everyone)
    cm = Copies(send, recv, local)
    for t in range(NS):
        pq[t, :, 0:256] = w_query[:, t * 256 : t * 256 + 256]
        pq[t, :, 256:384] = w_key[:, t * 128 : t * 128 + 128]
        pq[t, :, 384:512] = w_value[:, t * 128 : t * 128 + 128]
        pq[t, :, 512:640] = extra[...]
    all_in(everyone)

    aq = [cm.to(pq.at[peer_index(x, c, k, j)], a2a_q.at[s], p) for k, j, p in peers]
    lq = cm.here(pq.at[s], a2a_q.at[s])
    g_tok = SeqGather(cm, tok, xg, co)
    g_tok.start()
    for t in range(NS):
        pm[t, :, 0:FFS] = w_gate[:, t * FFS : t * FFS + FFS]
        pm[t, :, FFS : 2 * FFS] = w_up[:, t * FFS : t * FFS + FFS]
    wod[0:WR, :] = w_out[...]
    wod[WR : WR + FR, :] = w_down[...]

    def quarter(i):
        return pl.ds(pl.multiple_of(i * 512, 512), 512)

    def chunk(i):
        return pl.ds(pl.multiple_of(i * 128, 128), 128)

    o_one = [cm.to(wod.at[:, quarter((y + k) % AXIS)], o1.at[y], yp[k - 1]) for k in (1, 2, 3)]
    l_one = cm.here(wod.at[:, quarter(y)], o1.at[y])
    am = [cm.to(pm.at[peer_index(x, c, k, j)], a2a_m.at[s], p) for k, j, p in peers]
    lm = cm.here(pm.at[s], a2a_m.at[s])
    lq.wait()
    for copy in aq:
        copy.wait_recv()
    g_q = DpGather(cm, a2a_q.reshape(NS * WR, QKV + GCOL), wq, co, 0)
    g_q.start()
    l_one.wait()
    for copy in o_one:
        copy.wait_recv()
    o_two = [cm.to(o1.at[:, :, chunk((z + k) % AXIS)], o2.at[z], zp[k - 1]) for k in (1, 2, 3)]
    l_two = cm.here(o1.at[:, :, chunk(z)], o2.at[z])
    g_q.spread()
    l_two.wait()
    for copy in o_two:
        copy.wait_recv()

    def rows_of(t, lo, n):
        return o2.at[pl.ds((t % 2) * 2, 2), t // 2, pl.ds(lo, n)]

    o_three = []
    for k, j, p in peers:
        t = peer_index(x, c, k, j)
        o_three.append(cm.to(rows_of(t, 0, WR), o3o.at[:, s], p))
        o_three.append(cm.to(rows_of(t, WR, FR), o3d.at[:, s], p))
    l_three = [
        cm.here(rows_of(s, 0, WR), o3o.at[:, s]),
        cm.here(rows_of(s, WR, FR), o3d.at[:, s]),
    ]
    g_q.turn()
    g_tok.forward()
    g_q.last()
    lm.wait()
    for copy in am:
        copy.wait_recv()
    g_m = DpGather(cm, a2a_m.reshape(NS * WR, 2 * FFS), wgu, co, 0)
    g_m.start()
    for copy in l_three:
        copy.wait()
    for copy in o_three:
        copy.wait_recv()
    g_o = DpGather(cm, o3o.reshape(2 * SPAN, SPAN), wo_b, co, 0)
    g_o.start()
    g_d = DpGather(cm, o3d.reshape(FFS, SPAN), wd_b, co, 0)
    g_d.start()
    g_m.spread()
    g_o.spread()
    g_d.spread()
    g_o.turn(True)
    g_m.turn()
    g_d.turn()
    g_q.wait()
    wq_out = cm.here(wq.at[:, :, :, pl.ds(0, QKV)], gq_o)

    wq2 = wq.reshape(WIDTH, QKV + GCOL)
    gcols = wq2[:, QKV:]
    flat = gcols.astype(f32).T
    gains[...] = flat[:8]
    gain_one = flat[0:1]
    rows = lax.broadcasted_iota(jnp.int32, (WIDTH, HEAD_DIM), 0)
    cols = lax.broadcasted_iota(jnp.int32, (WIDTH, HEAD_DIM), 1)
    pick = (rows == cols * WR).astype(bf16)
    head_gains = dot(flat[:8].astype(bf16), pick)
    gain_q, gain_k = head_gains[2:3], head_gains[3:4]
    gains[2:4, 0:HEAD_DIM] = head_gains[2:4]

    def normed(i, _):
        cut = pl.ds((i % 4) * 32, 32)
        v = xg[i // 4, cut, :].astype(f32)
        part[i // 4, cut, :] = (v * rms(v) * gain_one).astype(bf16)
        return 0

    g_tok.last()
    g_cot = SeqGather(cm, cot, dy_v, co)
    g_cot.start()
    for k in (0, 1, 3, 2):
        g_tok.wait_chip(k)
    lax.fori_loop(0, LENGTH // 32, normed, 0)
    h1_copy = cm.here(part, h1_o)

    def project(i, _):
        h = part[pl.ds(2 * i, 2)].reshape(2 * SPAN, WIDTH)
        p = dot(h, wq2[:, :QKV])
        cut = pl.ds(pl.multiple_of(i * 256, 256), 256)
        pre[cut, :] = p[:, :384]
        vb[cut, :] = p[:, 384:].astype(bf16)
        co_t, si_t = rope_rows(table[cut, :])
        for h_i in range(2):
            u = p[:, h_i * 128 : h_i * 128 + 128]
            u = u * rms(u) * gain_q
            u = (u * co_t + swap(u) * si_t).astype(bf16)
            qb[pl.ds(2 * i, 2), pl.ds(h_i * SPAN, SPAN), :] = u.reshape(2, SPAN, HEAD_DIM)
        u = p[:, 256:384]
        u = u * rms(u) * gain_k
        kb[cut, :] = (u * co_t + swap(u) * si_t).astype(bf16)
        return 0

    lax.fori_loop(0, 4, project, 0)
    outs = [cm.here(pre, pre_o), cm.here(qb, qb_o), cm.here(kb, kb_o), cm.here(vb, vb_o)]
    h1_copy.wait()
    g_tok.drain()
    g_o.wait()
    wo_copy = [
        cm.here(wo_b.at[yy, zz], wo_v.at[:, pl.ds((yy * AXIS + zz) * 128, 128)])
        for yy in range(AXIS)
        for zz in range(AXIS)
    ]
    for copy in wo_copy:
        copy.wait()
    wo_out = cm.here(wo_v, wo_o)
    g_cot.forward()

    rs = SeqScatter(part, sib_recv, x_recv, rs_sems, co)

    def attend(i, slot):
        sc = dot_nt(qb[i], kb[...]) * score_scale
        r = lax.broadcasted_iota(jnp.int32, (2 * SPAN, LENGTH), 0) % SPAN + i * SPAN
        k = lax.broadcasted_iota(jnp.int32, (2 * SPAN, LENGTH), 1)
        sc = jnp.where(k <= r, sc, -1e30)
        top = jnp.max(sc, axis=-1, keepdims=True)
        ex = jnp.exp(sc - top)
        tot = jnp.sum(ex, axis=-1, keepdims=True)
        pb = (ex / tot).astype(bf16)
        o = dot(pb, vb[...]).astype(bf16)
        o = jnp.concatenate([o[:SPAN], o[SPAN:]], axis=1)
        ob[pl.ds(pl.multiple_of(i * SPAN, SPAN), SPAN), :] = o
        part[slot] = dot(o, wo_v[...]).astype(bf16)

    def pair(n, _):
        chip = (x + off(n)) % AXIS
        attend(chip * 2 + 1 - c, 2 * n)
        rs.sib_copy(n).start()

        @pl.when(n > 0)
        def _():
            rs.combine(n - 1)

        attend(chip * 2 + c, 2 * n + 1)
        return 0

    lax.fori_loop(0, 4, pair, 0)
    rs.combine(3)
    g_cot.last()
    g_m.last()
    g_d.last()
    rs.arrive()

    def residual(i, _):
        cut = pl.ds(i * 32, 32)
        v = xg[s, cut, :].astype(f32) + rs.rows(cut)
        x1_v[cut, :] = v
        h2_loc[cut, :] = (v * rms(v) * gains[1:2, :]).astype(bf16)
        return 0

    lax.fori_loop(0, SPAN // 32, residual, 0)
    rs.finish()
    outs += [cm.here(x1_v, x1_o), cm.here(ob, ob_o)]

    g_h2 = SeqGather(cm, h2_loc, xg, co)
    g_h2.start()
    g_d.wait()
    wd_copy = [
        cm.here(wd_b.at[yy, zz], wd_v.at[:, pl.ds((yy * AXIS + zz) * 128, 128)])
        for yy in range(AXIS)
        for zz in range(AXIS)
    ]
    g_m.wait()
    for copy in wd_copy:
        copy.wait()
    rs = SeqScatter(part, sib_recv, x_recv, rs_sems2, co)
    wgu2 = wgu.reshape(WIDTH, 2 * FFS)
    order = {2: 0, 1: 1, 3: 2, 0: 3}

    def chip_of(k):
        return (x + k) % AXIS

    def forward(k):
        chip = chip_of(k)
        rows = pl.ds(pl.multiple_of(chip * 256, 256), 256)
        two = pl.ds(2 * chip, 2)

        def tile(f, _):
            lo = pl.multiple_of(f * 256, 256)
            h = xg[two].reshape(256, WIDTH)
            gate = dot(h, wgu2[:, pl.ds(lo, 256)])
            up = dot(h, wgu2[:, pl.ds(pl.multiple_of(lo + FFS, 256), 256)])
            dh = dot_nt(dy_v[two].reshape(256, WIDTH), wd_v[pl.ds(lo, 256), :])
            sig = jax.nn.sigmoid(gate)
            silu = gate * sig
            hid[rows, pl.ds(lo, 256)] = (silu * up).astype(bf16)
            dgate = dh * up * (sig * (1.0 + gate * (1.0 - sig)))
            dgu[rows, pl.ds(lo, 256)] = dgate.astype(bf16)
            dgu[rows, pl.ds(pl.multiple_of(lo + FFS, 256), 256)] = (dh * silu).astype(bf16)
            return 0

        lax.fori_loop(0, FFS // 256, tile, 0)

    def put(ref, n, cols, o):
        ref[2 * n + 1 - c, :, cols] = o[:SPAN]
        ref[2 * n + c, :, cols] = o[SPAN:]

    def back(k):
        n = order[k]
        rows = pl.ds(pl.multiple_of(chip_of(k) * 256, 256), 256)

        def tile(m, _):
            cols = pl.ds(pl.multiple_of(m * 256, 256), 256)
            put(part, n, cols, dot_nt(dgu[rows, :], wgu2[cols, :]).astype(bf16))
            return 0

        lax.fori_loop(0, WIDTH // 256, tile, 0)
        rs.sib_copy(n).start()

    g_h2.wait_chip(0)
    g_cot.wait_chip(0)
    forward(0)
    g_h2.forward()
    back(0)
    g_h2.wait_chip(3)
    g_cot.wait_chip(3)
    forward(3)
    g_h2.last()
    back(3)
    g_h2.wait_chip(1)
    g_cot.wait_chip(1)
    forward(1)
    rs.combine(order[3])
    back(1)
    g_h2.wait_chip(2)
    g_cot.wait_chip(2)
    forward(2)
    rs.combine(order[1])
    back(2)
    rs.combine(order[0])
    cm.finish()

    def down_grad(m, _):
        cut = pl.ds(pl.multiple_of(m * 256, 256), 256)
        o = dot_tn(hid[:, cut], dy_v[...].reshape(LENGTH, WIDTH)).astype(bf16)
        for yy in range(AXIS):
            for zz in range(AXIS):
                lo = (yy * AXIS + zz) * 128
                wd_b[yy, zz, cut, :] = o[:, lo : lo + 128]
        return 0

    lax.fori_loop(0, 1, down_grad, 0)
    rs.combine(order[2])
    lax.fori_loop(1, FFS // 256, down_grad, 0)
    r_d = DpScatter(cm, wd_b, d_acc, d_one, None, co, 128)
    r_d.start()

    for k in range(4):
        n = order[k]
        rows = pl.ds(pl.multiple_of(chip_of(k) * 256, 256), 256)

        def down(m, _):
            cols = pl.ds(pl.multiple_of(m * 512, 512), 512)
            put(pdv, n, cols, dot(hid[rows, :], wd_v[:, cols]).astype(bf16))
            return 0

        lax.fori_loop(0, WIDTH // 512, down, 0)
    outs.append(cm.here(pdv, pd_o))

    def gate_up(m, _):
        cols = pl.ds(pl.multiple_of(m * 256, 256), 256)
        wgu2[cols, :] = dot_tn(xg[:, :, cols].reshape(LENGTH, 256), dgu[...]).astype(bf16)
        return 0

    lax.fori_loop(0, WIDTH // 256, gate_up, 0)
    outs.append(cm.here(wgu, ggu_o))
    rs.arrive()
    gain_two = gains[1:2, :]

    def mlp_back(i, acc):
        cut = pl.ds(i * 32, 32)
        v = x1_v[cut, :]
        inv = rms(v)
        unit = v * inv
        dh2 = rs.rows(cut)
        dx1 = dy_v[s, cut, :].astype(f32) + rms_back(dh2, gain_two, unit, inv)
        dx1_o[cut, :] = dx1
        dab_o[cut, :] = dx1.astype(bf16)
        return acc + jnp.sum(dh2 * unit, axis=0, keepdims=True)

    acc = lax.fori_loop(0, SPAN // 32, mlp_back, jnp.zeros((1, WIDTH), f32))
    gain2_o[...] = jnp.broadcast_to(acc, (8, WIDTH))
    r_d.add_first()
    outs.append(cm.here(d_acc, dacc_o))
    rs.finish()
    wo_out.wait()
    wq_out.wait()
    for copy in outs:
        copy.wait()
    cm.finish()


def front(*args):
    any_, vm = pl.BlockSpec(memory_space=pl.ANY), pl.BlockSpec(memory_space=pltpu.VMEM)
    sds = jax.ShapeDtypeStruct
    vmem = pltpu.VMEM
    n_copies, n_local = 160, 72
    return pl.pallas_call(
        front_kernel,
        name="attn_forward",
        out_shape=[
            sds((SPAN, WIDTH), f32), sds((SPAN, WIDTH), f32), sds((SPAN, WIDTH), bf16),
            sds((8, WIDTH), f32), sds((8, SPAN, WIDTH), bf16), sds((LENGTH, 384), f32),
            sds((8, 2 * SPAN, 128), bf16), sds((LENGTH, 128), bf16), sds((LENGTH, 128), bf16),
            sds((LENGTH, 256), bf16), sds((8, WIDTH), f32), sds((4, 4, 128, QKV), bf16),
            sds((256, WIDTH), bf16), sds((4, 4, 128, 2 * FFS), bf16), sds((8, SPAN, WIDTH), bf16),
            sds((2, 4, FFS // 2, 128), bf16),
        ],
        in_specs=[any_] * 2 + [vm] * 9,
        out_specs=[any_, vm, vm, vm, any_, any_, any_, any_, any_, any_, vm, any_, any_, any_, any_, any_],
        scratch_shapes=[
            vmem((8, SPAN, WIDTH), bf16),
            vmem((NS, WR, QKV + GCOL), bf16), vmem((NS, WR, 2 * FFS), bf16),
            vmem((WR + FR, WIDTH), bf16),
            vmem((NS, WR, QKV + GCOL), bf16), vmem((NS, WR, 2 * FFS), bf16),
            vmem((4, 4, 128, QKV + GCOL), bf16),
            vmem((4, 4, 256, 128), bf16), vmem((256, WIDTH), bf16),
            vmem((4, 4, FFS, 128), bf16), vmem((FFS, WIDTH), bf16),
            vmem((4, 4, 128, 2 * FFS), bf16),
            vmem((4, WR + FR, 512), bf16), vmem((4, 4, WR + FR, 128), bf16),
            vmem((2, NS, WR, 128), bf16), vmem((2, NS, FR, 128), bf16),
            vmem((SPAN, WIDTH), bf16),
            vmem((8, SPAN, WIDTH), bf16), vmem((LENGTH, FFS), bf16), vmem((LENGTH, 2 * FFS), bf16),
            vmem((8, SPAN, WIDTH), bf16), vmem((2, 3, AXIS, FFS // 2, 128), bf16),
            vmem((SPAN, WIDTH), f32), vmem((LENGTH, 384), f32), vmem((8, 2 * SPAN, 128), bf16),
            vmem((LENGTH, 128), bf16), vmem((LENGTH, 128), bf16), vmem((LENGTH, 256), bf16),
            vmem((2, 4, FFS // 2, 128), bf16),
            *scatter_scratch(),
            pltpu.SemaphoreType.DMA((4, 4)),
            pltpu.SemaphoreType.DMA((n_copies,)),
            pltpu.SemaphoreType.DMA((n_copies,)),
            pltpu.SemaphoreType.DMA((n_local,)),
        ],
        compiler_params=pltpu.CompilerParams(
            collective_id=1, has_side_effects=True, vmem_limit_bytes=VMEM_LIMIT
        ),
    )(*args)


class RowsHome:
    def __init__(self, cm, res, r2, r1, out, co):
        self.cm, self.res, self.r2, self.r1, self.out, self.co = cm, res, r2, r1, out, co
        self.peers, self.yp, self.zp = around(*co)

    def step(self, sends, here):
        self.wait()
        self.arriving = [self.cm.to(*a) for a in sends]
        self.local = self.cm.here(*here)

    def wait(self):
        if hasattr(self, "arriving"):
            self.local.wait()
            for copy in self.arriving:
                copy.wait_recv()

    def over_seq(self):
        y, z, x, c = self.co
        s = x * 2 + c
        dst = self.r2.at[pl.ds((s % 2) * 2, 2), s // 2]
        self.step(
            [(self.res.at[:, peer_index(x, c, k, j)], dst, p) for k, j, p in self.peers],
            (self.res.at[:, s], dst),
        )

    def over_z(self):
        y, z, x, c = self.co
        dst = self.r1.at[:, :, pl.ds(pl.multiple_of(z * 128, 128), 128)]
        self.step(
            [(self.r2.at[(z + k) % AXIS], dst, self.zp[k - 1]) for k in (1, 2, 3)],
            (self.r2.at[z], dst),
        )

    def over_y(self):
        y, z, x, c = self.co
        dst = self.out.at[:, pl.ds(pl.multiple_of(y * 512, 512), 512)]
        self.step(
            [(self.r1.at[(y + k) % AXIS], dst, self.yp[k - 1]) for k in (1, 2, 3)],
            (self.r1.at[y], dst),
        )


def back_kernel(
    dab_loc, pd, ggu, h1, gq, wo, dacc, dx1, tok, x1, pre_i, qb_i, kb_i, vb_i, ob_i,
    gain2, gains, table,
    gt_o, block_o, gwq_o, gwk_o, gwv_o, gwo_o, gwg_o, gwu_o, gwd_o, gg_o,
    dab, h1_v, wq, wo_v, pbuf, dob, dk, dv, dqkv, gacc,
    part, sib_recv, x_recv, rs_sems, kept, sib2, x2, rs2_sems,
    m_acc, m_one, m_two, o_acc, o_one, o_two, q_acc, q_one, q_two, d_two,
    mo, mr, qo, qr, go, gqk, oo, o2g, o1g, ow, od, d2g, d1g, dw,
    gg, g_one, g_two, g_all, g_sum, d_acc, tok_v, x1_v, pre, qb, kb, vb, ob,
    send, recv, local,
):
    co = y, z, x, c = coords()
    s = x * 2 + c
    peers, yp, zp = around(*co)
    everyone = [p for _, _, p in peers] + yp + zp
    greet(everyone)
    cm = Copies(send, recv, local)
    l_qk = [cm.here(qb_i, qb), cm.here(kb_i, kb)]
    l_pd = [cm.here(pd.at[2 * n + 1], kept.at[n]) for n in range(4)]
    l_wo = cm.here(wo, wo_v)
    l_wq = cm.here(gq, wq)

    def h1_load(m):
        return cm.here(h1.at[:, :, pl.ds(m * 256, 256)], h1_v.at[m % 2])

    l_h1 = [h1_load(0), h1_load(1)]
    l_in = [
        cm.here(vb_i, vb), cm.here(ob_i, ob), cm.here(pre_i, pre), cm.here(dacc, d_acc),
        cm.here(dx1, gt_o), cm.here(tok, tok_v), cm.here(x1, x1_v),
    ]
    all_in(everyone)
    g_dab = SeqGather(cm, dab_loc, dab, co)
    g_dab.start()
    r_d = DpScatter(cm, None, d_acc, None, d_two, co, 128)
    for copy in l_in:
        copy.wait()
    r_d.send_second()
    r_m = DpScatter(cm, ggu, m_acc, m_one, m_two, co, 16)
    r_m.start()
    rs2 = SeqScatter(pd, sib2, x2, rs2_sems, co, kept)
    for n in range(4):
        l_pd[n].wait()
        rs2.sib_copy(n).start()

    def probs(i, _):
        sc = dot_nt(qb[i], kb[...]) * score_scale
        r = lax.broadcasted_iota(jnp.int32, (2 * SPAN, LENGTH), 0) % SPAN + i * SPAN
        k = lax.broadcasted_iota(jnp.int32, (2 * SPAN, LENGTH), 1)
        sc = jnp.where(k <= r, sc, -1e30)
        ex = jnp.exp(sc - jnp.max(sc, axis=-1, keepdims=True))
        pbuf[i] = (ex / jnp.sum(ex, axis=-1, keepdims=True)).astype(bf16)
        return 0

    for copy in l_qk:
        copy.wait()
    lax.fori_loop(0, 4, probs, 0)
    g_dab.forward()
    lax.fori_loop(4, 8, probs, 0)
    dk[...] = jnp.zeros_like(dk)
    dv[...] = jnp.zeros_like(dv)
    gacc[...] = jnp.zeros_like(gacc)
    l_wo.wait()

    def out_back(k):
        g_dab.wait_chip(k)
        two = pl.ds(2 * ((x + k) % AXIS), 2)
        o = dot_nt(dab[two].reshape(2 * SPAN, WIDTH), wo_v[...]).astype(bf16)
        for j in range(2):
            blk = o[j * SPAN : (j + 1) * SPAN]
            dob[2 * ((x + k) % AXIS) + j] = jnp.concatenate([blk[:, :128], blk[:, 128:]], axis=0)

    out_back(0)
    out_back(3)
    out_back(1)
    for n in range(4):
        rs2.combine(n, False)
    g_dab.last()
    for n in range(3):
        rs2.x_copy(n).start()
    out_back(2)

    def out_grad(m, _):
        cols = pl.ds(pl.multiple_of(m * 512, 512), 512)
        o = dot_tn(ob[...], dab[:, :, cols].reshape(LENGTH, 512)).astype(bf16)
        for j in range(AXIS):
            go[m, j] = o[:, j * 128 : j * 128 + 128]
        return 0

    lax.fori_loop(0, AXIS, out_grad, 0)
    r_o = DpScatter(cm, go, o_acc, o_one, o_two, co, 128)
    r_o.start()

    rs = SeqScatter(part, sib_recv, x_recv, rs_sems, co)
    l_wq.wait()
    wq2 = wq.reshape(WIDTH, QKV)
    gain_q, gain_k = gains[2:3, 0:128], gains[3:4, 0:128]

    def head_back(g, u, gain, co_t, si_t):
        g = g * co_t - swap(g) * si_t
        inv = rms(u)
        unit = u * inv
        return rms_back(g, gain, unit, inv), jnp.sum(g * unit, axis=0, keepdims=True)

    def slot_of(chip):
        k = (chip - x + AXIS) % AXIS
        return jnp.where(k == 2, 0, jnp.where(k == 1, 1, jnp.where(k == 3, 2, 3)))

    def chip_back(t, _):
        chip = 3 - t

        def block(j, _):
            i = chip * 2 + 1 - j
            q, do, p = qb[i], dob[i], pbuf[i]
            dp = dot_nt(do, vb[...])
            pf = p.astype(f32)
            delta = jnp.sum(pf * dp, axis=-1, keepdims=True)
            ds = (pf * (dp - delta)).astype(bf16)
            dk[...] += dot_tn(ds, q)
            dv[...] += dot_tn(p, do)
            dq = dot(ds, kb[...]) * score_scale
            cut = pl.ds(pl.multiple_of(i * SPAN, SPAN), SPAN)
            u = jnp.concatenate([pre[cut, 0:128], pre[cut, 128:256]], axis=0)
            co_t, si_t = rope_rows(table[cut, :])
            co_t = jnp.concatenate([co_t] * 2, axis=0)
            si_t = jnp.concatenate([si_t] * 2, axis=0)
            dqp, gsum = head_back(dq, u, gain_q, co_t, si_t)
            gacc[0:1, :] += gsum
            dqp = dqp.astype(bf16)
            dqkv[cut, 0:128] = dqp[:SPAN]
            dqkv[cut, 128:256] = dqp[SPAN:]
            return 0

        lax.fori_loop(0, 2, block, 0)
        cut = pl.ds(pl.multiple_of(chip * 256, 256), 256)
        co_t, si_t = rope_rows(table[cut, :])
        dkp, gsum = head_back(dk[cut, :] * score_scale, pre[cut, 256:384], gain_k, co_t, si_t)
        gacc[1:2, :] += gsum
        dqkv[cut, 256:384] = dkp.astype(bf16)
        dqkv[cut, 384:512] = dv[cut, :].astype(bf16)
        n = slot_of(chip)

        @pl.when(t % 2 == 1)
        def _():
            rs.combine(slot_of(chip + 1))

        def tile(m, _):
            cols = pl.ds(pl.multiple_of(m * 512, 512), 512)
            o = dot_nt(dqkv[cut, :], wq2[cols, :]).astype(bf16)
            part[2 * n + 1 - c, :, cols] = o[:SPAN]
            part[2 * n + c, :, cols] = o[SPAN:]
            return 0

        lax.fori_loop(0, WIDTH // 512, tile, 0)
        rs.sib_copy(n).start()
        return 0

    lax.fori_loop(0, 2, chip_back, 0)
    rs.combine(slot_of(2))
    r_m.mid()
    lax.fori_loop(2, 4, chip_back, 0)
    rs.combine(slot_of(0))

    for m in range(8):
        l_h1[m].wait()
        o = dot_tn(h1_v[m % 2].reshape(LENGTH, 256), dqkv[...]).astype(bf16)
        gqk[m // 2, 2 * (m % 2)] = o[:SPAN]
        gqk[m // 2, 2 * (m % 2) + 1] = o[SPAN:]
        if m < 6:
            l_h1.append(h1_load(m + 2))
    r_q = DpScatter(cm, gqk, q_acc, q_one, q_two, co, 64)
    r_q.start()
    r_o.mid()
    r_d.last(od.reshape(FFS, SPAN))
    h_d = RowsHome(cm, od, d2g, d1g, dw, co)
    h_d.over_seq()
    r_m.last(mo.reshape(NS * WR, 2 * FFS))
    a_m = [cm.to(mo.at[peer_index(x, c, k, j)], mr.at[s], p) for k, j, p in peers]
    l_mo = cm.here(mo.at[s], mr.at[s])

    rs.arrive()
    gain_one = gains[0:1, :]

    def input_back(i, acc):
        cut = pl.ds(i * 32, 32)
        v = tok_v[cut, :].astype(f32)
        inv = rms(v)
        unit = v * inv
        dh1 = rs.rows(cut)
        gt_o[cut, :] = gt_o[cut, :] + rms_back(dh1, gain_one, unit, inv)
        return acc + jnp.sum(dh1 * unit, axis=0, keepdims=True)

    gain1 = lax.fori_loop(0, SPAN // 32, input_back, jnp.zeros((1, WIDTH), f32))

    dev_i = lax.broadcasted_iota(jnp.int32, (ND * NS, WIDTH), 0)
    col_j = lax.broadcasted_iota(jnp.int32, (ND * NS, WIDTH), 1)
    mine = col_j // WR == dev_i
    row_j = lax.broadcasted_iota(jnp.int32, (WIDTH, 128), 0)
    lane = lax.broadcasted_iota(jnp.int32, (WIDTH, 128), 1)
    rows = jnp.zeros((ND * NS, 128), f32)
    for v, shift in ((gain1, 0), (gain2[0:1, :], WR)):
        rows = rows + dot(
            jnp.where(mine, v, 0.0).astype(bf16), (lane == row_j % WR + shift).astype(bf16)
        )
    eye_i = lax.broadcasted_iota(jnp.int32, (128, 128), 0)
    eye_j = lax.broadcasted_iota(jnp.int32, (128, 128), 1)
    for n in range(2):
        rows = rows + dot(
            jnp.where(eye_i == eye_j, gacc[n : n + 1, :], 0.0).astype(bf16),
            (eye_j == 2 * WR + n).astype(bf16),
        )
    gg[...] = rows.reshape(AXIS, AXIS, NS, 128)
    g_first = [cm.to(gg.at[(y + k) % AXIS], g_one.at[k - 1], yp[k - 1]) for k in (1, 2, 3)]
    h_d.over_z()
    r_q.mid()
    r_o.last(oo.reshape(2 * SPAN, SPAN))
    h_o = RowsHome(cm, oo, o2g, o1g, ow, co)
    h_o.over_seq()
    for copy in g_first:
        copy.wait_recv()
    gg[y] = gg[y] + g_one[0] + g_one[1] + g_one[2]
    g_second = [cm.to(gg.at[y, (z + k) % AXIS], g_two.at[k - 1], zp[k - 1]) for k in (1, 2, 3)]
    l_mo.wait()
    for copy in a_m:
        copy.wait_recv()
    for t in range(NS):
        gwg_o[:, t * FFS : t * FFS + FFS] = mr[t, :, 0:FFS].astype(f32)
        gwu_o[:, t * FFS : t * FFS + FFS] = mr[t, :, FFS : 2 * FFS].astype(f32)
    h_d.over_y()
    h_o.over_z()
    for copy in g_second:
        copy.wait_recv()
    g_all[s] = gg[y, z] + g_two[0] + g_two[1] + g_two[2]
    g_third = [cm.to(g_all.at[s], g_all.at[s], p) for _, _, p in peers]
    r_q.last(qo.reshape(NS * WR, QKV))
    a_q = [cm.to(qo.at[peer_index(x, c, k, j)], qr.at[s], p) for k, j, p in peers]
    l_qo = cm.here(qo.at[s], qr.at[s])
    h_d.wait()
    gwd_o[...] = dw[...].astype(f32)
    h_o.over_y()
    rs2.arrive()

    def out_rows(i, _):
        cut = pl.ds(i * 32, 32)
        block_o[cut, :] = (x1_v[cut, :] + rs2.rows(cut)).astype(bf16)
        return 0

    lax.fori_loop(0, SPAN // 32, out_rows, 0)
    for copy in g_third:
        copy.wait_recv()
    total = g_all[0]
    for t in range(1, NS):
        total = total + g_all[t]
    g_sum[...] = total
    gg_o[...] = jnp.broadcast_to(g_sum[pl.ds(s, 1), :], (8, 128))
    h_o.wait()
    gwo_o[...] = ow[...].astype(f32)
    l_qo.wait()
    for copy in a_q:
        copy.wait_recv()
    for t in range(NS):
        gwq_o[:, t * 256 : t * 256 + 256] = qr[t, :, 0:256].astype(f32)
        gwk_o[:, t * 128 : t * 128 + 128] = qr[t, :, 256:384].astype(f32)
        gwv_o[:, t * 128 : t * 128 + 128] = qr[t, :, 384:512].astype(f32)
    rs.finish()
    rs2.finish()
    cm.finish()


def back(*args):
    any_, vm = pl.BlockSpec(memory_space=pl.ANY), pl.BlockSpec(memory_space=pltpu.VMEM)
    sds = jax.ShapeDtypeStruct
    vmem = pltpu.VMEM
    n_copies, n_local = 128, 48
    return pl.pallas_call(
        back_kernel,
        name="attn_backward",
        out_shape=[
            sds((SPAN, WIDTH), f32), sds((SPAN, WIDTH), bf16),
            sds((WR, 2048), f32), sds((WR, 1024), f32), sds((WR, 1024), f32), sds((WR, WIDTH), f32),
            sds((WR, NS * FFS), f32), sds((WR, NS * FFS), f32), sds((FR, WIDTH), f32),
            sds((8, 128), f32),
        ],
        in_specs=[any_] * 15 + [vm] * (len(args) - 15),
        out_specs=[vm] * 10,
        scratch_shapes=[
            vmem((8, SPAN, WIDTH), bf16), vmem((2, 8, SPAN, 256), bf16),
            vmem((4, 4, 128, QKV), bf16), vmem((256, WIDTH), bf16),
            vmem((8, 2 * SPAN, LENGTH), bf16), vmem((8, 2 * SPAN, 128), bf16),
            vmem((LENGTH, 128), f32), vmem((LENGTH, 128), f32), vmem((LENGTH, QKV), bf16),
            vmem((8, 128), f32),
            *scatter_scratch(), vmem((4, SPAN, WIDTH), bf16), *scatter_scratch()[1:],
            *dp_scatter_scratch(64, 2 * FFS), *dp_scatter_scratch(SPAN, 128),
            *dp_scatter_scratch(64, QKV), vmem((2, 3, FFS // 2, 128), bf16),
            vmem((NS, WR, 2 * FFS), bf16), vmem((NS, WR, 2 * FFS), bf16),
            vmem((NS, WR, QKV), bf16), vmem((NS, WR, QKV), bf16),
            vmem((4, 4, 256, 128), bf16), vmem((4, 4, SPAN, QKV), bf16),
            vmem((2, NS, WR, 128), bf16), vmem((4, 4, WR, 128), bf16), vmem((4, WR, 512), bf16),
            vmem((WR, WIDTH), bf16),
            vmem((2, NS, FR, 128), bf16), vmem((4, 4, FR, 128), bf16), vmem((4, FR, 512), bf16),
            vmem((FR, WIDTH), bf16),
            vmem((4, 4, NS, 128), f32), vmem((3, 4, NS, 128), f32), vmem((3, NS, 128), f32),
            vmem((NS, NS, 128), f32), vmem((NS, 128), f32),
            vmem((2, 4, FFS // 2, 128), bf16), vmem((SPAN, WIDTH), bf16), vmem((SPAN, WIDTH), f32),
            vmem((LENGTH, 384), f32), vmem((8, 2 * SPAN, 128), bf16),
            vmem((LENGTH, 128), bf16), vmem((LENGTH, 128), bf16), vmem((LENGTH, 256), bf16),
            pltpu.SemaphoreType.DMA((n_copies,)),
            pltpu.SemaphoreType.DMA((n_copies,)),
            pltpu.SemaphoreType.DMA((n_local,)),
        ],
        compiler_params=pltpu.CompilerParams(
            collective_id=2, has_side_effects=True, vmem_limit_bytes=VMEM_LIMIT
        ),
    )(*args)


def hand_over_kernel(*refs):
    n = len(refs) // 2
    sems = refs[-1]
    copies = [pltpu.make_async_copy(refs[i], refs[n + i], sems.at[i]) for i in range(n)]
    for copy in copies:
        copy.start()
    for copy in copies:
        copy.wait()


def hand_over(*arrays):
    any_ = pl.BlockSpec(memory_space=pl.ANY)
    return pl.pallas_call(
        hand_over_kernel,
        name="hand_over",
        out_shape=[jax.ShapeDtypeStruct(a.shape, a.dtype) for a in arrays],
        in_specs=[pl.BlockSpec(memory_space=pltpu.VMEM)] * len(arrays),
        out_specs=[any_] * len(arrays),
        scratch_shapes=[pltpu.SemaphoreType.DMA((len(arrays),))],
    )(*arrays)


def shards(
    tokens, gain_attn, w_query, key_weight, value_weight, w_out, gain_query,
    key_norm_gain, gain_mlp, w_gate, w_up, w_down, cotangent,
):
    extra = jnp.stack(
        [
            gain_attn,
            gain_mlp,
            jnp.broadcast_to(gain_query, (WR,)),
            jnp.broadcast_to(key_norm_gain, (WR,)),
        ],
        axis=1,
    )
    extra = jnp.pad(extra, ((0, 0), (0, GCOL - 4)))
    table = rope_constants()
    (x1, dx1, dab, gain2, h1, pre, qb, kb, vb, ob, gains, gq, wo, ggu, pd, dacc) = front(
        tokens[0], cotangent[0], extra, w_query, key_weight, value_weight, w_out, w_gate, w_up,
        w_down, table,
    )
    gt, block, g_q, g_k, g_v, g_out, g_gate, g_up, g_down, gg = back(
        dab, pd, ggu, h1, gq, wo, dacc, dx1, tokens[0], x1, pre, qb, kb, vb, ob, gain2, gains, table,
    )
    block, gt, g_q, g_k, g_v, g_out, g_gate, g_up, g_down = hand_over(
        block, gt, g_q, g_k, g_v, g_out, g_gate, g_up, g_down
    )
    gg = gg[0]
    return (
        block[None], gt[None], gg[:WR], g_q, g_k, g_v, g_out,
        gg[2 * WR : 2 * WR + 1], gg[2 * WR + 1 : 2 * WR + 2], gg[WR : 2 * WR],
        g_gate, g_up, g_down,
    )


def solution(mesh):
    both = P(("dp", "seq"))
    rows = P(("dp", "seq"), None)
    act = P("dp", "seq", None)
    in_specs = (act, both, rows, rows, rows, rows, both, both, both, rows, rows, rows, act)
    out_specs = (act, act, both, rows, rows, rows, rows, both, both, both, rows, rows, rows)
    return jax.shard_map(
        shards, mesh=mesh, in_specs=in_specs, out_specs=out_specs, check_vma=False
    )
```

```python
import functools
import math

import jax
import jax.numpy as jnp
import numpy as np
from jax import lax
from jax.experimental import pallas as pl
from jax.experimental.pallas import tpu as pltpu
from jax.sharding import PartitionSpec as P

QUERY_HEADS = 16
KEY_VALUE_HEADS = 8
HEAD_DIM = 128

eps_norm = 1e-06
rope_base = 1000000.0
score_scale = 1.0 / math.sqrt(HEAD_DIM)

f32 = jnp.float32
bf16 = jnp.bfloat16

AXIS = 4
ND, NS = 16, 8
SPAN = 128
WIDTH = 2048
LENGTH = SPAN * NS
WR = 16
FR = 48
FFS = ND * FR
QKV = 512
GCOL = 128
VMEM_LIMIT = 60 * 2**20
MESH = pl.DeviceIdType.MESH


def dot(a, b):
    return jnp.dot(a, b, preferred_element_type=f32)


def dot_tn(a, b):
    return lax.dot_general(a, b, (((0,), (0,)), ((), ())), preferred_element_type=f32)


def dot_nt(a, b):
    return lax.dot_general(a, b, (((1,), (1,)), ((), ())), preferred_element_type=f32)


def rms(values):
    return lax.rsqrt(jnp.mean(values * values, axis=-1, keepdims=True) + eps_norm)


def rms_back(grad_out, gain, unit, inv):
    grad_unit = grad_out * gain
    return inv * (grad_unit - unit * jnp.mean(grad_unit * unit, axis=-1, keepdims=True))


def rope_constants():
    half = HEAD_DIM // 2
    freqs = np.float32(rope_base) ** (
        -(np.arange(half, dtype=np.float32) * np.float32(2.0) / np.float32(2 * half))
    )
    angles = np.arange(LENGTH, dtype=np.float32)[:, None] * freqs.astype(np.float32)[None, :]
    cos, sin = np.cos(angles), np.sin(angles)
    return np.concatenate([cos, sin], axis=1).astype(np.float32)


def coords():
    dp, sq = lax.axis_index("dp"), lax.axis_index("seq")
    return dp // AXIS, dp % AXIS, sq // 2, sq % 2


def device(y, z, x, c):
    return (y * AXIS + z, x * 2 + c)


def seq_peers(y, z, x, c):
    return [
        (k, j, device(y, z, (x + k) % AXIS, (c + j) % 2))
        for k in range(AXIS)
        for j in range(2)
        if (k, j) != (0, 0)
    ]


def greet(peers):
    sem = pltpu.get_barrier_semaphore()
    for peer in peers:
        pl.semaphore_signal(sem, inc=1, device_id=peer, device_id_type=MESH)


def all_in(peers):
    pl.semaphore_wait(pltpu.get_barrier_semaphore(), len(peers))


def around(y, z, x, c):
    yp = [device((y + k) % AXIS, z, x, c) for k in (1, 2, 3)]
    zp = [device(y, (z + k) % AXIS, x, c) for k in (1, 2, 3)]
    return seq_peers(y, z, x, c), yp, zp


class Copies:
    def __init__(self, send, recv, local):
        self.send, self.recv, self.local = send, recv, local
        self.n, self.n_local = 0, 0
        self.sent = []

    def to(self, src, dst, dev):
        copy = pltpu.make_async_remote_copy(
            src_ref=src, dst_ref=dst, send_sem=self.send.at[self.n], recv_sem=self.recv.at[self.n],
            device_id=dev, device_id_type=MESH,
        )
        self.n += 1
        copy.start()
        self.sent.append(copy)
        return copy

    def here(self, src, dst):
        copy = pltpu.make_async_copy(src, dst, self.local.at[self.n_local])
        self.n_local += 1
        copy.start()
        return copy

    def finish(self):
        for copy in self.sent:
            copy.wait_send()
        self.sent = []

    def drain(self, copies):
        for copy in copies:
            copy.wait_send()
        done = {id(copy) for copy in copies}
        self.sent = [copy for copy in self.sent if id(copy) not in done]


class SeqGather:
    def __init__(self, cm, own, buf, co):
        self.cm, self.own, self.buf, self.co = cm, own, buf, co
        self.half = buf.shape[1] // 2

    def slot(self, k):
        y, z, x, c = self.co
        return self.buf.at[((x + k) % AXIS) * 2 + c]

    def start(self):
        y, z, x, c = self.co
        self.sib = device(y, z, x, 1 - c)
        self.plus, self.minus = device(y, z, (x + 1) % AXIS, c), device(y, z, (x + 3) % AXIS, c)
        self.a = self.cm.to(self.own, self.slot(0), self.plus)
        self.b = self.cm.to(self.own, self.slot(0), self.minus)
        self.s0 = self.cm.to(self.own, self.slot(0), self.sib)
        self.l = self.cm.here(self.own, self.slot(0))

    def forward(self):
        h = self.half
        lo, hi = pl.ds(0, h), pl.ds(h, h)
        self.a.wait_recv()
        left = self.slot(3)
        self.fa = self.cm.to(left.at[lo], left.at[lo], self.plus)
        self.s1 = self.cm.to(left, left, self.sib)
        self.b.wait_recv()
        right = self.slot(1)
        self.fb = self.cm.to(right.at[hi], right.at[hi], self.minus)
        self.s2 = self.cm.to(right, right, self.sib)

    def last(self):
        h = self.half
        lo, hi = pl.ds(0, h), pl.ds(h, h)
        opp = self.slot(2)
        self.fa.wait_recv()
        self.s3 = self.cm.to(opp.at[lo], opp.at[lo], self.sib)
        self.fb.wait_recv()
        self.s4 = self.cm.to(opp.at[hi], opp.at[hi], self.sib)

    def drain(self):
        self.cm.drain(
            [self.a, self.b, self.s0, self.fa, self.s1, self.fb, self.s2, self.s3, self.s4]
        )

    def wait_chip(self, k):
        if k == 0:
            self.l.wait()
            self.s0.wait_recv()
        elif k == 3:
            self.s1.wait_recv()
        elif k == 1:
            self.s2.wait_recv()
        else:
            self.s3.wait_recv()
            self.s4.wait_recv()


class DpGather:
    def __init__(self, cm, own, buf, co, axis):
        self.cm, self.own, self.buf, self.co, self.axis = cm, own, buf, co, axis
        n = own.shape[axis]
        self.h, self.q = n // 2, n // 4

    def part(self, ref, half, quarter=None):
        lo = half * self.h + (0 if quarter is None else quarter * self.q)
        size = self.h if quarter is None else self.q
        cut = pl.ds(lo, size)
        lead = len(ref.shape) - 2
        index = (slice(None),) * lead + ((cut, slice(None)) if self.axis == 0 else (slice(None), cut))
        return ref.at[index]

    def both(self, src_p, dst_p, src_m, dst_m, along):
        y, z, x, c = self.co
        if along == 0:
            plus, minus = device((y + 1) % AXIS, z, x, c), device((y + 3) % AXIS, z, x, c)
        else:
            plus, minus = device(y, (z + 1) % AXIS, x, c), device(y, (z + 3) % AXIS, x, c)
        return (self.cm.to(src_p, dst_p, plus), self.cm.to(src_m, dst_m, minus))

    def start(self):
        y, z, _, _ = self.co
        mine = self.buf.at[y, z]
        self.l = self.cm.here(self.own, mine)
        self.one = []
        for half in (0, 1):
            src, dst = self.part(self.own, half), self.part(mine, half)
            self.one.append(self.both(src, dst, src, dst, half))

    def spread(self):
        y, z, _, _ = self.co
        self.two = []
        for half in (0, 1):
            if half == 0:
                left, right = self.buf.at[(y + 3) % AXIS, z], self.buf.at[(y + 1) % AXIS, z]
            else:
                left, right = self.buf.at[y, (z + 3) % AXIS], self.buf.at[y, (z + 1) % AXIS]
            for copy in self.one[half]:
                copy.wait_recv()
            lp, rp = self.part(left, half, 0), self.part(right, half, 1)
            self.two.append(self.both(lp, lp, rp, rp, half))

    def line(self, half, k):
        y, z, _, _ = self.co
        if half == 0:
            return self.buf.at[:, (z + k) % AXIS]
        return self.buf.at[(y + k) % AXIS]

    def turn(self, far=False):
        y, z, xx, c = self.co
        self.l.wait()
        self.three, self.four = [], [[], []]
        for half in (0, 1):
            for copy in self.two[half]:
                copy.wait_recv()
            mine = self.part(self.line(half, 0), half)
            self.three.append(self.both(mine, mine, mine, mine, 1 - half))
            if far:
                there = device(y, (z + 2) % AXIS, xx, c) if half == 0 else device((y + 2) % AXIS, z, xx, c)
                self.four[half] = [self.cm.to(mine, mine, there), *self.three[half]]

    def last(self):
        self.four = []
        for half in (0, 1):
            for copy in self.three[half]:
                copy.wait_recv()
            lp = self.part(self.line(half, 3), half, 0)
            rp = self.part(self.line(half, 1), half, 1)
            self.four.append(self.both(lp, lp, rp, rp, 1 - half))

    def wait(self):
        for half in (0, 1):
            for copy in self.four[half]:
                copy.wait_recv()


def off(n):
    return jnp.where(n == 0, 2, jnp.where(n == 1, 1, jnp.where(n == 2, 3, 0)))


class SeqScatter:
    def __init__(self, part, sib_recv, x_recv, sems, co, kept=None):
        self.part, self.sib_recv, self.x_recv, self.sems, self.co = part, sib_recv, x_recv, sems, co
        self.kept = kept

    def ours(self, n):
        return self.part.at[2 * n + 1] if self.kept is None else self.kept.at[n]

    def sib_copy(self, n):
        y, z, x, c = self.co
        return pltpu.make_async_remote_copy(
            src_ref=self.part.at[2 * n], dst_ref=self.sib_recv.at[n],
            send_sem=self.sems.at[0, n], recv_sem=self.sems.at[1, n],
            device_id=device(y, z, x, 1 - c), device_id_type=MESH,
        )

    def x_copy(self, n):
        y, z, x, c = self.co
        return pltpu.make_async_remote_copy(
            src_ref=self.ours(n), dst_ref=self.x_recv.at[n],
            send_sem=self.sems.at[2, n], recv_sem=self.sems.at[3, n],
            device_id=device(y, z, (x + off(n)) % AXIS, c), device_id_type=MESH,
        )

    def combine(self, n, go=True):
        self.sib_copy(n).wait_recv()
        ours = self.ours(n)

        def add(i, _):
            cut = pl.ds(i * 32, 32)
            total = ours[cut, :].astype(f32) + self.sib_recv[n, cut, :].astype(f32)
            ours[cut, :] = total.astype(bf16)
            return 0

        lax.fori_loop(0, SPAN // 32, add, 0)
        if go:

            @pl.when(n < 3)
            def _():
                self.x_copy(n).start()

    def arrive(self):
        for n in range(3):
            self.x_copy(n).wait_recv()

    def rows(self, cut):
        total = self.ours(3)[cut, :].astype(f32)
        for n in range(3):
            total = total + self.x_recv[n, cut, :].astype(f32)
        return total

    def finish(self):
        for n in range(4):
            self.sib_copy(n).wait_send()
        for n in range(3):
            self.x_copy(n).wait_send()


def scatter_scratch():
    return [
        pltpu.VMEM((8, SPAN, WIDTH), bf16),
        pltpu.VMEM((4, SPAN, WIDTH), bf16),
        pltpu.VMEM((3, SPAN, WIDTH), bf16),
        pltpu.SemaphoreType.DMA((4, 4)),
    ]


def swap(u):
    return pltpu.roll(u, HEAD_DIM // 2, 1)


def rope_rows(table):
    low = lax.broadcasted_iota(jnp.int32, table.shape, 1) < HEAD_DIM // 2
    other = swap(table)
    return jnp.where(low, table, other), jnp.where(low, -other, table)


def peer_index(x, c, k, j):
    return ((x + k) % AXIS) * 2 + (c + j) % 2


class DpScatter:
    def __init__(self, cm, grad, acc, one, two, co, tile):
        self.cm, self.grad, self.acc, self.r1, self.r2 = cm, grad, acc, one, two
        self.co, self.tile = co, tile
        self.h = acc.shape[2]

    def part(self, ref, half):
        return ref.at[:, pl.ds(half * self.h, self.h)]

    def line(self, half, k):
        y, z, _, _ = self.co
        if half == 0:
            return self.part(self.grad.at[(y + k) % AXIS], half)
        return self.part(self.grad.at[:, (z + k) % AXIS], half)

    def away(self, along, k):
        y, z, x, c = self.co
        if along == 0:
            return device((y + k) % AXIS, z, x, c)
        return device(y, (z + k) % AXIS, x, c)

    def start(self):
        self.own = [self.cm.here(self.line(h, 0), self.acc.at[h]) for h in (0, 1)]
        self.first = [[], []]
        for k in (2, 1, 3):
            for h in (0, 1):
                self.first[h].append(
                    self.cm.to(self.line(h, k), self.r1.at[h, k - 1], self.away(h, k))
                )

    def add_first(self):
        rows = self.acc.shape[2]
        for h in (0, 1):
            self.own[h].wait()
            for copy in self.first[h]:
                copy.wait_recv()

            def add(t, _, h=h):
                q = t // (rows // self.tile)
                cut = pl.ds((t % (rows // self.tile)) * self.tile, self.tile)
                total = self.acc[h, q, cut, :].astype(f32)
                for k in range(3):
                    total = total + self.r1[h, k, q, cut, :].astype(f32)
                self.acc[h, q, cut, :] = total.astype(bf16)
                return 0

            lax.fori_loop(0, AXIS * (rows // self.tile), add, 0)

    def send_second(self):
        y, z, _, _ = self.co
        self.second = [[], []]
        for h in (0, 1):
            mine = z if h == 0 else y
            for k in (2, 1, 3):
                self.second[h].append(
                    self.cm.to(self.acc.at[h, (mine + k) % AXIS], self.r2.at[h, k - 1], self.away(1 - h, k))
                )

    def mid(self):
        self.add_first()
        self.send_second()

    def last(self, out):
        y, z, _, _ = self.co
        rows, cols = self.acc.shape[2:]
        for h in (0, 1):
            for copy in self.second[h]:
                copy.wait_recv()
            mine = z if h == 0 else y

            def add(t, _, h=h, mine=mine):
                cut = pl.ds(t * self.tile, self.tile)
                total = self.acc[h, mine, cut, :].astype(f32)
                for k in range(3):
                    total = total + self.r2[h, k, cut, :].astype(f32)
                out[pl.ds(h * self.h + t * self.tile, self.tile), :] = total.astype(out.dtype)
                return 0

            lax.fori_loop(0, rows // self.tile, add, 0)


def dp_scatter_scratch(rows, cols):
    return [
        pltpu.VMEM((2, AXIS, rows, cols), bf16),
        pltpu.VMEM((2, 3, AXIS, rows, cols), bf16),
        pltpu.VMEM((2, 3, rows, cols), bf16),
    ]


def front_kernel(
    tok, cot, extra, w_query, w_key, w_value, w_out, w_gate, w_up, w_down, table,
    x1_o, dx1_o, dab_o, gain2_o, h1_o, pre_o, qb_o, kb_o, vb_o, ob_o, gains, gq_o, wo_o, ggu_o, pd_o, dacc_o,
    xg, pq, pm, wod, a2a_q, a2a_m, wq, wo_b, wo_v, wd_b, wd_v, wgu, o1, o2, o3o, o3d, h2_loc,
    dy_v, hid, dgu, pdv, d_one, x1_v, pre, qb, kb, vb, ob, d_acc,
    part, sib_recv, x_recv, rs_sems, rs_sems2, send, recv, local,
):
    co = y, z, x, c = coords()
    s = x * 2 + c
    peers, yp, zp = around(*co)
    everyone = [p for _, _, p in peers] + yp + zp
    greet(everyone)
    cm = Copies(send, recv, local)
    for t in range(NS):
        pq[t, :, 0:256] = w_query[:, t * 256 : t * 256 + 256]
        pq[t, :, 256:384] = w_key[:, t * 128 : t * 128 + 128]
        pq[t, :, 384:512] = w_value[:, t * 128 : t * 128 + 128]
        pq[t, :, 512:640] = extra[...]
    all_in(everyone)

    aq = [cm.to(pq.at[peer_index(x, c, k, j)], a2a_q.at[s], p) for k, j, p in peers]
    lq = cm.here(pq.at[s], a2a_q.at[s])
    g_tok = SeqGather(cm, tok, xg, co)
    g_tok.start()
    for t in range(NS):
        pm[t, :, 0:FFS] = w_gate[:, t * FFS : t * FFS + FFS]
        pm[t, :, FFS : 2 * FFS] = w_up[:, t * FFS : t * FFS + FFS]
    wod[0:WR, :] = w_out[...]
    wod[WR : WR + FR, :] = w_down[...]

    def quarter(i):
        return pl.ds(pl.multiple_of(i * 512, 512), 512)

    def chunk(i):
        return pl.ds(pl.multiple_of(i * 128, 128), 128)

    o_one = [cm.to(wod.at[:, quarter((y + k) % AXIS)], o1.at[y], yp[k - 1]) for k in (1, 2, 3)]
    l_one = cm.here(wod.at[:, quarter(y)], o1.at[y])
    am = [cm.to(pm.at[peer_index(x, c, k, j)], a2a_m.at[s], p) for k, j, p in peers]
    lm = cm.here(pm.at[s], a2a_m.at[s])
    lq.wait()
    for copy in aq:
        copy.wait_recv()
    g_q = DpGather(cm, a2a_q.reshape(NS * WR, QKV + GCOL), wq, co, 0)
    g_q.start()
    l_one.wait()
    for copy in o_one:
        copy.wait_recv()
    o_two = [cm.to(o1.at[:, :, chunk((z + k) % AXIS)], o2.at[z], zp[k - 1]) for k in (1, 2, 3)]
    l_two = cm.here(o1.at[:, :, chunk(z)], o2.at[z])
    g_q.spread()
    l_two.wait()
    for copy in o_two:
        copy.wait_recv()

    def rows_of(t, lo, n):
        return o2.at[pl.ds((t % 2) * 2, 2), t // 2, pl.ds(lo, n)]

    o_three = []
    for k, j, p in peers:
        t = peer_index(x, c, k, j)
        o_three.append(cm.to(rows_of(t, 0, WR), o3o.at[:, s], p))
        o_three.append(cm.to(rows_of(t, WR, FR), o3d.at[:, s], p))
    l_three = [
        cm.here(rows_of(s, 0, WR), o3o.at[:, s]),
        cm.here(rows_of(s, WR, FR), o3d.at[:, s]),
    ]
    g_q.turn()
    g_tok.forward()
    g_q.last()
    lm.wait()
    for copy in am:
        copy.wait_recv()
    g_m = DpGather(cm, a2a_m.reshape(NS * WR, 2 * FFS), wgu, co, 0)
    g_m.start()
    for copy in l_three:
        copy.wait()
    for copy in o_three:
        copy.wait_recv()
    g_o = DpGather(cm, o3o.reshape(2 * SPAN, SPAN), wo_b, co, 0)
    g_o.start()
    g_d = DpGather(cm, o3d.reshape(FFS, SPAN), wd_b, co, 0)
    g_d.start()
    g_m.spread()
    g_o.spread()
    g_d.spread()
    g_o.turn(True)
    g_m.turn()
    g_d.turn()
    g_q.wait()
    wq_out = cm.here(wq.at[:, :, :, pl.ds(0, QKV)], gq_o)

    wq2 = wq.reshape(WIDTH, QKV + GCOL)
    gcols = wq2[:, QKV:]
    flat = gcols.astype(f32).T
    gains[...] = flat[:8]
    gain_one = flat[0:1]
    rows = lax.broadcasted_iota(jnp.int32, (WIDTH, HEAD_DIM), 0)
    cols = lax.broadcasted_iota(jnp.int32, (WIDTH, HEAD_DIM), 1)
    pick = (rows == cols * WR).astype(bf16)
    head_gains = dot(flat[:8].astype(bf16), pick)
    gain_q, gain_k = head_gains[2:3], head_gains[3:4]
    gains[2:4, 0:HEAD_DIM] = head_gains[2:4]

    def normed(i, _):
        cut = pl.ds((i % 4) * 32, 32)
        v = xg[i // 4, cut, :].astype(f32)
        part[i // 4, cut, :] = (v * rms(v) * gain_one).astype(bf16)
        return 0

    g_tok.last()
    g_cot = SeqGather(cm, cot, dy_v, co)
    g_cot.start()
    for k in (0, 1, 3, 2):
        g_tok.wait_chip(k)
    lax.fori_loop(0, LENGTH // 32, normed, 0)
    h1_copy = cm.here(part, h1_o)

    def project(i, _):
        h = part[pl.ds(2 * i, 2)].reshape(2 * SPAN, WIDTH)
        p = dot(h, wq2[:, :QKV])
        cut = pl.ds(pl.multiple_of(i * 256, 256), 256)
        pre[cut, :] = p[:, :384]
        vb[cut, :] = p[:, 384:].astype(bf16)
        co_t, si_t = rope_rows(table[cut, :])
        for h_i in range(2):
            u = p[:, h_i * 128 : h_i * 128 + 128]
            u = u * rms(u) * gain_q
            u = (u * co_t + swap(u) * si_t).astype(bf16)
            qb[pl.ds(2 * i, 2), pl.ds(h_i * SPAN, SPAN), :] = u.reshape(2, SPAN, HEAD_DIM)
        u = p[:, 256:384]
        u = u * rms(u) * gain_k
        kb[cut, :] = (u * co_t + swap(u) * si_t).astype(bf16)
        return 0

    lax.fori_loop(0, 4, project, 0)
    outs = [cm.here(pre, pre_o), cm.here(qb, qb_o), cm.here(kb, kb_o), cm.here(vb, vb_o)]
    h1_copy.wait()
    g_tok.drain()
    g_o.wait()
    wo_copy = [
        cm.here(wo_b.at[yy, zz], wo_v.at[:, pl.ds((yy * AXIS + zz) * 128, 128)])
        for yy in range(AXIS)
        for zz in range(AXIS)
    ]
    for copy in wo_copy:
        copy.wait()
    wo_out = cm.here(wo_v, wo_o)
    g_cot.forward()

    rs = SeqScatter(part, sib_recv, x_recv, rs_sems, co)

    def attend(i, slot):
        sc = dot_nt(qb[i], kb[...]) * score_scale
        r = lax.broadcasted_iota(jnp.int32, (2 * SPAN, LENGTH), 0) % SPAN + i * SPAN
        k = lax.broadcasted_iota(jnp.int32, (2 * SPAN, LENGTH), 1)
        sc = jnp.where(k <= r, sc, -1e30)
        top = jnp.max(sc, axis=-1, keepdims=True)
        ex = jnp.exp(sc - top)
        tot = jnp.sum(ex, axis=-1, keepdims=True)
        pb = (ex / tot).astype(bf16)
        o = dot(pb, vb[...]).astype(bf16)
        o = jnp.concatenate([o[:SPAN], o[SPAN:]], axis=1)
        ob[pl.ds(pl.multiple_of(i * SPAN, SPAN), SPAN), :] = o
        part[slot] = dot(o, wo_v[...]).astype(bf16)

    def pair(n, _):
        chip = (x + off(n)) % AXIS
        attend(chip * 2 + 1 - c, 2 * n)
        rs.sib_copy(n).start()

        @pl.when(n > 0)
        def _():
            rs.combine(n - 1)

        attend(chip * 2 + c, 2 * n + 1)
        return 0

    lax.fori_loop(0, 4, pair, 0)
    rs.combine(3)
    g_cot.last()
    g_m.last()
    g_d.last()
    rs.arrive()

    def residual(i, _):
        cut = pl.ds(i * 32, 32)
        v = xg[s, cut, :].astype(f32) + rs.rows(cut)
        x1_v[cut, :] = v
        h2_loc[cut, :] = (v * rms(v) * gains[1:2, :]).astype(bf16)
        return 0

    lax.fori_loop(0, SPAN // 32, residual, 0)
    rs.finish()
    outs += [cm.here(x1_v, x1_o), cm.here(ob, ob_o)]

    g_h2 = SeqGather(cm, h2_loc, xg, co)
    g_h2.start()
    g_d.wait()
    wd_copy = [
        cm.here(wd_b.at[yy, zz], wd_v.at[:, pl.ds((yy * AXIS + zz) * 128, 128)])
        for yy in range(AXIS)
        for zz in range(AXIS)
    ]
    g_m.wait()
    for copy in wd_copy:
        copy.wait()
    rs = SeqScatter(part, sib_recv, x_recv, rs_sems2, co)
    wgu2 = wgu.reshape(WIDTH, 2 * FFS)
    order = {2: 0, 1: 1, 3: 2, 0: 3}

    def chip_of(k):
        return (x + k) % AXIS

    def forward(k):
        chip = chip_of(k)
        rows = pl.ds(pl.multiple_of(chip * 256, 256), 256)
        two = pl.ds(2 * chip, 2)

        def tile(f, _):
            lo = pl.multiple_of(f * 256, 256)
            h = xg[two].reshape(256, WIDTH)
            gate = dot(h, wgu2[:, pl.ds(lo, 256)])
            up = dot(h, wgu2[:, pl.ds(pl.multiple_of(lo + FFS, 256), 256)])
            dh = dot_nt(dy_v[two].reshape(256, WIDTH), wd_v[pl.ds(lo, 256), :])
            sig = jax.nn.sigmoid(gate)
            silu = gate * sig
            hid[rows, pl.ds(lo, 256)] = (silu * up).astype(bf16)
            dgate = dh * up * (sig * (1.0 + gate * (1.0 - sig)))
            dgu[rows, pl.ds(lo, 256)] = dgate.astype(bf16)
            dgu[rows, pl.ds(pl.multiple_of(lo + FFS, 256), 256)] = (dh * silu).astype(bf16)
            return 0

        lax.fori_loop(0, FFS // 256, tile, 0)

    def put(ref, n, cols, o):
        ref[2 * n + 1 - c, :, cols] = o[:SPAN]
        ref[2 * n + c, :, cols] = o[SPAN:]

    def back(k):
        n = order[k]
        rows = pl.ds(pl.multiple_of(chip_of(k) * 256, 256), 256)

        def tile(m, _):
            cols = pl.ds(pl.multiple_of(m * 256, 256), 256)
            put(part, n, cols, dot_nt(dgu[rows, :], wgu2[cols, :]).astype(bf16))
            return 0

        lax.fori_loop(0, WIDTH // 256, tile, 0)
        rs.sib_copy(n).start()

    g_h2.wait_chip(0)
    g_cot.wait_chip(0)
    forward(0)
    g_h2.forward()
    back(0)
    g_h2.wait_chip(3)
    g_cot.wait_chip(3)
    forward(3)
    g_h2.last()
    back(3)
    g_h2.wait_chip(1)
    g_cot.wait_chip(1)
    forward(1)
    rs.combine(order[3])
    back(1)
    g_h2.wait_chip(2)
    g_cot.wait_chip(2)
    forward(2)
    rs.combine(order[1])
    cm.finish()

    def down_grad(m, _):
        cut = pl.ds(pl.multiple_of(m * 256, 256), 256)
        o = dot_tn(hid[:, cut], dy_v[...].reshape(LENGTH, WIDTH)).astype(bf16)
        for yy in range(AXIS):
            for zz in range(AXIS):
                lo = (yy * AXIS + zz) * 128
                wd_b[yy, zz, cut, :] = o[:, lo : lo + 128]
        return 0

    lax.fori_loop(0, FFS // 256, down_grad, 0)
    r_d = DpScatter(cm, wd_b, d_acc, d_one, None, co, 128)
    r_d.start()
    back(2)
    rs.combine(order[0])

    for k in (0, 3, 1, 2):
        n = order[k]
        rows = pl.ds(pl.multiple_of(chip_of(k) * 256, 256), 256)

        def down(m, _):
            cols = pl.ds(pl.multiple_of(m * 512, 512), 512)
            put(pdv, n, cols, dot(hid[rows, :], wd_v[:, cols]).astype(bf16))
            return 0

        lax.fori_loop(0, WIDTH // 512, down, 0)
        if k == 3:
            rs.combine(order[2])
    outs.append(cm.here(pdv, pd_o))

    def gate_up(m, _):
        cols = pl.ds(pl.multiple_of(m * 256, 256), 256)
        wgu2[cols, :] = dot_tn(xg[:, :, cols].reshape(LENGTH, 256), dgu[...]).astype(bf16)
        return 0

    lax.fori_loop(0, WIDTH // 256, gate_up, 0)
    outs.append(cm.here(wgu, ggu_o))
    rs.arrive()
    gain_two = gains[1:2, :]

    def mlp_back(i, acc):
        cut = pl.ds(i * 32, 32)
        v = x1_v[cut, :]
        inv = rms(v)
        unit = v * inv
        dh2 = rs.rows(cut)
        dx1 = dy_v[s, cut, :].astype(f32) + rms_back(dh2, gain_two, unit, inv)
        dx1_o[cut, :] = dx1
        dab_o[cut, :] = dx1.astype(bf16)
        return acc + jnp.sum(dh2 * unit, axis=0, keepdims=True)

    acc = lax.fori_loop(0, SPAN // 32, mlp_back, jnp.zeros((1, WIDTH), f32))
    gain2_o[...] = jnp.broadcast_to(acc, (8, WIDTH))
    r_d.add_first()
    outs.append(cm.here(d_acc, dacc_o))
    rs.finish()
    wo_out.wait()
    wq_out.wait()
    for copy in outs:
        copy.wait()
    cm.finish()


def front(*args):
    any_, vm = pl.BlockSpec(memory_space=pl.ANY), pl.BlockSpec(memory_space=pltpu.VMEM)
    sds = jax.ShapeDtypeStruct
    vmem = pltpu.VMEM
    n_copies, n_local = 160, 72
    return pl.pallas_call(
        front_kernel,
        name="attn_forward",
        out_shape=[
            sds((SPAN, WIDTH), f32), sds((SPAN, WIDTH), f32), sds((SPAN, WIDTH), bf16),
            sds((8, WIDTH), f32), sds((8, SPAN, WIDTH), bf16), sds((LENGTH, 384), f32),
            sds((8, 2 * SPAN, 128), bf16), sds((LENGTH, 128), bf16), sds((LENGTH, 128), bf16),
            sds((LENGTH, 256), bf16), sds((8, WIDTH), f32), sds((4, 4, 128, QKV), bf16),
            sds((256, WIDTH), bf16), sds((4, 4, 128, 2 * FFS), bf16), sds((8, SPAN, WIDTH), bf16),
            sds((2, 4, FFS // 2, 128), bf16),
        ],
        in_specs=[any_] * 2 + [vm] * 9,
        out_specs=[any_, vm, vm, vm, any_, any_, any_, any_, any_, any_, vm, any_, any_, any_, any_, any_],
        scratch_shapes=[
            vmem((8, SPAN, WIDTH), bf16),
            vmem((NS, WR, QKV + GCOL), bf16), vmem((NS, WR, 2 * FFS), bf16),
            vmem((WR + FR, WIDTH), bf16),
            vmem((NS, WR, QKV + GCOL), bf16), vmem((NS, WR, 2 * FFS), bf16),
            vmem((4, 4, 128, QKV + GCOL), bf16),
            vmem((4, 4, 256, 128), bf16), vmem((256, WIDTH), bf16),
            vmem((4, 4, FFS, 128), bf16), vmem((FFS, WIDTH), bf16),
            vmem((4, 4, 128, 2 * FFS), bf16),
            vmem((4, WR + FR, 512), bf16), vmem((4, 4, WR + FR, 128), bf16),
            vmem((2, NS, WR, 128), bf16), vmem((2, NS, FR, 128), bf16),
            vmem((SPAN, WIDTH), bf16),
            vmem((8, SPAN, WIDTH), bf16), vmem((LENGTH, FFS), bf16), vmem((LENGTH, 2 * FFS), bf16),
            vmem((8, SPAN, WIDTH), bf16), vmem((2, 3, AXIS, FFS // 2, 128), bf16),
            vmem((SPAN, WIDTH), f32), vmem((LENGTH, 384), f32), vmem((8, 2 * SPAN, 128), bf16),
            vmem((LENGTH, 128), bf16), vmem((LENGTH, 128), bf16), vmem((LENGTH, 256), bf16),
            vmem((2, 4, FFS // 2, 128), bf16),
            *scatter_scratch(),
            pltpu.SemaphoreType.DMA((4, 4)),
            pltpu.SemaphoreType.DMA((n_copies,)),
            pltpu.SemaphoreType.DMA((n_copies,)),
            pltpu.SemaphoreType.DMA((n_local,)),
        ],
        compiler_params=pltpu.CompilerParams(
            collective_id=1, has_side_effects=True, vmem_limit_bytes=VMEM_LIMIT
        ),
    )(*args)


class RowsHome:
    def __init__(self, cm, res, r2, r1, out, co):
        self.cm, self.res, self.r2, self.r1, self.out, self.co = cm, res, r2, r1, out, co
        self.peers, self.yp, self.zp = around(*co)

    def step(self, sends, here):
        self.wait()
        self.arriving = [self.cm.to(*a) for a in sends]
        self.local = self.cm.here(*here)

    def wait(self):
        if hasattr(self, "arriving"):
            self.local.wait()
            for copy in self.arriving:
                copy.wait_recv()

    def over_seq(self):
        y, z, x, c = self.co
        s = x * 2 + c
        dst = self.r2.at[pl.ds((s % 2) * 2, 2), s // 2]
        self.step(
            [(self.res.at[:, peer_index(x, c, k, j)], dst, p) for k, j, p in self.peers],
            (self.res.at[:, s], dst),
        )

    def over_z(self):
        y, z, x, c = self.co
        dst = self.r1.at[:, :, pl.ds(pl.multiple_of(z * 128, 128), 128)]
        self.step(
            [(self.r2.at[(z + k) % AXIS], dst, self.zp[k - 1]) for k in (1, 2, 3)],
            (self.r2.at[z], dst),
        )

    def over_y(self):
        y, z, x, c = self.co
        dst = self.out.at[:, pl.ds(pl.multiple_of(y * 512, 512), 512)]
        self.step(
            [(self.r1.at[(y + k) % AXIS], dst, self.yp[k - 1]) for k in (1, 2, 3)],
            (self.r1.at[y], dst),
        )


def back_kernel(
    dab_loc, pd, ggu, h1, gq, wo, dacc, dx1, tok, x1, pre_i, qb_i, kb_i, vb_i, ob_i,
    gain2, gains, table,
    gt_o, block_o, gwq_o, gwk_o, gwv_o, gwo_o, gwg_o, gwu_o, gwd_o, gg_o,
    dab, h1_v, wq, wo_v, pbuf, dob, dk, dv, dqkv, gacc,
    part, sib_recv, x_recv, rs_sems, kept, sib2, x2, rs2_sems,
    m_acc, m_one, m_two, o_acc, o_one, o_two, q_acc, q_one, q_two, d_two,
    mo, mr, qo, qr, go, gqk, oo, o2g, o1g, ow, od, d2g, d1g, dw,
    gg, g_one, g_two, g_all, g_sum, d_acc, tok_v, x1_v, pre, qb, kb, vb, ob,
    send, recv, local,
):
    co = y, z, x, c = coords()
    s = x * 2 + c
    peers, yp, zp = around(*co)
    everyone = [p for _, _, p in peers] + yp + zp
    greet(everyone)
    cm = Copies(send, recv, local)
    l_qk = [cm.here(qb_i, qb), cm.here(kb_i, kb)]
    l_pd = [cm.here(pd.at[2 * n + 1], kept.at[n]) for n in range(4)]
    l_wo = cm.here(wo, wo_v)
    l_wq = cm.here(gq, wq)

    def h1_load(m):
        return cm.here(h1.at[:, :, pl.ds(m * 256, 256)], h1_v.at[m % 2])

    l_h1 = [h1_load(0), h1_load(1)]
    l_in = [
        cm.here(vb_i, vb), cm.here(ob_i, ob), cm.here(pre_i, pre), cm.here(dacc, d_acc),
        cm.here(dx1, gt_o), cm.here(tok, tok_v), cm.here(x1, x1_v),
    ]
    all_in(everyone)
    g_dab = SeqGather(cm, dab_loc, dab, co)
    g_dab.start()
    r_d = DpScatter(cm, None, d_acc, None, d_two, co, 128)
    l_in[3].wait()
    r_d.send_second()
    r_m = DpScatter(cm, ggu, m_acc, m_one, m_two, co, 16)
    r_m.start()
    rs2 = SeqScatter(pd, sib2, x2, rs2_sems, co, kept)
    for n in range(4):
        l_pd[n].wait()
        rs2.sib_copy(n).start()

    def probs(i, _):
        sc = dot_nt(qb[i], kb[...]) * score_scale
        r = lax.broadcasted_iota(jnp.int32, (2 * SPAN, LENGTH), 0) % SPAN + i * SPAN
        k = lax.broadcasted_iota(jnp.int32, (2 * SPAN, LENGTH), 1)
        sc = jnp.where(k <= r, sc, -1e30)
        ex = jnp.exp(sc - jnp.max(sc, axis=-1, keepdims=True))
        pbuf[i] = (ex / jnp.sum(ex, axis=-1, keepdims=True)).astype(bf16)
        return 0

    for copy in l_qk:
        copy.wait()
    lax.fori_loop(0, 4, probs, 0)
    g_dab.forward()
    lax.fori_loop(4, 8, probs, 0)
    dk[...] = jnp.zeros_like(dk)
    dv[...] = jnp.zeros_like(dv)
    gacc[...] = jnp.zeros_like(gacc)
    for n in (0, 1, 2, 4, 5, 6):
        l_in[n].wait()
    l_wo.wait()

    def out_back(k):
        g_dab.wait_chip(k)
        two = pl.ds(2 * ((x + k) % AXIS), 2)
        o = dot_nt(dab[two].reshape(2 * SPAN, WIDTH), wo_v[...]).astype(bf16)
        for j in range(2):
            blk = o[j * SPAN : (j + 1) * SPAN]
            dob[2 * ((x + k) % AXIS) + j] = jnp.concatenate([blk[:, :128], blk[:, 128:]], axis=0)

    out_back(0)
    out_back(3)
    out_back(1)
    for n in range(4):
        rs2.combine(n, False)
    g_dab.last()
    for n in range(3):
        rs2.x_copy(n).start()
    out_back(2)

    def out_grad(m, _):
        cols = pl.ds(pl.multiple_of(m * 512, 512), 512)
        o = dot_tn(ob[...], dab[:, :, cols].reshape(LENGTH, 512)).astype(bf16)
        for j in range(AXIS):
            go[m, j] = o[:, j * 128 : j * 128 + 128]
        return 0

    lax.fori_loop(0, AXIS, out_grad, 0)
    r_o = DpScatter(cm, go, o_acc, o_one, o_two, co, 128)
    r_o.start()

    rs = SeqScatter(part, sib_recv, x_recv, rs_sems, co)
    l_wq.wait()
    wq2 = wq.reshape(WIDTH, QKV)
    gain_q, gain_k = gains[2:3, 0:128], gains[3:4, 0:128]

    def head_back(g, u, gain, co_t, si_t):
        g = g * co_t - swap(g) * si_t
        inv = rms(u)
        unit = u * inv
        return rms_back(g, gain, unit, inv), jnp.sum(g * unit, axis=0, keepdims=True)

    def slot_of(chip):
        k = (chip - x + AXIS) % AXIS
        return jnp.where(k == 2, 0, jnp.where(k == 1, 1, jnp.where(k == 3, 2, 3)))

    def chip_back(t, _):
        chip = 3 - t

        def block(j, _):
            i = chip * 2 + 1 - j
            q, do, p = qb[i], dob[i], pbuf[i]
            dp = dot_nt(do, vb[...])
            pf = p.astype(f32)
            delta = jnp.sum(pf * dp, axis=-1, keepdims=True)
            ds = (pf * (dp - delta)).astype(bf16)
            dk[...] += dot_tn(ds, q)
            dv[...] += dot_tn(p, do)
            dq = dot(ds, kb[...]) * score_scale
            cut = pl.ds(pl.multiple_of(i * SPAN, SPAN), SPAN)
            u = jnp.concatenate([pre[cut, 0:128], pre[cut, 128:256]], axis=0)
            co_t, si_t = rope_rows(table[cut, :])
            co_t = jnp.concatenate([co_t] * 2, axis=0)
            si_t = jnp.concatenate([si_t] * 2, axis=0)
            dqp, gsum = head_back(dq, u, gain_q, co_t, si_t)
            gacc[0:1, :] += gsum
            dqp = dqp.astype(bf16)
            dqkv[cut, 0:128] = dqp[:SPAN]
            dqkv[cut, 128:256] = dqp[SPAN:]
            return 0

        lax.fori_loop(0, 2, block, 0)
        cut = pl.ds(pl.multiple_of(chip * 256, 256), 256)
        co_t, si_t = rope_rows(table[cut, :])
        dkp, gsum = head_back(dk[cut, :] * score_scale, pre[cut, 256:384], gain_k, co_t, si_t)
        gacc[1:2, :] += gsum
        dqkv[cut, 256:384] = dkp.astype(bf16)
        dqkv[cut, 384:512] = dv[cut, :].astype(bf16)
        n = slot_of(chip)

        @pl.when(t % 2 == 1)
        def _():
            rs.combine(slot_of(chip + 1))

        def tile(m, _):
            cols = pl.ds(pl.multiple_of(m * 512, 512), 512)
            o = dot_nt(dqkv[cut, :], wq2[cols, :]).astype(bf16)
            part[2 * n + 1 - c, :, cols] = o[:SPAN]
            part[2 * n + c, :, cols] = o[SPAN:]
            return 0

        lax.fori_loop(0, WIDTH // 512, tile, 0)
        rs.sib_copy(n).start()
        return 0

    lax.fori_loop(0, 2, chip_back, 0)
    rs.combine(slot_of(2))
    lax.fori_loop(2, 4, chip_back, 0)
    rs.combine(slot_of(0))
    r_m.mid()

    for m in range(8):
        l_h1[m].wait()
        o = dot_tn(h1_v[m % 2].reshape(LENGTH, 256), dqkv[...]).astype(bf16)
        gqk[m // 2, 2 * (m % 2)] = o[:SPAN]
        gqk[m // 2, 2 * (m % 2) + 1] = o[SPAN:]
        if m < 6:
            l_h1.append(h1_load(m + 2))
    r_q = DpScatter(cm, gqk, q_acc, q_one, q_two, co, 64)
    r_q.start()
    r_o.mid()
    r_d.last(od.reshape(FFS, SPAN))
    h_d = RowsHome(cm, od, d2g, d1g, dw, co)
    h_d.over_seq()
    r_m.last(mo.reshape(NS * WR, 2 * FFS))
    a_m = [cm.to(mo.at[peer_index(x, c, k, j)], mr.at[s], p) for k, j, p in peers]
    l_mo = cm.here(mo.at[s], mr.at[s])

    rs.arrive()
    gain_one = gains[0:1, :]

    def input_back(i, acc):
        cut = pl.ds(i * 32, 32)
        v = tok_v[cut, :].astype(f32)
        inv = rms(v)
        unit = v * inv
        dh1 = rs.rows(cut)
        gt_o[cut, :] = gt_o[cut, :] + rms_back(dh1, gain_one, unit, inv)
        return acc + jnp.sum(dh1 * unit, axis=0, keepdims=True)

    gain1 = lax.fori_loop(0, SPAN // 32, input_back, jnp.zeros((1, WIDTH), f32))

    dev_i = lax.broadcasted_iota(jnp.int32, (ND * NS, WIDTH), 0)
    col_j = lax.broadcasted_iota(jnp.int32, (ND * NS, WIDTH), 1)
    mine = col_j // WR == dev_i
    row_j = lax.broadcasted_iota(jnp.int32, (WIDTH, 128), 0)
    lane = lax.broadcasted_iota(jnp.int32, (WIDTH, 128), 1)
    rows = jnp.zeros((ND * NS, 128), f32)
    for v, shift in ((gain1, 0), (gain2[0:1, :], WR)):
        rows = rows + dot(
            jnp.where(mine, v, 0.0).astype(bf16), (lane == row_j % WR + shift).astype(bf16)
        )
    eye_i = lax.broadcasted_iota(jnp.int32, (128, 128), 0)
    eye_j = lax.broadcasted_iota(jnp.int32, (128, 128), 1)
    for n in range(2):
        rows = rows + dot(
            jnp.where(eye_i == eye_j, gacc[n : n + 1, :], 0.0).astype(bf16),
            (eye_j == 2 * WR + n).astype(bf16),
        )
    gg[...] = rows.reshape(AXIS, AXIS, NS, 128)
    g_first = [cm.to(gg.at[(y + k) % AXIS], g_one.at[k - 1], yp[k - 1]) for k in (1, 2, 3)]
    h_d.over_z()
    r_q.mid()
    r_o.last(oo.reshape(2 * SPAN, SPAN))
    h_o = RowsHome(cm, oo, o2g, o1g, ow, co)
    h_o.over_seq()
    for copy in g_first:
        copy.wait_recv()
    gg[y] = gg[y] + g_one[0] + g_one[1] + g_one[2]
    g_second = [cm.to(gg.at[y, (z + k) % AXIS], g_two.at[k - 1], zp[k - 1]) for k in (1, 2, 3)]
    l_mo.wait()
    for copy in a_m:
        copy.wait_recv()
    for t in range(NS):
        gwg_o[:, t * FFS : t * FFS + FFS] = mr[t, :, 0:FFS].astype(f32)
        gwu_o[:, t * FFS : t * FFS + FFS] = mr[t, :, FFS : 2 * FFS].astype(f32)
    h_d.over_y()
    h_o.over_z()
    for copy in g_second:
        copy.wait_recv()
    g_all[s] = gg[y, z] + g_two[0] + g_two[1] + g_two[2]
    g_third = [cm.to(g_all.at[s], g_all.at[s], p) for _, _, p in peers]
    r_q.last(qo.reshape(NS * WR, QKV))
    a_q = [cm.to(qo.at[peer_index(x, c, k, j)], qr.at[s], p) for k, j, p in peers]
    l_qo = cm.here(qo.at[s], qr.at[s])
    h_d.wait()
    gwd_o[...] = dw[...].astype(f32)
    h_o.over_y()
    rs2.arrive()

    def out_rows(i, _):
        cut = pl.ds(i * 32, 32)
        block_o[cut, :] = (x1_v[cut, :] + rs2.rows(cut)).astype(bf16)
        return 0

    lax.fori_loop(0, SPAN // 32, out_rows, 0)
    for copy in g_third:
        copy.wait_recv()
    total = g_all[0]
    for t in range(1, NS):
        total = total + g_all[t]
    g_sum[...] = total
    gg_o[...] = jnp.broadcast_to(g_sum[pl.ds(s, 1), :], (8, 128))
    h_o.wait()
    gwo_o[...] = ow[...].astype(f32)
    l_qo.wait()
    for copy in a_q:
        copy.wait_recv()
    for t in range(NS):
        gwq_o[:, t * 256 : t * 256 + 256] = qr[t, :, 0:256].astype(f32)
        gwk_o[:, t * 128 : t * 128 + 128] = qr[t, :, 256:384].astype(f32)
        gwv_o[:, t * 128 : t * 128 + 128] = qr[t, :, 384:512].astype(f32)
    rs.finish()
    rs2.finish()
    cm.finish()


def back(*args):
    any_, vm = pl.BlockSpec(memory_space=pl.ANY), pl.BlockSpec(memory_space=pltpu.VMEM)
    sds = jax.ShapeDtypeStruct
    vmem = pltpu.VMEM
    n_copies, n_local = 128, 48
    return pl.pallas_call(
        back_kernel,
        name="attn_backward",
        out_shape=[
            sds((SPAN, WIDTH), f32), sds((SPAN, WIDTH), bf16),
            sds((WR, 2048), f32), sds((WR, 1024), f32), sds((WR, 1024), f32), sds((WR, WIDTH), f32),
            sds((WR, NS * FFS), f32), sds((WR, NS * FFS), f32), sds((FR, WIDTH), f32),
            sds((8, 128), f32),
        ],
        in_specs=[any_] * 15 + [vm] * (len(args) - 15),
        out_specs=[vm] * 10,
        scratch_shapes=[
            vmem((8, SPAN, WIDTH), bf16), vmem((2, 8, SPAN, 256), bf16),
            vmem((4, 4, 128, QKV), bf16), vmem((256, WIDTH), bf16),
            vmem((8, 2 * SPAN, LENGTH), bf16), vmem((8, 2 * SPAN, 128), bf16),
            vmem((LENGTH, 128), f32), vmem((LENGTH, 128), f32), vmem((LENGTH, QKV), bf16),
            vmem((8, 128), f32),
            *scatter_scratch(), vmem((4, SPAN, WIDTH), bf16), *scatter_scratch()[1:],
            *dp_scatter_scratch(64, 2 * FFS), *dp_scatter_scratch(SPAN, 128),
            *dp_scatter_scratch(64, QKV), vmem((2, 3, FFS // 2, 128), bf16),
            vmem((NS, WR, 2 * FFS), bf16), vmem((NS, WR, 2 * FFS), bf16),
            vmem((NS, WR, QKV), bf16), vmem((NS, WR, QKV), bf16),
            vmem((4, 4, 256, 128), bf16), vmem((4, 4, SPAN, QKV), bf16),
            vmem((2, NS, WR, 128), bf16), vmem((4, 4, WR, 128), bf16), vmem((4, WR, 512), bf16),
            vmem((WR, WIDTH), bf16),
            vmem((2, NS, FR, 128), bf16), vmem((4, 4, FR, 128), bf16), vmem((4, FR, 512), bf16),
            vmem((FR, WIDTH), bf16),
            vmem((4, 4, NS, 128), f32), vmem((3, 4, NS, 128), f32), vmem((3, NS, 128), f32),
            vmem((NS, NS, 128), f32), vmem((NS, 128), f32),
            vmem((2, 4, FFS // 2, 128), bf16), vmem((SPAN, WIDTH), bf16), vmem((SPAN, WIDTH), f32),
            vmem((LENGTH, 384), f32), vmem((8, 2 * SPAN, 128), bf16),
            vmem((LENGTH, 128), bf16), vmem((LENGTH, 128), bf16), vmem((LENGTH, 256), bf16),
            pltpu.SemaphoreType.DMA((n_copies,)),
            pltpu.SemaphoreType.DMA((n_copies,)),
            pltpu.SemaphoreType.DMA((n_local,)),
        ],
        compiler_params=pltpu.CompilerParams(
            collective_id=2, has_side_effects=True, vmem_limit_bytes=VMEM_LIMIT
        ),
    )(*args)


def hand_over_kernel(*refs):
    n = len(refs) // 2
    sems = refs[-1]
    copies = [pltpu.make_async_copy(refs[i], refs[n + i], sems.at[i]) for i in range(n)]
    for copy in copies:
        copy.start()
    for copy in copies:
        copy.wait()


def hand_over(*arrays):
    any_ = pl.BlockSpec(memory_space=pl.ANY)
    return pl.pallas_call(
        hand_over_kernel,
        name="hand_over",
        out_shape=[jax.ShapeDtypeStruct(a.shape, a.dtype) for a in arrays],
        in_specs=[pl.BlockSpec(memory_space=pltpu.VMEM)] * len(arrays),
        out_specs=[any_] * len(arrays),
        scratch_shapes=[pltpu.SemaphoreType.DMA((len(arrays),))],
    )(*arrays)


def shards(
    tokens, gain_attn, w_query, key_weight, value_weight, w_out, gain_query,
    key_norm_gain, gain_mlp, w_gate, w_up, w_down, cotangent,
):
    extra = jnp.stack(
        [
            gain_attn,
            gain_mlp,
            jnp.broadcast_to(gain_query, (WR,)),
            jnp.broadcast_to(key_norm_gain, (WR,)),
        ],
        axis=1,
    )
    extra = jnp.pad(extra, ((0, 0), (0, GCOL - 4)))
    table = rope_constants()
    (x1, dx1, dab, gain2, h1, pre, qb, kb, vb, ob, gains, gq, wo, ggu, pd, dacc) = front(
        tokens[0], cotangent[0], extra, w_query, key_weight, value_weight, w_out, w_gate, w_up,
        w_down, table,
    )
    gt, block, g_q, g_k, g_v, g_out, g_gate, g_up, g_down, gg = back(
        dab, pd, ggu, h1, gq, wo, dacc, dx1, tokens[0], x1, pre, qb, kb, vb, ob, gain2, gains, table,
    )
    block, gt, g_q, g_k, g_v, g_out, g_gate, g_up, g_down = hand_over(
        block, gt, g_q, g_k, g_v, g_out, g_gate, g_up, g_down
    )
    gg = gg[0]
    return (
        block[None], gt[None], gg[:WR], g_q, g_k, g_v, g_out,
        gg[2 * WR : 2 * WR + 1], gg[2 * WR + 1 : 2 * WR + 2], gg[WR : 2 * WR],
        g_gate, g_up, g_down,
    )


def solution(mesh):
    both = P(("dp", "seq"))
    rows = P(("dp", "seq"), None)
    act = P("dp", "seq", None)
    in_specs = (act, both, rows, rows, rows, rows, both, both, both, rows, rows, rows, act)
    out_specs = (act, act, both, rows, rows, rows, rows, both, both, both, rows, rows, rows)
    return jax.shard_map(
        shards, mesh=mesh, in_specs=in_specs, out_specs=out_specs, check_vma=False
    )
```
